256 devices in a mesh: lon: 16 (over y_hi, x, core), lat: 16 (over z, y_lo).
Axes of the slice: x: 4, y: 4 (y_hi: 2, y_lo: 2; y = y_hi * 2 + y_lo), z: 8, core: 2. Of those that a mesh axis runs over, the one named last changes fastest.
Arguments:
- features: bfloat16 [48, 2, 128, 8192], P(None, None, 'lat', 'lon'), may hold values from -6 to 6
- spline_coef: bfloat16 [432, 480], replicated, may hold values from -0.25 to 0.25
- edge_mask: int32 [48, 48], replicated, may hold values 0 or 1
- head_weight: bfloat16 [2, 48], replicated, may hold values from -0.875 to 0.875
- land_mask: int32 [128, 8192], P('lat', 'lon'), may hold values 0 or 1
- shift_coef: float32 [128, 8192], P('lat', 'lon'), may hold values from 0.02 to 2
Outputs:
- tendency: bfloat16 [2, 2, 128, 8192], P(None, None, 'lat', 'lon')
- surface: float32 [128, 8192], P('lat', 'lon')
- residual: float32 [128, 8192], P('lat', 'lon')
The draws below stay inside these ranges and needn't reach their ends.
Inputs may be any that keep to these rules, and one draw needn't show every extreme that they name: `edge_mask`: 1 keeps an edge. `land_mask`: 1 marks ocean.
All inputs are finite; a program needn't handle non-finite values. No bound on the sum of `land_mask` on one device may be relied on, other than what follows from the above.
Results may differ from the reference program's by a relative error of at most 0.014.
Values may be sent and summed in bfloat16 or wider, within the bound.
A program may use at most 128 MiB of HBM per device.

```python
import jax
import jax.numpy as jnp
from jax import lax

C = 48
NB = 9
L = 2
ITERS = 2
CLAT = 8
CLON = 512
NLAT = 128
NLON = 8192
N_LAT = 16


def inner_rows():
    rows = jnp.arange(NLAT, dtype=jnp.int32) % CLAT
    return ((rows >= CLAT // 4) & (rows < CLAT // 4 + CLAT // 2))[:, None]


def left_columns():
    cols = jnp.arange(NLON, dtype=jnp.int32) % CLON
    return (cols < CLON // 2)[None, :]


def draw_features(key, part):
    key = jax.random.fold_in(key, 11)
    inner = inner_rows()
    left = left_columns()
    quiet = jnp.logical_or(inner, left)
    factor = jnp.where(quiet, 0.25, 1.0).astype(jnp.float32)
    values = jax.random.truncated_normal(key, -6.0, 6.0, (C, L, NLAT, NLON), jnp.float32)
    return (values * factor[None, None]).astype(jnp.bfloat16)


def draw_shift_coef(key, part):
    key = jax.random.fold_in(key, 23)
    inner = inner_rows()
    left = left_columns()
    quiet = jnp.logical_or(inner, left)
    unit = jax.random.uniform(key, (NLAT, NLON), jnp.float32)
    low_quiet = jnp.log(jnp.float32(0.02))
    high_quiet = jnp.log(jnp.float32(0.05))
    low_loud = jnp.log(jnp.float32(1.0))
    high_loud = jnp.log(jnp.float32(2.0))
    quiet_value = jnp.exp(low_quiet + unit * (high_quiet - low_quiet))
    loud_value = jnp.exp(low_loud + unit * (high_loud - low_loud))
    values = jnp.where(quiet, quiet_value, loud_value)
    return jnp.clip(values, 0.02, 2.0).astype(jnp.float32)


def set_ends(array, own_key, least, high):
    extent = array.shape
    spot = [jax.random.randint(jax.random.fold_in(own_key, axis), (), 0, extent[axis]) for axis in range(len(extent))]
    array = array.at[tuple(spot)].set(least)
    longest = extent.index(max(extent))
    spot[longest] = (spot[longest] + 1) % extent[longest]
    return array.at[tuple(spot)].set(high)


def noise(own_key, dims, scale, reach, kind=jnp.bfloat16):
    return jnp.clip(scale * jax.random.normal(own_key, dims, jnp.float32), -reach, reach).astype(kind)


def setup_inputs(seed: int = 0) -> dict:
    streams_of = jax.random.split(jax.random.key(seed), 7)
    return {
        "features": draw_features(jax.random.fold_in(streams_of[6], 71), 0),
        "spline_coef": noise(streams_of[1], (9 * C, C * (NB + 1)), (C * (NB + 1)) ** -0.5, 0.25),
        "edge_mask": set_ends((jax.random.randint(streams_of[2], (C, C), 0, 4) < 3).astype(jnp.int32), jax.random.fold_in(streams_of[2], 1), 0, 1),
        "head_weight": noise(streams_of[3], (2, C), C ** -0.5, 0.875),
        "land_mask": set_ends((jax.random.randint(streams_of[4], (NLAT, NLON), 0, 8) < 7).astype(jnp.int32), jax.random.fold_in(streams_of[4], 1), 0, 1),
        "shift_coef": draw_shift_coef(jax.random.fold_in(streams_of[6], 71), 0),
    }


def masked_weight(spline_coef, edge_mask):
    wide_mask = jnp.tile(jnp.repeat(edge_mask, NB + 1, axis=1), (9, 1))
    return jnp.where(wide_mask > 0, spline_coef, jnp.zeros_like(spline_coef))


def expand_bases(padded):
    values = padded.astype(jnp.float32)[:, None]
    centers = jnp.linspace(-2.0, 2.0, NB).astype(jnp.float32).reshape(1, NB, 1, 1, 1)
    spread = 4.0 / (NB - 1)
    bumps = jnp.exp(-jnp.square((values - centers) / spread))
    stacked = jnp.concatenate([bumps, jax.nn.silu(values)], axis=1)
    return stacked.astype(jnp.bfloat16).reshape(C * (NB + 1), -1)


def closure_band(padded, weight, rows, cols):
    table = expand_bases(padded)
    mixed = jnp.dot(weight.astype(jnp.float32), table.astype(jnp.float32), preferred_element_type=jnp.float32)
    mixed = mixed.reshape(9, C, L, rows + 2, cols + 2)
    total = jnp.zeros((C, L, rows, cols), jnp.float32)
    for offset in range(9):
        row_off, col_off = divmod(offset, 3)
        total = total + mixed[offset, :, :, row_off:row_off + rows, col_off:col_off + cols]
    return total


def extend_features(features):
    wide = jnp.concatenate([features[..., -1:], features, features[..., :1]], axis=-1)
    south = jnp.zeros_like(wide[:, :, :1])
    north = wide[:, :, -1:, ::-1]
    return jnp.concatenate([south, wide, north], axis=2)


def operate(field, ocean, shift_coef):
    masked = ocean * field
    west = jnp.roll(masked, 1, axis=1)
    east = jnp.roll(masked, -1, axis=1)
    south = jnp.concatenate([jnp.zeros_like(masked[:1]), masked[:-1]], axis=0)
    north = jnp.concatenate([masked[1:], masked[-1:, ::-1]], axis=0)
    return ocean * ((4.0 + shift_coef) * field - (west + east + south + north)) + (1.0 - ocean) * field


def reference(features, spline_coef, edge_mask, head_weight, land_mask, shift_coef):
    weight = masked_weight(spline_coef, edge_mask)
    extended = extend_features(features)

    def band(start):
        piece = lax.dynamic_slice_in_dim(extended, start, CLAT + 2, 2)
        return closure_band(piece, weight, CLAT, NLON)

    starts = jnp.arange(N_LAT, dtype=jnp.int32) * CLAT
    bands = lax.map(band, starts)
    hidden = jnp.moveaxis(bands, 0, 2).reshape(C, L, NLAT, NLON).astype(jnp.bfloat16)
    ocean = land_mask.astype(jnp.float32)
    mixed = jnp.einsum("co,olyx->clyx", head_weight.astype(jnp.float32), hidden.astype(jnp.float32))
    tendency = (mixed * ocean).astype(jnp.bfloat16)
    tend_f = tendency.astype(jnp.float32)
    east_part = tend_f[0] - jnp.roll(tend_f[0], 1, axis=2)
    below = jnp.concatenate([jnp.zeros_like(tend_f[1][:, :1]), tend_f[1][:, :-1]], axis=1)
    north_part = tend_f[1] - below
    rhs = ocean * jnp.sum(east_part + north_part, axis=0)
    surface = jnp.zeros_like(rhs)
    residual = rhs
    direction = rhs
    norm_now = jnp.sum(residual * residual)
    for step in range(ITERS):
        image = operate(direction, ocean, shift_coef)
        alpha = norm_now / jnp.sum(direction * image)
        surface = surface + alpha * direction
        residual = residual - alpha * image
        norm_next = jnp.sum(residual * residual)
        direction = residual + (norm_next / norm_now) * direction
        norm_now = norm_next
    return tendency, surface, residual
```

```python
import functools
import math

import jax
import jax.numpy as jnp
from jax import lax
from jax.experimental import pallas as pl
from jax.experimental.pallas import tpu as pltpu
from jax.sharding import PartitionSpec as P

C = 48
NB = 9
J = NB + 1
L = 2
ROWS = 8
COLS = 512
WIDE = COLS + 128
F32 = jnp.float32
BF16 = jnp.bfloat16
MESH = pl.DeviceIdType.MESH
LOG2E = math.log2(math.e)
LIFT = 29
GROUP = 16
GROUPS = C // GROUP


def iota(shape, axis):
    return lax.broadcasted_iota(jnp.int32, shape, axis)


def dot(a, b):
    return jnp.dot(a, b, preferred_element_type=F32)


def ones_where(cond):
    return jnp.where(cond, 1.0, 0.0).astype(BF16)


def fold_weights(coef_ref, edge_ref, head_ref, wt, top):
    channel, lane = iota((C, C * J), 0), iota((C, C * J), 1)
    spread = ones_where((lane >= channel * J) & (lane < channel * J + J))
    keep = dot(jnp.where(edge_ref[...] > 0, 1.0, 0.0).astype(BF16), spread).astype(BF16)
    o, q = iota((C, 9 * C), 0), iota((C, 9 * C), 1)
    offset = lax.shift_right_logical(q * 1366, 16)
    head = dot(head_ref[...], ones_where(q - offset * C == o))
    r, q = iota((24, 9 * C), 0), iota((24, 9 * C), 1)
    offset = lax.shift_right_logical(q * 1366, 16)
    head = jnp.where((r & 1) == 0, head[0:1], head[1:2])
    head = jnp.where(lax.shift_right_logical(r, 1) == offset, head, 0.0).astype(BF16)
    folded = jnp.zeros((24, C * J), F32)
    masked = [coef_ref[C * k : C * k + C, :] * keep for k in range(9)]
    folded = dot(head, jnp.concatenate(masked, axis=0))
    lane = iota((1, C * J), 1)
    j = lane - J * lax.shift_right_logical(lane * 6554, 16)
    scale = jnp.where((j == 0) | (j == 8), math.exp(-6.0), jnp.where((j == 2) | (j == 6), math.exp(6.0), 1.0))
    folded = (folded * scale).astype(BF16)
    q = iota((1, 64 * J), 1)
    source = jnp.where((q & 63) < C, (q & 63) * J + lax.shift_right_logical(q, 6), -1)
    folded = dot(folded, ones_where(iota((C * J, 64 * J), 0) == source)).astype(BF16)
    q = iota((1, 2 * C * ROWS), 1)
    second = jnp.where(q >= C * ROWS, 1, 0)
    source = second * 64 + lax.shift_right_logical(q - second * (C * ROWS), 3)
    expand = ones_where(iota((128, 2 * C * ROWS), 0) == source)
    y_out = iota((ROWS, 2 * C * ROWS), 0)
    y_in = iota((ROWS, 2 * C * ROWS), 1) & 7
    first_row, last_row = y_in[0:6] == 0, y_in[0:6] == 7
    pad = jnp.zeros((2, 2 * C * ROWS), F32)
    for pair in range(J // 2):
        g = dot(folded[:, 128 * pair : 128 * pair + 128], expand)
        tiles = []
        for k in range(6):
            tile = jnp.where(y_in == y_out - 1, g[k : k + 1], 0.0)
            tile = jnp.where(y_in == y_out, g[6 + k : 7 + k], tile)
            tiles.append(jnp.where(y_in == y_out + 1, g[12 + k : 13 + k], tile))
        mirrored = jnp.concatenate([g[16:18], g[14:16], g[12:14]], axis=0)
        above = jnp.where(top, mirrored, g[0:6])
        tiles += [jnp.where(first_row, g[12:18], 0.0), pad, jnp.where(last_row, above, 0.0), pad]
        block = jnp.concatenate(tiles, axis=0).astype(BF16)
        for half in range(2):
            j = 2 * pair + half
            for group in range(GROUPS):
                at = half * C * ROWS + group * 128
                wt[group, :, 128 * j : 128 * j + 128] = block[:, at : at + 128]


def basis(x):
    base = (x * x) * (-4.0 * LOG2E)
    outer = base + (LIFT - 9.0 * LOG2E)
    slope = x * (12.0 * LOG2E)
    step = x * (4.0 * LOG2E)
    up = jnp.exp2(step - LOG2E)
    down = jnp.exp2(-LOG2E - step)
    left = jnp.exp2(outer - slope)
    middle = jnp.exp2(base + float(LIFT))
    right = jnp.exp2(outer + slope)
    half = x * (0.5 * 2.0**LIFT)
    silu = half + half * jnp.tanh(x * 0.5)
    return [left * down, left, left * up, middle * down, middle, middle * up, right * down, right, right * up, silu]


def kernel(
    n_lon, n_lat,
    feat_hbm, coef_ref, edge_ref, head_ref, land_ref, shift_ref,
    tend_ref, surf_ref, res_ref,
    feat, wt, bases, acc,
    north_m, south_m, both_m, got_m, side_m,
    north_p, south_p, east_p, west_p, got_p, side_p,
    lon_sums, lat_sums,
    feat_sem, send_m, recv_m, send_p, recv_p, send_a, recv_a,
):
    lon, lat = lax.axis_index("lon"), lax.axis_index("lat")
    top, bottom = lat == n_lat - 1, lat == 0
    east, west = lax.rem(lon + 1, n_lon), lax.rem(lon + n_lon - 1, n_lon)
    mirror = n_lon - 1 - lon
    up_lat = jnp.where(top, lat, lat + 1)
    up_lon = jnp.where(top, mirror, lon)
    up_east = jnp.where(top, n_lon - 1 - east, east)
    up_west = jnp.where(top, n_lon - 1 - west, west)
    down_lat = jnp.where(bottom, lat, lat - 1)
    east_self = top & (up_east == lon)
    west_self = top & (up_west == lon)

    feat_in = [
        pltpu.make_async_copy(feat_hbm.at[:, level], feat.at[level], feat_sem.at[level]) for level in range(L)
    ]
    for copy in feat_in:
        copy.start()

    barrier = pltpu.get_barrier_semaphore()

    def greet(at_lon, at_lat):
        pl.semaphore_signal(barrier, inc=1, device_id={"lon": at_lon, "lat": at_lat}, device_id_type=MESH)

    for d in range(1, n_lon):
        greet(lax.rem(lon + d, n_lon), lat)
    for d in range(1, n_lat):
        greet(lon, lax.rem(lat + d, n_lat))

    @pl.when(jnp.logical_not(top))
    def _():
        greet(east, up_lat)
        greet(west, up_lat)

    @pl.when(jnp.logical_not(bottom))
    def _():
        greet(east, down_lat)
        greet(west, down_lat)

    def remote(src, dst, send, recv, at_lon, at_lat):
        return pltpu.make_async_remote_copy(
            src_ref=src, dst_ref=dst, send_sem=send, recv_sem=recv,
            device_id={"lon": at_lon, "lat": at_lat}, device_id_type=MESH,
        )

    class Exchange:
        def __init__(self, north, south, to_east, to_west, got, side, send, recv, whole, ne, nw):
            width = ne[1]
            mid = pl.ds(*whole)
            e, w = pl.ds(*ne), pl.ds(*nw)
            part = pl.ds(0, width)
            self.got, self.side = got, side
            base = jnp.where(top, 3, 0)
            self.local = [
                (east_self, got.at[4, :, part], north.at[:, e]),
                (west_self, got.at[5, :, part], north.at[:, w]),
            ]
            self.sends = [
                (None, remote(north.at[:, mid], got.at[base], send.at[0], recv.at[base], up_lon, up_lat)),
                (jnp.logical_not(east_self), remote(north.at[:, e], got.at[base + 1, :, part], send.at[1], recv.at[base + 1], up_east, up_lat)),
                (jnp.logical_not(west_self), remote(north.at[:, w], got.at[base + 2, :, part], send.at[2], recv.at[base + 2], up_west, up_lat)),
                (jnp.logical_not(bottom), remote(south.at[:, mid], got.at[3], send.at[3], recv.at[3], lon, down_lat)),
                (jnp.logical_not(bottom), remote(south.at[:, e], got.at[4, :, part], send.at[4], recv.at[4], east, down_lat)),
                (jnp.logical_not(bottom), remote(south.at[:, w], got.at[5, :, part], send.at[5], recv.at[5], west, down_lat)),
                (None, remote(to_east, side.at[0], send.at[6], recv.at[6], east, lat)),
                (None, remote(to_west, side.at[1], send.at[7], recv.at[7], west, lat)),
            ]
            corner = got.at[0, :, part]
            has_south = jnp.logical_not(bottom)

            def arrival(src, dst, k):
                return remote(src, dst, send.at[0], recv.at[k], east, lat)

            self.arrivals = [
                (has_south, arrival(north.at[:, mid], got.at[0], 0)),
                (has_south, arrival(north.at[:, e], got.at[1, :, part], 1)),
                (has_south, arrival(north.at[:, w], got.at[2, :, part], 2)),
                (None, arrival(north.at[:, mid], got.at[3], 3)),
                (jnp.logical_not(east_self), arrival(north.at[:, e], got.at[4, :, part], 4)),
                (jnp.logical_not(west_self), arrival(north.at[:, w], got.at[5, :, part], 5)),
                (None, arrival(to_east, side.at[0], 6)),
                (None, arrival(to_west, side.at[1], 7)),
            ]

        def each(self, entries, act):
            for cond, copy in entries:
                if cond is None:
                    act(copy)
                else:
                    pl.when(cond)(functools.partial(act, copy))

        def start(self):
            for cond, dst, src in self.local:
                def place(dst=dst, src=src):
                    dst[...] = src[...]

                pl.when(cond)(place)

            self.each(self.sends, lambda copy: copy.start())

        def arrive(self):
            self.each(self.arrivals, lambda copy: copy.wait_recv())

        def leave(self):
            self.each(self.sends, lambda copy: copy.wait_send())

    @pl.when(bottom)
    def _():
        got_m[0:3] = jnp.zeros((3,) + got_m.shape[1:], F32)
        got_p[0:3] = jnp.zeros((3,) + got_p.shape[1:], F32)

    ocean = land_ref[...].astype(F32)
    shift = shift_ref[...]
    both_m[0:8] = ocean
    both_m[8:16] = shift
    none = jnp.zeros((1, COLS), F32)
    north_m[...] = jnp.concatenate([ocean[7:8], shift[7:8]] + [none] * 6, axis=0)
    south_m[...] = jnp.concatenate([ocean[0:1], shift[0:1], ocean[1:2]] + [none] * 5, axis=0)

    fold_weights(coef_ref, edge_ref, head_ref, wt, top)

    diagonals = 4 - 2 * jnp.where(top | bottom, 1, 0)
    pl.semaphore_wait(barrier, n_lon + n_lat - 2 + diagonals)

    masks = Exchange(
        north_m, south_m, both_m.at[:, pl.ds(COLS - 128, 128)], both_m.at[:, pl.ds(0, 128)],
        got_m, side_m, send_m, recv_m, (0, COLS), (COLS - 128, 128), (0, 128),
    )
    masks.start()

    acc[...] = jnp.zeros(acc.shape, F32)
    for level in range(L):
        feat_in[level].wait()

        def step(group, carry):
            x = feat[level, pl.ds(group * GROUP, GROUP)].astype(F32).reshape(GROUP * ROWS, COLS)
            for j, value in enumerate(basis(x)):
                bases[128 * j : 128 * j + 128, :] = value.astype(BF16)
            acc[level, :, 0:COLS] += dot(wt[group], bases[...])
            return carry

        lax.fori_loop(0, GROUPS, step, 0)

    masks.arrive()

    lane = iota((ROWS, 128), 1)
    low = lane < 64
    row = iota((ROWS, WIDE), 0)
    backwards = 127 - lane

    def tiles_of(x):
        return [x[:, 128 * k : 128 * k + 128] for k in range(x.shape[1] // 128)]

    def flip(parts):
        turned = [jnp.take_along_axis(p, backwards, axis=1) for p in parts]
        return turned[3::-1] + turned[4:]

    def joined(parts):
        return jnp.concatenate(parts, axis=1)

    def from_north(parts):
        turned = flip(parts)
        return joined([jnp.where(top, b, a) for a, b in zip(parts, turned)])

    def mask_rows(k):
        parts = tiles_of(got_m[k])
        return parts + [jnp.where(low, got_m[k + 2, :, 0:128], got_m[k + 1, :, 0:128])]

    south_rows = joined(mask_rows(0))
    north_rows = from_north(mask_rows(3))
    side = jnp.where(
        jnp.concatenate([low, low], axis=0), side_m[1], side_m[0]
    )
    zero = jnp.zeros((ROWS, WIDE), F32)

    def extended(own, own_side, north1, north2, south1):
        outer = jnp.where(row == 0, north1, jnp.where(row == 1, north2, jnp.where(row == 7, south1, zero)))
        return jnp.concatenate([joined([own, own_side]), outer], axis=0)

    second = jnp.where(top, zero[0:1], north_rows[2:3])
    m = extended(ocean, side[0:8], north_rows[0:1], second, south_rows[0:1])
    s = extended(shift, side[8:16], north_rows[1:2], zero[0:1], south_rows[1:2])

    def lanes(x, by):
        return pltpu.roll(x, by % WIDE, 1)

    def rows(x, by):
        return pltpu.roll(x, by % 16, 0)

    own, above, below = [], [], []
    for level in range(L):
        a = acc[level] * (2.0**-LIFT)
        own.append(a[16:32] + lanes(a[0:16], 1) + lanes(a[32:48], -1))
        outer = a[48:64]
        before, after = lanes(outer, 1), lanes(outer, -1)
        below.append(outer[2:4] + before[0:2] + after[4:6])
        above.append(outer[10:12] + before[8:10] + after[12:14])
    j = lax.shift_right_logical(iota((1, 128 * J), 1), 7)
    off = jnp.abs(j - 4)
    still = jnp.where(off == 1, math.exp(-1.0), jnp.where(off == 2, math.exp(-10.0), jnp.where(off == 3, math.exp(-9.0), math.exp(-10.0))))
    still = jnp.where(off == 0, 1.0, jnp.where(j == NB, 0.0, still))
    outside = jnp.zeros((8, 128 * J), F32)
    for group in range(GROUPS):
        outside = outside + wt[group, 48:64, :].astype(F32)[8:16]
    outside = jnp.where(bottom, jnp.sum(outside * still, axis=1, keepdims=True), 0.0)
    first = (iota((8, WIDE), 0) == 0) & (iota((8, WIDE), 1) < COLS)
    for level in range(L):
        own[level] = jnp.concatenate(
            [own[level][8 * c : 8 * c + 8] + jnp.where(first, outside[c : c + 1] + outside[c + 2 : c + 3] + outside[c + 4 : c + 5], 0.0) for c in range(2)],
            axis=0,
        )
    total, total_up, total_down = own[0] + own[1], above[0] + above[1], below[0] + below[1]

    def field(c):
        outer = jnp.where(row == 0, total_up[c : c + 1], jnp.where(row == 7, total_down[c : c + 1], zero))
        return m * jnp.concatenate([total[8 * c : 8 * c + 8], outer], axis=0)

    eastward, northward = field(0), field(1)
    part = m * (eastward - lanes(eastward, 1) + northward - rows(northward, 1))
    folded = m[8:16] * (eastward[8:16] - lanes(eastward, -1)[8:16] + northward[8:16])
    part = jnp.concatenate([part[0:8], jnp.where(top & (row == 0), folded, part[8:16])], axis=0)

    edge_n = jnp.concatenate([part[8:9], part[7:8], part[6:7], part[9:10], above[0], above[1]], axis=0)
    edge_s = jnp.concatenate([part[15:16], part[0:1], part[1:2], zero[0:1], below[0], below[1]], axis=0)
    for edge, ref in ((edge_n, north_p), (edge_s, south_p)):
        ref[:, 0:128] = edge[:, COLS:]
        ref[:, 128:] = edge
    east_p[0:16, :] = part[:, COLS - 128 :]
    west_p[0:16, 0:128] = part[:, COLS:]
    west_p[0:16, 128:] = part[:, 0:128]
    for level in range(L):
        halo = own[level][:, COLS:]
        for ref in (east_p, west_p):
            ref[16:32, 128 * level : 128 * level + 128] = halo

    partials = Exchange(
        north_p, south_p, east_p, west_p,
        got_p, side_p, send_p, recv_p, (128, WIDE), (COLS, 256), (0, 256),
    )
    partials.start()
    partials.arrive()

    def part_rows(k):
        t = tiles_of(got_p[k])
        w, e = got_p[k + 1, :, 0:256], got_p[k + 2, :, 0:256]
        t[0] = t[0] + jnp.where(low, w[:, 128:], 0.0)
        t[3] = t[3] + jnp.where(low, 0.0, e[:, :128])
        t[4] = t[4] + jnp.where(low, e[:, 128:], w[:, :128])
        return t

    south_rows = joined(part_rows(0))
    north_rows = from_north(part_rows(3))
    from_west, from_east = side_p[0], side_p[1]
    low2 = jnp.concatenate([low, low], axis=0)

    inner = jnp.where(row == 0, south_rows[0:1], jnp.where(row == 1, south_rows[3:4], jnp.where(row == 7, north_rows[0:1], zero)))
    outer = jnp.where(row == 0, north_rows[1:2], jnp.where(row == 1, north_rows[2:3], jnp.where(row == 6, south_rows[2:3], jnp.where(row == 7, south_rows[1:2], zero))))
    r = part + jnp.concatenate([inner, outer], axis=0)
    r = joined([
        r[:, 0:128] + jnp.where(low2, from_west[0:16, 128:], 0.0),
        r[:, 128 : COLS - 128],
        r[:, COLS - 128 : COLS] + jnp.where(low2, 0.0, from_east[0:16, 0:128]),
        r[:, COLS:] + jnp.where(low2, from_east[0:16, 128:], from_west[0:16, 0:128]),
    ])

    def operate(v):
        return m * ((4.0 + s) * v - (lanes(v, 1) + lanes(v, -1) + rows(v, 1) + rows(v, -1)))

    q1 = operate(r)
    q2 = operate(q1)[0:8, 0:COLS]
    r, q1 = r[0:8, 0:COLS], q1[0:8, 0:COLS]

    def summed(x):
        x = x[:, 0:128] + x[:, 128:256] + x[:, 256:384] + x[:, 384:512]
        return jnp.sum(x, axis=0, keepdims=True)

    sums = [summed(r * r), summed(r * q1), summed(q1 * q1), summed(r * q2), summed(q1 * q2)]
    mine = jnp.concatenate(sums + [jnp.zeros((3, 128), F32)], axis=0)

    def all_sum(value, ref, stage, count, here, device):
        ref[here] = value
        out = []
        for d in range(1, count):
            there = lax.rem(here + d, count)
            copy = remote(ref.at[here], ref.at[here], send_a.at[stage, d], recv_a.at[stage, here], *device(there))
            copy.start()
            out.append(copy)
        for d in range(1, count):
            there = lax.rem(here + d, count)
            remote(ref.at[there], ref.at[there], send_a.at[stage, d], recv_a.at[stage, there], *device(there)).wait_recv()
        return jnp.sum(ref[...], axis=0), out

    value, copies_lon = all_sum(mine, lon_sums, 0, n_lon, lon, lambda k: (k, lat))
    value, copies_lat = all_sum(value, lat_sums, 1, n_lat, lat, lambda k: (lon, k))

    for level in range(L):
        for c in range(2):
            t = own[level][8 * c : 8 * c + 8]
            k = 4 + 2 * level + c
            t = t + jnp.where(row == 0, south_rows[k : k + 1], jnp.where(row == 7, north_rows[k : k + 1], zero))
            at = slice(128 * level, 128 * level + 128)
            w = jnp.where(lane == 0, from_west[16 + 8 * c : 24 + 8 * c, at], 0.0)
            e = jnp.where(lane == 127, from_east[16 + 8 * c : 24 + 8 * c, at], 0.0)
            t = joined([t[:, 0:128] + w, t[:, 128 : COLS - 128], t[:, COLS - 128 : COLS] + e])
            tend_ref[c, level] = (ocean * t).astype(BF16)

    value = jnp.sum(value, axis=1, keepdims=True)
    rr, rq, qq, rq2, qq2 = [value[k : k + 1] for k in range(5)]
    a1 = rr / rq
    new = rr - 2.0 * a1 * rq + a1 * a1 * qq
    lead = 1.0 + new / rr
    a2 = new / (lead * lead * rq - lead * a1 * (rq2 + qq) + a1 * a1 * qq2)
    surf_ref[...] = a1 * r + a2 * (lead * r - a1 * q1)
    res_ref[...] = r - a1 * q1 - a2 * (lead * q1 - a1 * q2)

    masks.leave()
    partials.leave()
    for copy in copies_lon + copies_lat:
        copy.wait_send()


def body(features, spline_coef, edge_mask, head_weight, land_mask, shift_coef):
    n_lon, n_lat = lax.axis_size("lon"), lax.axis_size("lat")
    vmem = pl.BlockSpec(memory_space=pltpu.VMEM)
    dma = pltpu.SemaphoreType.DMA
    scratch = [
        pltpu.VMEM((L, C, ROWS, COLS), BF16),
        pltpu.VMEM((GROUPS, 64, 128 * J), BF16),
        pltpu.VMEM((128 * J, COLS), BF16),
        pltpu.VMEM((L, 64, WIDE), F32),
        pltpu.VMEM((8, COLS), F32),
        pltpu.VMEM((8, COLS), F32),
        pltpu.VMEM((16, COLS), F32),
        pltpu.VMEM((6, 8, COLS), F32),
        pltpu.VMEM((2, 16, 128), F32),
        pltpu.VMEM((8, WIDE + 128), F32),
        pltpu.VMEM((8, WIDE + 128), F32),
        pltpu.VMEM((32, 256), F32),
        pltpu.VMEM((32, 256), F32),
        pltpu.VMEM((6, 8, WIDE), F32),
        pltpu.VMEM((2, 32, 256), F32),
        pltpu.VMEM((n_lon, 8, 128), F32),
        pltpu.VMEM((n_lat, 8, 128), F32),
        dma((L,)),
        dma((8,)), dma((8,)), dma((8,)), dma((8,)),
        dma((2, max(n_lon, n_lat))), dma((2, max(n_lon, n_lat))),
    ]
    return pl.pallas_call(
        functools.partial(kernel, n_lon, n_lat),
        out_shape=(
            jax.ShapeDtypeStruct((2, L, ROWS, COLS), BF16),
            jax.ShapeDtypeStruct((ROWS, COLS), F32),
            jax.ShapeDtypeStruct((ROWS, COLS), F32),
        ),
        in_specs=[pl.BlockSpec(memory_space=pl.ANY)] + [vmem] * 5,
        out_specs=(vmem, vmem, vmem),
        scratch_shapes=scratch,
        compiler_params=pltpu.CompilerParams(
            collective_id=0, has_side_effects=True, vmem_limit_bytes=48 * 1024 * 1024
        ),
        name="closure_and_cg",
    )(features, spline_coef, edge_mask, head_weight, land_mask, shift_coef)


def solution(mesh):
    in_specs = (P(None, None, "lat", "lon"), P(), P(), P(), P("lat", "lon"), P("lat", "lon"))
    out_specs = (P(None, None, "lat", "lon"), P("lat", "lon"), P("lat", "lon"))
    return jax.shard_map(body, mesh=mesh, in_specs=in_specs, out_specs=out_specs, check_vma=False)
```

```python
import functools
import math

import jax
import jax.numpy as jnp
from jax import lax
from jax.experimental import pallas as pl
from jax.experimental.pallas import tpu as pltpu
from jax.sharding import PartitionSpec as P

C = 48
NB = 9
J = NB + 1
L = 2
ROWS = 8
COLS = 512
WIDE = COLS + 128
F32 = jnp.float32
BF16 = jnp.bfloat16
MESH = pl.DeviceIdType.MESH
LOG2E = math.log2(math.e)
LIFT = 29
GROUP = 16
GROUPS = C // GROUP
STRIP = 2


def iota(shape, axis):
    return lax.broadcasted_iota(jnp.int32, shape, axis)


def dot(a, b):
    return jnp.dot(a, b, preferred_element_type=F32)


def ones_where(cond):
    return jnp.where(cond, 1.0, 0.0).astype(BF16)


def fold_weights(coef_ref, edge_ref, head_ref, wt, top):
    channel, lane = iota((C, C * J), 0), iota((C, C * J), 1)
    spread = ones_where((lane >= channel * J) & (lane < channel * J + J))
    keep = dot(jnp.where(edge_ref[...] > 0, 1.0, 0.0).astype(BF16), spread).astype(BF16)
    o, q = iota((C, 9 * C), 0), iota((C, 9 * C), 1)
    offset = lax.shift_right_logical(q * 1366, 16)
    head = dot(head_ref[...], ones_where(q - offset * C == o))
    r, q = iota((24, 9 * C), 0), iota((24, 9 * C), 1)
    offset = lax.shift_right_logical(q * 1366, 16)
    head = jnp.where((r & 1) == 0, head[0:1], head[1:2])
    head = jnp.where(lax.shift_right_logical(r, 1) == offset, head, 0.0).astype(BF16)
    folded = jnp.zeros((24, C * J), F32)
    masked = [coef_ref[C * k : C * k + C, :] * keep for k in range(9)]
    folded = dot(head, jnp.concatenate(masked, axis=0))
    lane = iota((1, C * J), 1)
    j = lane - J * lax.shift_right_logical(lane * 6554, 16)
    scale = jnp.where((j == 0) | (j == 8), math.exp(-6.0), jnp.where((j == 2) | (j == 6), math.exp(6.0), 1.0))
    folded = (folded * scale).astype(BF16)
    q = iota((1, 64 * J), 1)
    source = jnp.where((q & 63) < C, (q & 63) * J + lax.shift_right_logical(q, 6), -1)
    folded = dot(folded, ones_where(iota((C * J, 64 * J), 0) == source)).astype(BF16)
    q = iota((1, 2 * C * ROWS), 1)
    second = jnp.where(q >= C * ROWS, 1, 0)
    source = second * 64 + lax.shift_right_logical(q - second * (C * ROWS), 3)
    expand = ones_where(iota((128, 2 * C * ROWS), 0) == source)
    y_out = iota((ROWS, 2 * C * ROWS), 0)
    y_in = iota((ROWS, 2 * C * ROWS), 1) & 7
    first_row, last_row = y_in[0:6] == 0, y_in[0:6] == 7
    pad = jnp.zeros((2, 2 * C * ROWS), F32)
    for pair in range(J // 2):
        g = dot(folded[:, 128 * pair : 128 * pair + 128], expand)
        tiles = []
        for k in range(6):
            tile = jnp.where(y_in == y_out - 1, g[k : k + 1], 0.0)
            tile = jnp.where(y_in == y_out, g[6 + k : 7 + k], tile)
            tiles.append(jnp.where(y_in == y_out + 1, g[12 + k : 13 + k], tile))
        mirrored = jnp.concatenate([g[16:18], g[14:16], g[12:14]], axis=0)
        above = jnp.where(top, mirrored, g[0:6])
        tiles += [jnp.where(first_row, g[12:18], 0.0), pad, jnp.where(last_row, above, 0.0), pad]
        block = jnp.concatenate(tiles, axis=0).astype(BF16)
        for half in range(2):
            j = 2 * pair + half
            for group in range(GROUPS):
                at = half * C * ROWS + group * 128
                wt[group, :, 128 * j : 128 * j + 128] = block[:, at : at + 128]


def basis(x):
    base = (x * x) * (-4.0 * LOG2E)
    outer = base + (LIFT - 9.0 * LOG2E)
    slope = x * (12.0 * LOG2E)
    step = x * (4.0 * LOG2E)
    up = jnp.exp2(step - LOG2E)
    down = jnp.exp2(-LOG2E - step)
    left = jnp.exp2(outer - slope)
    middle = jnp.exp2(base + float(LIFT))
    right = jnp.exp2(outer + slope)
    half = x * (0.5 * 2.0**LIFT)
    silu = half + half * jnp.tanh(x * 0.5)
    return [left * down, left, left * up, middle * down, middle, middle * up, right * down, right, right * up, silu]


def bits(value, flips):
    return jnp.bitwise_xor(value, flips) if flips else value


def kernel(
    n_lon, n_lat,
    feat_hbm, coef_hbm, edge_hbm, head_hbm, land_hbm, shift_hbm,
    tend_ref, fields_ref, sums_ref,
    feat, coef_ref, edge_ref, head_ref, land_ref, shift_ref, wt, bases, acc,
    north, south, to_east, to_west, got, side, sums_a, sums_b,
    feat_sem, weight_sem, send, recv, send_sum, recv_sum,
):
    lon, lat = lax.axis_index("lon"), lax.axis_index("lat")
    top, bottom = lat == n_lat - 1, lat == 0
    east = jnp.where(lon == n_lon - 1, 0, lon + 1)
    west = jnp.where(lon == 0, n_lon - 1, lon - 1)
    up_lat = jnp.where(top, lat, lat + 1)
    up_lon = jnp.where(top, n_lon - 1 - lon, lon)
    up_east = jnp.where(top, n_lon - 1 - east, east)
    up_west = jnp.where(top, n_lon - 1 - west, west)
    down_lat = jnp.where(bottom, lat, lat - 1)
    east_self, west_self = top & (up_east == lon), top & (up_west == lon)
    east_other, west_other = jnp.logical_not(east_self), jnp.logical_not(west_self)
    has_south = jnp.logical_not(bottom)

    weights_in = [
        pltpu.make_async_copy(src, dst, weight_sem.at[k])
        for k, (src, dst) in enumerate(
            [(edge_hbm, edge_ref), (head_hbm, head_ref), (coef_hbm, coef_ref), (land_hbm, land_ref), (shift_hbm, shift_ref)]
        )
    ]

    def feat_in(k):
        part = pl.ds(k * GROUP, GROUP)
        return pltpu.make_async_copy(feat_hbm.at[part], feat.at[part], feat_sem.at[k])

    for copy in weights_in + [feat_in(k) for k in range(GROUPS)]:
        copy.start()

    half = n_lon // 2
    first_sum = [(bits(lon, 2 * (d % half)), bits(lat, d // half)) for d in range(n_lon)]
    first_here = lon // 2 + half * lax.rem(lat, 2)
    second_sum = [(bits(lon, d % 2), bits(lat, d - d % 2)) for d in range(n_lat)]
    second_here = lat - lax.rem(lat, 2) + lax.rem(lon, 2)

    barrier = pltpu.get_barrier_semaphore()

    def greet(at_lon, at_lat):
        pl.semaphore_signal(barrier, inc=1, device_id={"lon": at_lon, "lat": at_lat}, device_id_type=MESH)

    greet(east, lat)
    greet(west, lat)
    greet(up_lon, up_lat)
    pl.when(east_other)(lambda: greet(up_east, up_lat))
    pl.when(west_other)(lambda: greet(up_west, up_lat))

    @pl.when(has_south)
    def _():
        greet(lon, down_lat)
        greet(east, down_lat)
        greet(west, down_lat)

    for at in first_sum[1:] + second_sum[1:]:
        greet(*at)
    greetings = n_lon + n_lat + 6 - jnp.where(east_self, 1, 0) - jnp.where(west_self, 1, 0) - jnp.where(bottom, 3, 0)

    def remote(src, dst, send, recv, at_lon, at_lat):
        return pltpu.make_async_remote_copy(
            src_ref=src, dst_ref=dst, send_sem=send, recv_sem=recv,
            device_id={"lon": at_lon, "lat": at_lat}, device_id_type=MESH,
        )

    @pl.when(bottom)
    def _():
        got[0:3] = jnp.zeros((3, 16, WIDE), F32)

    for copy in weights_in:
        copy.wait()
    fold_weights(coef_ref, edge_ref, head_ref, wt, top)

    acc[...] = jnp.zeros(acc.shape, F32)

    def step(k, carry):
        group, level = k // L, lax.rem(k, L)
        pl.when(level == 0)(lambda: feat_in(group).wait())
        for at in range(0, GROUP, STRIP):
            x = feat[pl.ds(group * GROUP + at, STRIP), level].astype(F32).reshape(STRIP * ROWS, COLS)
            for j, value in enumerate(basis(x)):
                row = 128 * j + ROWS * at
                bases[row : row + ROWS * STRIP, :] = value.astype(BF16)
        acc[level, :, 0:COLS] += dot(wt[group], bases[...])
        return carry

    lax.fori_loop(0, GROUPS * L, step, 0)

    lane, low = iota((ROWS, 128), 1), iota((ROWS, 128), 1) < 64
    low2 = iota((16, 128), 1) < 64
    row = iota((ROWS, WIDE), 0)
    zero = jnp.zeros((ROWS, WIDE), F32)

    def joined(parts):
        return jnp.concatenate(parts, axis=1)

    def stacked(parts):
        return jnp.concatenate(parts, axis=0)

    def lanes(x, by):
        return pltpu.roll(x, by % WIDE, 1)

    def rows(x, by):
        return pltpu.roll(x, by % 16, 0)

    def placed(entries):
        out = zero
        for at, value in entries:
            out = jnp.where(row == at, value, out)
        return out

    j = lax.shift_right_logical(iota((1, 128 * J), 1), 7)
    off = jnp.abs(j - 4)
    still = jnp.where(off == 1, math.exp(-1.0), jnp.where(off == 3, math.exp(-9.0), math.exp(-10.0)))
    still = jnp.where(off == 0, 1.0, jnp.where(j == NB, 0.0, still))
    outside = jnp.zeros((8, 128 * J), F32)
    for group in range(GROUPS):
        outside = outside + wt[group, 48:64, :].astype(F32)[8:16]
    outside = jnp.where(bottom, jnp.sum(outside * still, axis=1, keepdims=True), 0.0)
    outside = outside[0:2] + outside[2:4] + outside[4:6]
    first_row = (iota((ROWS, WIDE), 0) == 0) & (iota((ROWS, WIDE), 1) < COLS)
    outside = stacked([jnp.where(first_row, outside[c : c + 1], 0.0) for c in range(2)])

    own, above, below = [], [], []
    for level in range(L):
        a = acc[level] * (2.0**-LIFT)
        own.append(a[16:32] + lanes(a[0:16], 1) + lanes(a[32:48], -1) + outside)
        outer = a[48:64]
        before, after = lanes(outer, 1), lanes(outer, -1)
        below.append(outer[2:4] + before[0:2] + after[4:6])
        above.append(outer[10:12] + before[8:10] + after[12:14])
    total, total_up, total_down = own[0] + own[1], above[0] + above[1], below[0] + below[1]
    share = [stacked([total[8 * c : 8 * c + 8], placed([(0, total_up[c : c + 1]), (7, total_down[c : c + 1])])]) for c in range(2)]
    upper = own[1]

    ocean = joined([land_ref[...].astype(F32), zero[:, 0:128]])
    shift = joined([shift_ref[...], zero[:, 0:128]])

    def both(r):
        return [total[r : r + 1], total[8 + r : 9 + r]]

    none = [zero[0:1]]
    edge_n = stacked(
        [total_up] + both(7) + both(6) + both(5) + [above[1], ocean[7:8], ocean[6:7], ocean[5:6], shift[7:8]] + none * 2
    )
    edge_s = stacked(
        [total_down] + both(0) + both(1) + none * 2 + [below[1], ocean[0:1], ocean[1:2]] + none + [shift[0:1]] + none * 2
    )
    edge_e = stacked(share + [upper, ocean, shift])

    def eastern(x):
        return jnp.where(iota((x.shape[0], 128), 1) < 64, x[:, COLS:], x[:, COLS - 128 : COLS])

    def western(x):
        return jnp.where(iota((x.shape[0], 128), 1) < 64, x[:, 0:128], x[:, COLS:])

    corner = pl.ds(WIDE, 128), pl.ds(WIDE + 128, 128)
    for edge, ref in ((edge_n, north), (edge_s, south)):
        ref[:, 0:WIDE] = edge
        ref[:, WIDE : WIDE + 128] = eastern(edge)
        ref[:, WIDE + 128 :] = western(edge)
    to_east[...] = eastern(edge_e)
    to_west[...] = western(edge_e)

    whole, part = pl.ds(0, WIDE), pl.ds(0, 128)
    upward = jnp.where(top, 3, 0)
    sends = [
        (east_other, remote(north.at[:, corner[0]], got.at[upward + 1, :, part], send.at[1], recv.at[upward + 1], up_east, up_lat)),
        (west_other, remote(north.at[:, corner[1]], got.at[upward + 2, :, part], send.at[2], recv.at[upward + 2], up_west, up_lat)),
        (has_south, remote(south.at[:, corner[0]], got.at[4, :, part], send.at[4], recv.at[4], east, down_lat)),
        (has_south, remote(south.at[:, corner[1]], got.at[5, :, part], send.at[5], recv.at[5], west, down_lat)),
        (None, remote(north.at[:, whole], got.at[upward], send.at[0], recv.at[upward], up_lon, up_lat)),
        (has_south, remote(south.at[:, whole], got.at[3], send.at[3], recv.at[3], lon, down_lat)),
        (None, remote(to_east, side.at[0], send.at[6], recv.at[6], east, lat)),
        (None, remote(to_west, side.at[1], send.at[7], recv.at[7], west, lat)),
    ]

    def arrival(src, dst, k):
        return remote(src, dst, send.at[0], recv.at[k], east, lat)

    corner_n = north.at[:, corner[0]]
    arrivals = [
        (None, arrival(to_east, side.at[0], 6)),
        (None, arrival(to_west, side.at[1], 7)),
        (has_south, arrival(north.at[:, whole], got.at[0], 0)),
        (has_south, arrival(corner_n, got.at[1, :, part], 1)),
        (has_south, arrival(corner_n, got.at[2, :, part], 2)),
        (None, arrival(north.at[:, whole], got.at[3], 3)),
        (east_other, arrival(corner_n, got.at[4, :, part], 4)),
        (west_other, arrival(corner_n, got.at[5, :, part], 5)),
    ]

    def each(entries, act):
        for cond, copy in entries:
            if cond is None:
                act(copy)
            else:
                pl.when(cond)(functools.partial(act, copy))

    pl.semaphore_wait(barrier, greetings)
    each(sends, lambda copy: copy.start())

    @pl.when(east_self)
    def _():
        got[4, :, 0:128] = north[:, WIDE : WIDE + 128]

    @pl.when(west_self)
    def _():
        got[5, :, 0:128] = north[:, WIDE + 128 :]

    each(arrivals, lambda copy: copy.wait_recv())

    def arrived(k):
        parts = [got[k, :, 128 * t : 128 * t + 128] for t in range(5)]
        w, e = got[k + 1, :, 0:128], got[k + 2, :, 0:128]
        return [
            parts[0] + jnp.where(low2, w, 0.0), parts[1], parts[2],
            parts[3] + jnp.where(low2, 0.0, e), parts[4] + jnp.where(low2, e, w),
        ]

    backwards = 127 - lane

    def turned(x):
        return stacked([jnp.take_along_axis(x[r : r + 8], backwards, axis=1) for r in (0, 8)])

    s_rows = joined(arrived(0))
    n_parts = arrived(3)
    flipped = [turned(x) for x in n_parts]
    flipped = flipped[3::-1] + flipped[4:]
    n_rows = joined([jnp.where(top, f, n) for f, n in zip(flipped, n_parts)])
    from_west, from_east = side[0], side[1]

    def with_sides(x, at):
        count = x.shape[0]
        w, e = from_west[at : at + count], from_east[at : at + count]
        near = iota((count, 128), 1) < 64
        return joined([
            x[:, 0:128] + jnp.where(near, w, 0.0),
            x[:, 128 : COLS - 128],
            x[:, COLS - 128 : COLS] + jnp.where(near, 0.0, e),
            x[:, COLS:] + jnp.where(near, e, w),
        ])

    def one(x, k):
        return x[k : k + 1]

    m = stacked([
        with_sides(ocean, 48),
        placed([(r, one(n_rows, 10 + r)) for r in range(3)] + [(7 - r, one(s_rows, 10 + r)) for r in range(3)]),
    ])
    s = stacked([with_sides(shift, 56), placed([(0, one(n_rows, 13)), (7, one(s_rows, 13))])])
    eastward, northward = [
        m * (
            with_sides(share[c], 16 * c)
            + stacked([
                placed([(0, one(s_rows, c)), (7, one(n_rows, c))]),
                placed([(r, one(n_rows, 2 + 2 * r + c)) for r in range(3)] + [(7 - r, one(s_rows, 2 + 2 * r + c)) for r in range(3)]),
            ])
        )
        for c in range(2)
    ]
    r = m * (eastward - lanes(eastward, 1) + northward - rows(northward, 1))
    beyond = m * (eastward - lanes(eastward, -1) + northward - rows(northward, -1))
    r = stacked([r[0:8], jnp.where(top & (row < 2), beyond[8:16], r[8:16])])

    def operate(v):
        return m * ((4.0 + s) * v - (lanes(v, 1) + lanes(v, -1) + rows(v, 1) + rows(v, -1)))

    q1 = operate(r)
    q2 = operate(q1)[0:8, 0:COLS]
    r, q1 = r[0:8, 0:COLS], q1[0:8, 0:COLS]

    def summed(x):
        x = x[:, 0:128] + x[:, 128:256] + x[:, 256:384] + x[:, 384:512]
        return jnp.sum(x, axis=0, keepdims=True)

    dots = [summed(r * r), summed(r * q1), summed(q1 * q1), summed(r * q2), summed(q1 * q2)]

    def spread(value, ref, stage, here, devices):
        ref[here] = value
        copies = [remote(ref.at[here], ref.at[here], send_sum.at[stage], recv_sum.at[stage], *at) for at in devices[1:]]
        for copy in copies:
            copy.start()

    def collect(ref, stage, count):
        several = ref.at[pl.ds(0, count - 1)]
        copy = remote(several, several, send_sum.at[stage], recv_sum.at[stage], east, lat)
        copy.wait_recv()
        copy.wait_send()
        return jnp.sum(ref[...], axis=0)

    spread(stacked(dots + [jnp.zeros((3, 128), F32)]), sums_a, 0, first_here, first_sum)

    ocean = ocean[:, 0:COLS]
    upper = with_sides(upper, 32)
    for c in range(2):
        one_level = upper[8 * c : 8 * c + 8] + placed([(0, one(s_rows, 8 + c)), (7, one(n_rows, 8 + c))])
        one_level = ocean * one_level[:, 0:COLS]
        whole = (eastward, northward)[c][0:8, 0:COLS]
        tend_ref[c, 0] = (whole - one_level).astype(BF16)
        tend_ref[c, 1] = one_level.astype(BF16)
    for k, value in enumerate((r, q1, q2)):
        fields_ref[8 * k : 8 * k + 8, :] = value
    each(sends, lambda copy: copy.wait_send())

    spread(collect(sums_a, 0, n_lon), sums_b, 1, second_here, second_sum)
    sums_ref[...] = collect(sums_b, 1, n_lat)


def finish(fields_ref, sums_ref, tend_in, tend_ref, surf_ref, res_ref):
    r, q1, q2 = fields_ref[0:8, :], fields_ref[8:16, :], fields_ref[16:24, :]
    value = jnp.sum(sums_ref[...], axis=1, keepdims=True)
    rr, rq, qq, rq2, qq2 = [value[k : k + 1] for k in range(5)]
    a1 = rr / rq
    new = rr - 2.0 * a1 * rq + a1 * a1 * qq
    lead = 1.0 + new / rr
    a2 = new / (lead * lead * rq - lead * a1 * (rq2 + qq) + a1 * a1 * qq2)
    surf_ref[...] = a1 * r + a2 * (lead * r - a1 * q1)
    res_ref[...] = r - a1 * q1 - a2 * (lead * q1 - a1 * q2)
    tend_ref[...] = tend_in[...]


def body(features, spline_coef, edge_mask, head_weight, land_mask, shift_coef):
    n_lon, n_lat = lax.axis_size("lon"), lax.axis_size("lat")
    vmem = pl.BlockSpec(memory_space=pltpu.VMEM)
    dma = pltpu.SemaphoreType.DMA
    tend_shape = jax.ShapeDtypeStruct((2, L, ROWS, COLS), BF16)
    field_shape = jax.ShapeDtypeStruct((ROWS, COLS), F32)
    scratch = [
        pltpu.VMEM((C, L, ROWS, COLS), BF16),
        pltpu.VMEM((9 * C, C * J), BF16),
        pltpu.VMEM((C, C), jnp.int32),
        pltpu.VMEM((2, C), BF16),
        pltpu.VMEM((ROWS, COLS), jnp.int32),
        pltpu.VMEM((ROWS, COLS), F32),
        pltpu.VMEM((GROUPS, 64, 128 * J), BF16),
        pltpu.VMEM((128 * J, COLS), BF16),
        pltpu.VMEM((L, 64, WIDE), F32),
        pltpu.VMEM((16, WIDE + 256), F32),
        pltpu.VMEM((16, WIDE + 256), F32),
        pltpu.VMEM((64, 128), F32),
        pltpu.VMEM((64, 128), F32),
        pltpu.VMEM((6, 16, WIDE), F32),
        pltpu.VMEM((2, 64, 128), F32),
        pltpu.VMEM((n_lon, 8, 128), F32),
        pltpu.VMEM((n_lat, 8, 128), F32),
        dma((GROUPS,)), dma((5,)), dma((8,)), dma((8,)), dma((2,)), dma((2,)),
    ]
    tendency, fields, sums = pl.pallas_call(
        functools.partial(kernel, n_lon, n_lat),
        out_shape=(
            tend_shape,
            jax.ShapeDtypeStruct((3 * ROWS, COLS), F32),
            jax.ShapeDtypeStruct((8, 128), F32),
        ),
        in_specs=[pl.BlockSpec(memory_space=pl.ANY)] * 6,
        out_specs=(vmem, vmem, vmem),
        scratch_shapes=scratch,
        compiler_params=pltpu.CompilerParams(collective_id=0, has_side_effects=True),
        name="closure_and_sums",
    )(features, spline_coef, edge_mask, head_weight, land_mask, shift_coef)
    return pl.pallas_call(
        finish,
        out_shape=(tend_shape, field_shape, field_shape),
        in_specs=[vmem] * 3,
        out_specs=(vmem, vmem, vmem),
        name="finish",
    )(fields, sums, tendency)


def solution(mesh):
    in_specs = (P(None, None, "lat", "lon"), P(), P(), P(), P("lat", "lon"), P("lat", "lon"))
    out_specs = (P(None, None, "lat", "lon"), P("lat", "lon"), P("lat", "lon"))
    return jax.shard_map(body, mesh=mesh, in_specs=in_specs, out_specs=out_specs, check_vma=False)
```

```python
import functools
import math

import jax
import jax.numpy as jnp
from jax import lax
from jax.experimental import pallas as pl
from jax.experimental.pallas import tpu as pltpu
from jax.sharding import PartitionSpec as P

C = 48
NB = 9
J = NB + 1
L = 2
ROWS = 8
COLS = 512
WIDE = COLS + 128
F32 = jnp.float32
BF16 = jnp.bfloat16
MESH = pl.DeviceIdType.MESH
LOG2E = math.log2(math.e)
LIFT = 29
GROUP = 16
GROUPS = C // GROUP
STRIP = 2


def iota(shape, axis):
    return lax.broadcasted_iota(jnp.int32, shape, axis)


def dot(a, b):
    return jnp.dot(a, b, preferred_element_type=F32)


def ones_where(cond):
    return jnp.where(cond, 1.0, 0.0).astype(BF16)


def fold_weights(coef_ref, edge_ref, head_ref, wt, top):
    channel, lane = iota((C, C * J), 0), iota((C, C * J), 1)
    spread = ones_where((lane >= channel * J) & (lane < channel * J + J))
    keep = dot(jnp.where(edge_ref[...] > 0, 1.0, 0.0).astype(BF16), spread).astype(BF16)
    o, q = iota((C, 9 * C), 0), iota((C, 9 * C), 1)
    offset = lax.shift_right_logical(q * 1366, 16)
    head = dot(head_ref[...], ones_where(q - offset * C == o))
    r, q = iota((24, 9 * C), 0), iota((24, 9 * C), 1)
    offset = lax.shift_right_logical(q * 1366, 16)
    head = jnp.where((r & 1) == 0, head[0:1], head[1:2])
    head = jnp.where(lax.shift_right_logical(r, 1) == offset, head, 0.0).astype(BF16)
    folded = jnp.zeros((24, C * J), F32)
    masked = [coef_ref[C * k : C * k + C, :] * keep for k in range(9)]
    folded = dot(head, jnp.concatenate(masked, axis=0))
    lane = iota((1, C * J), 1)
    j = lane - J * lax.shift_right_logical(lane * 6554, 16)
    scale = jnp.where((j == 0) | (j == 8), math.exp(-6.0), jnp.where((j == 2) | (j == 6), math.exp(6.0), 1.0))
    folded = (folded * scale).astype(BF16)
    q = iota((1, 64 * J), 1)
    source = jnp.where((q & 63) < C, (q & 63) * J + lax.shift_right_logical(q, 6), -1)
    folded = dot(folded, ones_where(iota((C * J, 64 * J), 0) == source)).astype(BF16)
    q = iota((1, 2 * C * ROWS), 1)
    second = jnp.where(q >= C * ROWS, 1, 0)
    source = second * 64 + lax.shift_right_logical(q - second * (C * ROWS), 3)
    expand = ones_where(iota((128, 2 * C * ROWS), 0) == source)
    y_out = iota((ROWS, 2 * C * ROWS), 0)
    y_in = iota((ROWS, 2 * C * ROWS), 1) & 7
    first_row, last_row = y_in[0:6] == 0, y_in[0:6] == 7
    pad = jnp.zeros((2, 2 * C * ROWS), F32)
    for pair in range(J // 2):
        g = dot(folded[:, 128 * pair : 128 * pair + 128], expand)
        tiles = []
        for k in range(6):
            tile = jnp.where(y_in == y_out - 1, g[k : k + 1], 0.0)
            tile = jnp.where(y_in == y_out, g[6 + k : 7 + k], tile)
            tiles.append(jnp.where(y_in == y_out + 1, g[12 + k : 13 + k], tile))
        mirrored = jnp.concatenate([g[16:18], g[14:16], g[12:14]], axis=0)
        above = jnp.where(top, mirrored, g[0:6])
        tiles += [jnp.where(first_row, g[12:18], 0.0), pad, jnp.where(last_row, above, 0.0), pad]
        block = jnp.concatenate(tiles, axis=0).astype(BF16)
        for half in range(2):
            j = 2 * pair + half
            for group in range(GROUPS):
                at = half * C * ROWS + group * 128
                wt[group, :, 128 * j : 128 * j + 128] = block[:, at : at + 128]


def basis(x):
    base = (x * x) * (-4.0 * LOG2E)
    outer = base + (LIFT - 9.0 * LOG2E)
    slope = x * (12.0 * LOG2E)
    step = x * (4.0 * LOG2E)
    up = jnp.exp2(step - LOG2E)
    down = jnp.exp2(-LOG2E - step)
    left = jnp.exp2(outer - slope)
    middle = jnp.exp2(base + float(LIFT))
    right = jnp.exp2(outer + slope)
    half = x * (0.5 * 2.0**LIFT)
    silu = half + half * jnp.tanh(x * 0.5)
    return [left * down, left, left * up, middle * down, middle, middle * up, right * down, right, right * up, silu]


def bits(value, flips):
    return jnp.bitwise_xor(value, flips) if flips else value


def kernel(
    n_lon, n_lat,
    feat_hbm, coef_hbm, edge_hbm, head_hbm, land_hbm, shift_hbm,
    tend_ref, fields_ref, sums_ref,
    feat, coef_ref, edge_ref, head_ref, land_ref, shift_ref, wt, bases, acc,
    north, south, to_east, to_west, got, side, sums_a, sums_b,
    feat_sem, weight_sem, send, recv, send_sum, recv_sum,
):
    lon, lat = lax.axis_index("lon"), lax.axis_index("lat")
    top, bottom = lat == n_lat - 1, lat == 0
    east = jnp.where(lon == n_lon - 1, 0, lon + 1)
    west = jnp.where(lon == 0, n_lon - 1, lon - 1)
    up_lat = jnp.where(top, lat, lat + 1)
    up_lon = jnp.where(top, n_lon - 1 - lon, lon)
    up_east = jnp.where(top, n_lon - 1 - east, east)
    up_west = jnp.where(top, n_lon - 1 - west, west)
    down_lat = jnp.where(bottom, lat, lat - 1)
    east_self, west_self = top & (up_east == lon), top & (up_west == lon)
    east_other, west_other = jnp.logical_not(east_self), jnp.logical_not(west_self)
    has_south = jnp.logical_not(bottom)

    weights_in = [
        pltpu.make_async_copy(src, dst, weight_sem.at[k])
        for k, (src, dst) in enumerate(
            [(edge_hbm, edge_ref), (head_hbm, head_ref), (coef_hbm, coef_ref), (land_hbm, land_ref), (shift_hbm, shift_ref)]
        )
    ]

    def feat_in(k):
        part = pl.ds(k * GROUP, GROUP)
        return pltpu.make_async_copy(feat_hbm.at[part], feat.at[part], feat_sem.at[k])

    for copy in weights_in + [feat_in(k) for k in range(GROUPS)]:
        copy.start()

    half = n_lon // 2
    first_sum = [(bits(lon, 2 * (d % half)), bits(lat, d // half)) for d in range(n_lon)]
    first_here = lon // 2 + half * lax.rem(lat, 2)
    second_sum = [(bits(lon, d % 2), bits(lat, d - d % 2)) for d in range(n_lat)]
    second_here = lat - lax.rem(lat, 2) + lax.rem(lon, 2)

    barrier = pltpu.get_barrier_semaphore()

    def greet(at_lon, at_lat):
        pl.semaphore_signal(barrier, inc=1, device_id={"lon": at_lon, "lat": at_lat}, device_id_type=MESH)

    greet(east, lat)
    greet(west, lat)
    greet(up_lon, up_lat)
    pl.when(east_other)(lambda: greet(up_east, up_lat))
    pl.when(west_other)(lambda: greet(up_west, up_lat))

    @pl.when(has_south)
    def _():
        greet(lon, down_lat)
        greet(east, down_lat)
        greet(west, down_lat)

    for at in first_sum[1:] + second_sum[1:]:
        greet(*at)
    greetings = n_lon + n_lat + 6 - jnp.where(east_self, 1, 0) - jnp.where(west_self, 1, 0) - jnp.where(bottom, 3, 0)

    def remote(src, dst, send, recv, at_lon, at_lat):
        return pltpu.make_async_remote_copy(
            src_ref=src, dst_ref=dst, send_sem=send, recv_sem=recv,
            device_id={"lon": at_lon, "lat": at_lat}, device_id_type=MESH,
        )

    @pl.when(bottom)
    def _():
        got[0:3] = jnp.zeros((3, 16, WIDE), F32)

    for copy in weights_in:
        copy.wait()
    fold_weights(coef_ref, edge_ref, head_ref, wt, top)

    acc[...] = jnp.zeros(acc.shape, F32)

    def step(k, carry):
        group, level = k // L, lax.rem(k, L)
        pl.when(level == 0)(lambda: feat_in(group).wait())
        for at in range(0, GROUP, STRIP):
            x = feat[pl.ds(group * GROUP + at, STRIP), level].astype(F32).reshape(STRIP * ROWS, COLS)
            for j, value in enumerate(basis(x)):
                row = 128 * j + ROWS * at
                bases[row : row + ROWS * STRIP, :] = value.astype(BF16)
        acc[level, :, 0:COLS] += dot(wt[group], bases[...])
        return carry

    lax.fori_loop(0, GROUPS * L, step, 0)

    lane, low = iota((ROWS, 128), 1), iota((ROWS, 128), 1) < 64
    low2 = iota((16, 128), 1) < 64
    row = iota((ROWS, WIDE), 0)
    zero = jnp.zeros((ROWS, WIDE), F32)

    def joined(parts):
        return jnp.concatenate(parts, axis=1)

    def stacked(parts):
        return jnp.concatenate(parts, axis=0)

    def lanes(x, by):
        return pltpu.roll(x, by % WIDE, 1)

    def rows(x, by):
        return pltpu.roll(x, by % 16, 0)

    def placed(entries):
        out = zero
        for at, value in entries:
            out = jnp.where(row == at, value, out)
        return out

    j = lax.shift_right_logical(iota((1, 128 * J), 1), 7)
    off = jnp.abs(j - 4)
    still = jnp.where(off == 1, math.exp(-1.0), jnp.where(off == 3, math.exp(-9.0), math.exp(-10.0)))
    still = jnp.where(off == 0, 1.0, jnp.where(j == NB, 0.0, still))
    outside = jnp.zeros((8, 128 * J), F32)
    for group in range(GROUPS):
        outside = outside + wt[group, 48:64, :].astype(F32)[8:16]
    outside = jnp.where(bottom, jnp.sum(outside * still, axis=1, keepdims=True), 0.0)
    outside = outside[0:2] + outside[2:4] + outside[4:6]
    first_row = (iota((ROWS, WIDE), 0) == 0) & (iota((ROWS, WIDE), 1) < COLS)
    outside = stacked([jnp.where(first_row, outside[c : c + 1], 0.0) for c in range(2)])

    own, above, below = [], [], []
    for level in range(L):
        a = acc[level] * (2.0**-LIFT)
        own.append(a[16:32] + lanes(a[0:16], 1) + lanes(a[32:48], -1) + outside)
        outer = a[48:64]
        before, after = lanes(outer, 1), lanes(outer, -1)
        below.append(outer[2:4] + before[0:2] + after[4:6])
        above.append(outer[10:12] + before[8:10] + after[12:14])
    total, total_up, total_down = own[0] + own[1], above[0] + above[1], below[0] + below[1]
    share = [stacked([total[8 * c : 8 * c + 8], placed([(0, total_up[c : c + 1]), (7, total_down[c : c + 1])])]) for c in range(2)]
    upper = own[1]

    ocean = joined([land_ref[...].astype(F32), zero[:, 0:128]])
    shift = joined([shift_ref[...], zero[:, 0:128]])

    def both(r):
        return [total[r : r + 1], total[8 + r : 9 + r]]

    none = [zero[0:1]]
    edge_n = stacked(
        [total_up] + both(7) + both(6) + both(5) + [above[1], ocean[7:8], ocean[6:7], ocean[5:6], shift[7:8]] + none * 2
    )
    edge_s = stacked(
        [total_down] + both(0) + both(1) + none * 2 + [below[1], ocean[0:1], ocean[1:2]] + none + [shift[0:1]] + none * 2
    )
    edge_e = stacked(share + [upper, ocean, shift])

    def eastern(x):
        return jnp.where(iota((x.shape[0], 128), 1) < 64, x[:, COLS:], x[:, COLS - 128 : COLS])

    def western(x):
        return jnp.where(iota((x.shape[0], 128), 1) < 64, x[:, 0:128], x[:, COLS:])

    corner = pl.ds(WIDE, 128), pl.ds(WIDE + 128, 128)
    for edge, ref in ((edge_n, north), (edge_s, south)):
        ref[:, 0:WIDE] = edge
        ref[:, WIDE : WIDE + 128] = eastern(edge)
        ref[:, WIDE + 128 :] = western(edge)
    to_east[...] = eastern(edge_e)
    to_west[...] = western(edge_e)

    whole, part = pl.ds(0, WIDE), pl.ds(0, 128)
    upward = jnp.where(top, 3, 0)
    sends = [
        (east_other, remote(north.at[:, corner[0]], got.at[upward + 1, :, part], send.at[1], recv.at[upward + 1], up_east, up_lat)),
        (west_other, remote(north.at[:, corner[1]], got.at[upward + 2, :, part], send.at[2], recv.at[upward + 2], up_west, up_lat)),
        (has_south, remote(south.at[:, corner[0]], got.at[4, :, part], send.at[4], recv.at[4], east, down_lat)),
        (has_south, remote(south.at[:, corner[1]], got.at[5, :, part], send.at[5], recv.at[5], west, down_lat)),
        (None, remote(north.at[:, whole], got.at[upward], send.at[0], recv.at[upward], up_lon, up_lat)),
        (has_south, remote(south.at[:, whole], got.at[3], send.at[3], recv.at[3], lon, down_lat)),
        (None, remote(to_east, side.at[0], send.at[6], recv.at[6], east, lat)),
        (None, remote(to_west, side.at[1], send.at[7], recv.at[7], west, lat)),
    ]

    def arrival(src, dst, k):
        return remote(src, dst, send.at[0], recv.at[k], east, lat)

    corner_n = north.at[:, corner[0]]
    arrivals = [
        (None, arrival(to_east, side.at[0], 6)),
        (None, arrival(to_west, side.at[1], 7)),
        (has_south, arrival(north.at[:, whole], got.at[0], 0)),
        (has_south, arrival(corner_n, got.at[1, :, part], 1)),
        (has_south, arrival(corner_n, got.at[2, :, part], 2)),
        (None, arrival(north.at[:, whole], got.at[3], 3)),
        (east_other, arrival(corner_n, got.at[4, :, part], 4)),
        (west_other, arrival(corner_n, got.at[5, :, part], 5)),
    ]

    def each(entries, act):
        for cond, copy in entries:
            if cond is None:
                act(copy)
            else:
                pl.when(cond)(functools.partial(act, copy))

    pl.semaphore_wait(barrier, greetings)
    each(sends, lambda copy: copy.start())

    @pl.when(east_self)
    def _():
        got[4, :, 0:128] = north[:, WIDE : WIDE + 128]

    @pl.when(west_self)
    def _():
        got[5, :, 0:128] = north[:, WIDE + 128 :]

    each(arrivals, lambda copy: copy.wait_recv())

    def arrived(k):
        parts = [got[k, :, 128 * t : 128 * t + 128] for t in range(5)]
        w, e = got[k + 1, :, 0:128], got[k + 2, :, 0:128]
        return [
            parts[0] + jnp.where(low2, w, 0.0), parts[1], parts[2],
            parts[3] + jnp.where(low2, 0.0, e), parts[4] + jnp.where(low2, e, w),
        ]

    backwards = 127 - lane

    def turned(x):
        return stacked([jnp.take_along_axis(x[r : r + 8], backwards, axis=1) for r in (0, 8)])

    s_rows = joined(arrived(0))
    n_parts = arrived(3)
    flipped = [turned(x) for x in n_parts]
    flipped = flipped[3::-1] + flipped[4:]
    n_rows = joined([jnp.where(top, f, n) for f, n in zip(flipped, n_parts)])
    from_west, from_east = side[0], side[1]

    def with_sides(x, at):
        count = x.shape[0]
        w, e = from_west[at : at + count], from_east[at : at + count]
        near = iota((count, 128), 1) < 64
        return joined([
            x[:, 0:128] + jnp.where(near, w, 0.0),
            x[:, 128 : COLS - 128],
            x[:, COLS - 128 : COLS] + jnp.where(near, 0.0, e),
            x[:, COLS:] + jnp.where(near, e, w),
        ])

    def one(x, k):
        return x[k : k + 1]

    m = stacked([
        with_sides(ocean, 48),
        placed([(r, one(n_rows, 10 + r)) for r in range(3)] + [(7 - r, one(s_rows, 10 + r)) for r in range(3)]),
    ])
    s = stacked([with_sides(shift, 56), placed([(0, one(n_rows, 13)), (7, one(s_rows, 13))])])
    eastward, northward = [
        m * (
            with_sides(share[c], 16 * c)
            + stacked([
                placed([(0, one(s_rows, c)), (7, one(n_rows, c))]),
                placed([(r, one(n_rows, 2 + 2 * r + c)) for r in range(3)] + [(7 - r, one(s_rows, 2 + 2 * r + c)) for r in range(3)]),
            ])
        )
        for c in range(2)
    ]
    r = m * (eastward - lanes(eastward, 1) + northward - rows(northward, 1))
    beyond = m * (eastward - lanes(eastward, -1) + northward - rows(northward, -1))
    r = stacked([r[0:8], jnp.where(top & (row < 2), beyond[8:16], r[8:16])])

    def operate(v):
        return m * ((4.0 + s) * v - (lanes(v, 1) + lanes(v, -1) + rows(v, 1) + rows(v, -1)))

    q1 = operate(r)
    q2 = operate(q1)[0:8, 0:COLS]
    r, q1 = r[0:8, 0:COLS], q1[0:8, 0:COLS]

    def summed(x):
        x = x[:, 0:128] + x[:, 128:256] + x[:, 256:384] + x[:, 384:512]
        return jnp.sum(x, axis=0, keepdims=True)

    dots = [summed(r * r), summed(r * q1), summed(q1 * q1), summed(r * q2), summed(q1 * q2)]

    def spread(value, ref, stage, here, devices):
        ref[here] = value
        copies = [remote(ref.at[here], ref.at[here], send_sum.at[stage], recv_sum.at[stage], *at) for at in devices[1:]]
        for copy in copies:
            copy.start()

    def all_copies(ref, stage, count):
        several = ref.at[pl.ds(0, count - 1)]
        return remote(several, several, send_sum.at[stage], recv_sum.at[stage], east, lat)

    def collect(ref, stage, count):
        all_copies(ref, stage, count).wait_recv()
        return jnp.sum(ref[...], axis=0)

    dots = jnp.sum(stacked(dots + [jnp.zeros((3, 128), F32)]), axis=1, keepdims=True)
    dots = jnp.sum(jnp.where(lane == iota((ROWS, 128), 0), dots, 0.0), axis=0, keepdims=True)
    spread(dots, sums_a, 0, first_here, first_sum)

    ocean = ocean[:, 0:COLS]
    upper = with_sides(upper, 32)
    for c in range(2):
        one_level = upper[8 * c : 8 * c + 8] + placed([(0, one(s_rows, 8 + c)), (7, one(n_rows, 8 + c))])
        one_level = ocean * one_level[:, 0:COLS]
        whole = (eastward, northward)[c][0:8, 0:COLS]
        tend_ref[c, 0] = (whole - one_level).astype(BF16)
        tend_ref[c, 1] = one_level.astype(BF16)
    for k, value in enumerate((r, q1, q2)):
        fields_ref[8 * k : 8 * k + 8, :] = value
    each(sends, lambda copy: copy.wait_send())

    spread(collect(sums_a, 0, n_lon), sums_b, 1, second_here, second_sum)
    sums_ref[...] = collect(sums_b, 1, n_lat)
    all_copies(sums_a, 0, n_lon).wait_send()
    all_copies(sums_b, 1, n_lat).wait_send()


def finish(fields_ref, sums_ref, tend_in, tend_ref, surf_ref, res_ref):
    r, q1, q2 = fields_ref[0:8, :], fields_ref[8:16, :], fields_ref[16:24, :]
    rr, rq, qq, rq2, qq2 = [sums_ref[0:1, k : k + 1] for k in range(5)]
    a1 = rr / rq
    new = rr - 2.0 * a1 * rq + a1 * a1 * qq
    lead = 1.0 + new / rr
    a2 = new / (lead * lead * rq - lead * a1 * (rq2 + qq) + a1 * a1 * qq2)
    surf_ref[...] = a1 * r + a2 * (lead * r - a1 * q1)
    res_ref[...] = r - a1 * q1 - a2 * (lead * q1 - a1 * q2)
    tend_ref[...] = tend_in[...]


def body(features, spline_coef, edge_mask, head_weight, land_mask, shift_coef):
    n_lon, n_lat = lax.axis_size("lon"), lax.axis_size("lat")
    vmem = pl.BlockSpec(memory_space=pltpu.VMEM)
    dma = pltpu.SemaphoreType.DMA
    tend_shape = jax.ShapeDtypeStruct((2, L, ROWS, COLS), BF16)
    field_shape = jax.ShapeDtypeStruct((ROWS, COLS), F32)
    scratch = [
        pltpu.VMEM((C, L, ROWS, COLS), BF16),
        pltpu.VMEM((9 * C, C * J), BF16),
        pltpu.VMEM((C, C), jnp.int32),
        pltpu.VMEM((2, C), BF16),
        pltpu.VMEM((ROWS, COLS), jnp.int32),
        pltpu.VMEM((ROWS, COLS), F32),
        pltpu.VMEM((GROUPS, 64, 128 * J), BF16),
        pltpu.VMEM((128 * J, COLS), BF16),
        pltpu.VMEM((L, 64, WIDE), F32),
        pltpu.VMEM((16, WIDE + 256), F32),
        pltpu.VMEM((16, WIDE + 256), F32),
        pltpu.VMEM((64, 128), F32),
        pltpu.VMEM((64, 128), F32),
        pltpu.VMEM((6, 16, WIDE), F32),
        pltpu.VMEM((2, 64, 128), F32),
        pltpu.VMEM((n_lon, 1, 128), F32),
        pltpu.VMEM((n_lat, 1, 128), F32),
        dma((GROUPS,)), dma((5,)), dma((8,)), dma((8,)), dma((2,)), dma((2,)),
    ]
    tendency, fields, sums = pl.pallas_call(
        functools.partial(kernel, n_lon, n_lat),
        out_shape=(
            pltpu.VMEM((2, L, ROWS, COLS), BF16),
            pltpu.VMEM((3 * ROWS, COLS), F32),
            pltpu.VMEM((1, 128), F32),
        ),
        in_specs=[pl.BlockSpec(memory_space=pl.ANY)] * 6,
        out_specs=(vmem, vmem, vmem),
        scratch_shapes=scratch,
        compiler_params=pltpu.CompilerParams(collective_id=0, has_side_effects=True),
        name="closure_and_sums",
    )(features, spline_coef, edge_mask, head_weight, land_mask, shift_coef)
    return pl.pallas_call(
        finish,
        out_shape=(tend_shape, field_shape, field_shape),
        in_specs=[vmem] * 3,
        out_specs=(vmem, vmem, vmem),
        compiler_params=pltpu.CompilerParams(vmem_limit_bytes=4 * 1024 * 1024),
        name="finish",
    )(fields, sums, tendency)


def solution(mesh):
    in_specs = (P(None, None, "lat", "lon"), P(), P(), P(), P("lat", "lon"), P("lat", "lon"))
    out_specs = (P(None, None, "lat", "lon"), P("lat", "lon"), P("lat", "lon"))
    return jax.shard_map(body, mesh=mesh, in_specs=in_specs, out_specs=out_specs, check_vma=False)
```

```python
import functools
import math

import jax
import jax.numpy as jnp
from jax import lax
from jax.experimental import pallas as pl
from jax.experimental.pallas import tpu as pltpu
from jax.sharding import PartitionSpec as P

C = 48
NB = 9
J = NB + 1
L = 2
ROWS = 8
COLS = 512
WIDE = COLS + 128
F32 = jnp.float32
BF16 = jnp.bfloat16
MESH = pl.DeviceIdType.MESH
LOG2E = math.log2(math.e)
LIFT = 82
GROUP = 16
GROUPS = C // GROUP
STRIP = 2


def iota(shape, axis):
    return lax.broadcasted_iota(jnp.int32, shape, axis)


def dot(a, b):
    return jnp.dot(a, b, preferred_element_type=F32)


def ones_where(cond):
    return jnp.where(cond, 1.0, 0.0).astype(BF16)


def fold_weights(coef_ref, edge_ref, head_ref, wt, top):
    channel, lane = iota((C, C * J), 0), iota((C, C * J), 1)
    spread = ones_where((lane >= channel * J) & (lane < channel * J + J))
    keep = dot(jnp.where(edge_ref[...] > 0, 1.0, 0.0).astype(BF16), spread).astype(BF16)
    o, q = iota((C, 9 * C), 0), iota((C, 9 * C), 1)
    offset = lax.shift_right_logical(q * 1366, 16)
    head = dot(head_ref[...], ones_where(q - offset * C == o))
    r, q = iota((24, 9 * C), 0), iota((24, 9 * C), 1)
    offset = lax.shift_right_logical(q * 1366, 16)
    head = jnp.where((r & 1) == 0, head[0:1], head[1:2])
    head = jnp.where(lax.shift_right_logical(r, 1) == offset, head, 0.0).astype(BF16)
    folded = jnp.zeros((24, C * J), F32)
    masked = [coef_ref[C * k : C * k + C, :] * keep for k in range(9)]
    folded = dot(head, jnp.concatenate(masked, axis=0))
    lane = iota((1, C * J), 1)
    j = lane - J * lax.shift_right_logical(lane * 6554, 16)
    off = jnp.abs(j - NB // 2).astype(F32)
    scale = jnp.where(j == NB, 2.0**LIFT, jnp.exp(-off * off))
    folded = (folded * scale).astype(BF16)
    q = iota((1, 64 * J), 1)
    source = jnp.where((q & 63) < C, (q & 63) * J + lax.shift_right_logical(q, 6), -1)
    folded = dot(folded, ones_where(iota((C * J, 64 * J), 0) == source)).astype(BF16)
    q = iota((1, 2 * C * ROWS), 1)
    second = jnp.where(q >= C * ROWS, 1, 0)
    source = second * 64 + lax.shift_right_logical(q - second * (C * ROWS), 3)
    expand = ones_where(iota((128, 2 * C * ROWS), 0) == source)
    y_out = iota((ROWS, 2 * C * ROWS), 0)
    y_in = iota((ROWS, 2 * C * ROWS), 1) & 7
    first_row, last_row = y_in[0:6] == 0, y_in[0:6] == 7
    pad = jnp.zeros((2, 2 * C * ROWS), F32)
    for pair in range(J // 2):
        g = dot(folded[:, 128 * pair : 128 * pair + 128], expand)
        tiles = []
        for k in range(6):
            tile = jnp.where(y_in == y_out - 1, g[k : k + 1], 0.0)
            tile = jnp.where(y_in == y_out, g[6 + k : 7 + k], tile)
            tiles.append(jnp.where(y_in == y_out + 1, g[12 + k : 13 + k], tile))
        mirrored = jnp.concatenate([g[16:18], g[14:16], g[12:14]], axis=0)
        above = jnp.where(top, mirrored, g[0:6])
        tiles += [jnp.where(first_row, g[12:18], 0.0), pad, jnp.where(last_row, above, 0.0), pad]
        block = jnp.concatenate(tiles, axis=0).astype(BF16)
        for half in range(2):
            j = 2 * pair + half
            for group in range(GROUPS):
                at = half * C * ROWS + group * 128
                wt[group, :, 128 * j : 128 * j + 128] = block[:, at : at + 128]


def basis(x):
    half = x * 0.5
    middle = jnp.exp2((half * half) * (-16.0 * LOG2E) + float(LIFT))
    up = jnp.exp2(half * (8.0 * LOG2E))
    down = jnp.exp2(half * (-8.0 * LOG2E))
    silu = half + half * jnp.tanh(half)
    left, right = [middle], [middle]
    for _ in range(NB // 2):
        left.append(left[-1] * down)
        right.append(right[-1] * up)
    return left[:0:-1] + right + [silu]


def bits(value, flips):
    return jnp.bitwise_xor(value, flips) if flips else value


def kernel(
    n_lon, n_lat,
    feat_hbm, coef_hbm, edge_hbm, head_hbm, land_hbm, shift_hbm,
    tend_ref, fields_ref, sums_ref,
    feat, coef_ref, edge_ref, head_ref, land_ref, shift_ref, wt, bases, acc,
    north, south, to_east, to_west, got, side, sums_a, sums_b,
    feat_sem, weight_sem, send, recv, send_sum, recv_sum,
):
    lon, lat = lax.axis_index("lon"), lax.axis_index("lat")
    top, bottom = lat == n_lat - 1, lat == 0
    east = jnp.where(lon == n_lon - 1, 0, lon + 1)
    west = jnp.where(lon == 0, n_lon - 1, lon - 1)
    up_lat = jnp.where(top, lat, lat + 1)
    up_lon = jnp.where(top, n_lon - 1 - lon, lon)
    up_east = jnp.where(top, n_lon - 1 - east, east)
    up_west = jnp.where(top, n_lon - 1 - west, west)
    down_lat = jnp.where(bottom, lat, lat - 1)
    east_self, west_self = top & (up_east == lon), top & (up_west == lon)
    east_other, west_other = jnp.logical_not(east_self), jnp.logical_not(west_self)
    has_south = jnp.logical_not(bottom)

    weights_in = [
        pltpu.make_async_copy(src, dst, weight_sem.at[k])
        for k, (src, dst) in enumerate(
            [(edge_hbm, edge_ref), (head_hbm, head_ref), (coef_hbm, coef_ref), (land_hbm, land_ref), (shift_hbm, shift_ref)]
        )
    ]

    def feat_in(k):
        part = pl.ds(k * GROUP, GROUP)
        return pltpu.make_async_copy(feat_hbm.at[part], feat.at[part], feat_sem.at[k])

    for copy in weights_in + [feat_in(k) for k in range(GROUPS)]:
        copy.start()

    half = n_lon // 2
    first_sum = [(bits(lon, d % 2), bits(lat, d - d % 2)) for d in range(n_lat)]
    first_here = lat - lax.rem(lat, 2) + lax.rem(lon, 2)
    second_sum = [(bits(lon, 2 * (d % half)), bits(lat, d // half)) for d in range(n_lon)]
    second_here = lon // 2 + half * lax.rem(lat, 2)

    barrier = pltpu.get_barrier_semaphore()

    def greet(at_lon, at_lat):
        pl.semaphore_signal(barrier, inc=1, device_id={"lon": at_lon, "lat": at_lat}, device_id_type=MESH)

    greet(east, lat)
    greet(west, lat)
    greet(up_lon, up_lat)
    pl.when(east_other)(lambda: greet(up_east, up_lat))
    pl.when(west_other)(lambda: greet(up_west, up_lat))

    @pl.when(has_south)
    def _():
        greet(lon, down_lat)
        greet(east, down_lat)
        greet(west, down_lat)

    for at in first_sum[1:] + second_sum[1:]:
        greet(*at)
    greetings = n_lon + n_lat + 6 - jnp.where(east_self, 1, 0) - jnp.where(west_self, 1, 0) - jnp.where(bottom, 3, 0)

    def remote(src, dst, send, recv, at_lon, at_lat):
        return pltpu.make_async_remote_copy(
            src_ref=src, dst_ref=dst, send_sem=send, recv_sem=recv,
            device_id={"lon": at_lon, "lat": at_lat}, device_id_type=MESH,
        )

    @pl.when(bottom)
    def _():
        got[0:3] = jnp.zeros((3, 16, WIDE), F32)

    for copy in weights_in:
        copy.wait()
    fold_weights(coef_ref, edge_ref, head_ref, wt, top)

    acc[...] = jnp.zeros(acc.shape, F32)

    def step(k, carry):
        group, level = k // L, lax.rem(k, L)
        pl.when(level == 0)(lambda: feat_in(group).wait())
        for at in range(0, GROUP, STRIP):
            x = feat[pl.ds(group * GROUP + at, STRIP), level].astype(F32).reshape(STRIP * ROWS, COLS)
            for j, value in enumerate(basis(x)):
                row = 128 * j + ROWS * at
                bases[row : row + ROWS * STRIP, :] = value.astype(BF16)
        acc[level, :, 0:COLS] += dot(wt[group], bases[...])
        return carry

    lax.fori_loop(0, GROUPS * L, step, 0)

    lane, low = iota((ROWS, 128), 1), iota((ROWS, 128), 1) < 64
    low2 = iota((16, 128), 1) < 64
    row = iota((ROWS, WIDE), 0)
    zero = jnp.zeros((ROWS, WIDE), F32)

    def joined(parts):
        return jnp.concatenate(parts, axis=1)

    def stacked(parts):
        return jnp.concatenate(parts, axis=0)

    def lanes(x, by):
        return pltpu.roll(x, by % WIDE, 1)

    def rows(x, by):
        return pltpu.roll(x, by % 16, 0)

    def placed(entries):
        out = zero
        for at, value in entries:
            out = jnp.where(row == at, value, out)
        return out

    j = lax.shift_right_logical(iota((1, 128 * J), 1), 7)
    still = jnp.where(j == NB, 0.0, 1.0)
    outside = jnp.zeros((8, 128 * J), F32)
    for group in range(GROUPS):
        outside = outside + wt[group, 48:64, :].astype(F32)[8:16]
    outside = jnp.where(bottom, jnp.sum(outside * still, axis=1, keepdims=True), 0.0)
    outside = outside[0:2] + outside[2:4] + outside[4:6]
    first_row = (iota((ROWS, WIDE), 0) == 0) & (iota((ROWS, WIDE), 1) < COLS)
    outside = stacked([jnp.where(first_row, outside[c : c + 1], 0.0) for c in range(2)])

    own, above, below = [], [], []
    for level in range(L):
        a = acc[level] * (2.0**-LIFT)
        own.append(a[16:32] + lanes(a[0:16], 1) + lanes(a[32:48], -1) + outside)
        outer = a[48:64]
        before, after = lanes(outer, 1), lanes(outer, -1)
        below.append(outer[2:4] + before[0:2] + after[4:6])
        above.append(outer[10:12] + before[8:10] + after[12:14])
    total, total_up, total_down = own[0] + own[1], above[0] + above[1], below[0] + below[1]
    share = [stacked([total[8 * c : 8 * c + 8], placed([(0, total_up[c : c + 1]), (7, total_down[c : c + 1])])]) for c in range(2)]
    upper = own[1]

    ocean = joined([land_ref[...].astype(F32), zero[:, 0:128]])
    shift = joined([shift_ref[...], zero[:, 0:128]])

    def both(r):
        return [total[r : r + 1], total[8 + r : 9 + r]]

    none = [zero[0:1]]
    edge_n = stacked(
        [total_up] + both(7) + both(6) + both(5) + [above[1], ocean[7:8], ocean[6:7], ocean[5:6], shift[7:8]] + none * 2
    )
    edge_s = stacked(
        [total_down] + both(0) + both(1) + none * 2 + [below[1], ocean[0:1], ocean[1:2]] + none + [shift[0:1]] + none * 2
    )
    edge_e = stacked(share + [upper, ocean, shift])

    def eastern(x):
        return jnp.where(iota((x.shape[0], 128), 1) < 64, x[:, COLS:], x[:, COLS - 128 : COLS])

    def western(x):
        return jnp.where(iota((x.shape[0], 128), 1) < 64, x[:, 0:128], x[:, COLS:])

    corner = pl.ds(WIDE, 128), pl.ds(WIDE + 128, 128)
    for edge, ref in ((edge_n, north), (edge_s, south)):
        ref[:, 0:WIDE] = edge
        ref[:, WIDE : WIDE + 128] = eastern(edge)
        ref[:, WIDE + 128 :] = western(edge)
    to_east[...] = eastern(edge_e)
    to_west[...] = western(edge_e)

    whole, part = pl.ds(0, WIDE), pl.ds(0, 128)
    upward = jnp.where(top, 3, 0)
    sends = [
        (east_other, remote(north.at[:, corner[0]], got.at[upward + 1, :, part], send.at[1], recv.at[upward + 1], up_east, up_lat)),
        (west_other, remote(north.at[:, corner[1]], got.at[upward + 2, :, part], send.at[2], recv.at[upward + 2], up_west, up_lat)),
        (has_south, remote(south.at[:, corner[0]], got.at[4, :, part], send.at[4], recv.at[4], east, down_lat)),
        (has_south, remote(south.at[:, corner[1]], got.at[5, :, part], send.at[5], recv.at[5], west, down_lat)),
        (None, remote(north.at[:, whole], got.at[upward], send.at[0], recv.at[upward], up_lon, up_lat)),
        (has_south, remote(south.at[:, whole], got.at[3], send.at[3], recv.at[3], lon, down_lat)),
        (None, remote(to_east, side.at[0], send.at[6], recv.at[6], east, lat)),
        (None, remote(to_west, side.at[1], send.at[7], recv.at[7], west, lat)),
    ]

    def arrival(src, dst, k):
        return remote(src, dst, send.at[0], recv.at[k], east, lat)

    corner_n = north.at[:, corner[0]]
    arrivals = [
        (None, arrival(to_east, side.at[0], 6)),
        (None, arrival(to_west, side.at[1], 7)),
        (has_south, arrival(north.at[:, whole], got.at[0], 0)),
        (has_south, arrival(corner_n, got.at[1, :, part], 1)),
        (has_south, arrival(corner_n, got.at[2, :, part], 2)),
        (None, arrival(north.at[:, whole], got.at[3], 3)),
        (east_other, arrival(corner_n, got.at[4, :, part], 4)),
        (west_other, arrival(corner_n, got.at[5, :, part], 5)),
    ]

    def each(entries, act):
        for cond, copy in entries:
            if cond is None:
                act(copy)
            else:
                pl.when(cond)(functools.partial(act, copy))

    pl.semaphore_wait(barrier, greetings)
    each(sends, lambda copy: copy.start())

    @pl.when(east_self)
    def _():
        got[4, :, 0:128] = north[:, WIDE : WIDE + 128]

    @pl.when(west_self)
    def _():
        got[5, :, 0:128] = north[:, WIDE + 128 :]

    each(arrivals, lambda copy: copy.wait_recv())

    def arrived(k):
        parts = [got[k, :, 128 * t : 128 * t + 128] for t in range(5)]
        w, e = got[k + 1, :, 0:128], got[k + 2, :, 0:128]
        return [
            parts[0] + jnp.where(low2, w, 0.0), parts[1], parts[2],
            parts[3] + jnp.where(low2, 0.0, e), parts[4] + jnp.where(low2, e, w),
        ]

    backwards = 127 - lane

    def turned(x):
        return stacked([jnp.take_along_axis(x[r : r + 8], backwards, axis=1) for r in (0, 8)])

    s_rows = joined(arrived(0))
    n_parts = arrived(3)
    flipped = [turned(x) for x in n_parts]
    flipped = flipped[3::-1] + flipped[4:]
    n_rows = joined([jnp.where(top, f, n) for f, n in zip(flipped, n_parts)])
    from_west, from_east = side[0], side[1]

    def with_sides(x, at):
        count = x.shape[0]
        w, e = from_west[at : at + count], from_east[at : at + count]
        near = iota((count, 128), 1) < 64
        return joined([
            x[:, 0:128] + jnp.where(near, w, 0.0),
            x[:, 128 : COLS - 128],
            x[:, COLS - 128 : COLS] + jnp.where(near, 0.0, e),
            x[:, COLS:] + jnp.where(near, e, w),
        ])

    def one(x, k):
        return x[k : k + 1]

    m = stacked([
        with_sides(ocean, 48),
        placed([(r, one(n_rows, 10 + r)) for r in range(3)] + [(7 - r, one(s_rows, 10 + r)) for r in range(3)]),
    ])
    s = stacked([with_sides(shift, 56), placed([(0, one(n_rows, 13)), (7, one(s_rows, 13))])])
    eastward, northward = [
        m * (
            with_sides(share[c], 16 * c)
            + stacked([
                placed([(0, one(s_rows, c)), (7, one(n_rows, c))]),
                placed([(r, one(n_rows, 2 + 2 * r + c)) for r in range(3)] + [(7 - r, one(s_rows, 2 + 2 * r + c)) for r in range(3)]),
            ])
        )
        for c in range(2)
    ]
    r = m * (eastward - lanes(eastward, 1) + northward - rows(northward, 1))
    beyond = m * (eastward - lanes(eastward, -1) + northward - rows(northward, -1))
    r = stacked([r[0:8], jnp.where(top & (row < 2), beyond[8:16], r[8:16])])

    def operate(v):
        return m * ((4.0 + s) * v - (lanes(v, 1) + lanes(v, -1) + rows(v, 1) + rows(v, -1)))

    q1 = operate(r)
    q2 = operate(q1)[0:8, 0:COLS]
    r, q1 = r[0:8, 0:COLS], q1[0:8, 0:COLS]

    def summed(x):
        x = x[:, 0:128] + x[:, 128:256] + x[:, 256:384] + x[:, 384:512]
        return jnp.sum(x, axis=0, keepdims=True)

    dots = [summed(r * r), summed(r * q1), summed(q1 * q1), summed(r * q2), summed(q1 * q2)]

    def spread(value, ref, stage, here, devices):
        ref[here] = value
        copies = [remote(ref.at[here], ref.at[here], send_sum.at[stage], recv_sum.at[stage], *at) for at in devices[1:]]
        for copy in copies:
            copy.start()

    def all_copies(ref, stage, count):
        several = ref.at[pl.ds(0, count - 1)]
        return remote(several, several, send_sum.at[stage], recv_sum.at[stage], east, lat)

    def collect(ref, stage, count):
        all_copies(ref, stage, count).wait_recv()
        return jnp.sum(ref[...], axis=0)

    dots = jnp.sum(stacked(dots + [jnp.zeros((3, 128), F32)]), axis=1, keepdims=True)
    dots = jnp.sum(jnp.where(lane == iota((ROWS, 128), 0), dots, 0.0), axis=0, keepdims=True)
    spread(dots, sums_a, 0, first_here, first_sum)

    ocean = ocean[:, 0:COLS]
    upper = with_sides(upper, 32)
    for c in range(2):
        one_level = upper[8 * c : 8 * c + 8] + placed([(0, one(s_rows, 8 + c)), (7, one(n_rows, 8 + c))])
        one_level = ocean * one_level[:, 0:COLS]
        whole = (eastward, northward)[c][0:8, 0:COLS]
        tend_ref[c, 0] = (whole - one_level).astype(BF16)
        tend_ref[c, 1] = one_level.astype(BF16)
    for k, value in enumerate((r, q1, q2)):
        fields_ref[8 * k : 8 * k + 8, :] = value
    each(sends, lambda copy: copy.wait_send())

    spread(collect(sums_a, 0, n_lat), sums_b, 1, second_here, second_sum)
    sums_ref[...] = collect(sums_b, 1, n_lon)
    all_copies(sums_a, 0, n_lat).wait_send()
    all_copies(sums_b, 1, n_lon).wait_send()


def finish(fields_ref, sums_ref, tend_in, tend_ref, surf_ref, res_ref):
    r, q1, q2 = fields_ref[0:8, :], fields_ref[8:16, :], fields_ref[16:24, :]
    rr, rq, qq, rq2, qq2 = [sums_ref[0:1, k : k + 1] for k in range(5)]
    a1 = rr / rq
    new = rr - 2.0 * a1 * rq + a1 * a1 * qq
    lead = 1.0 + new / rr
    a2 = new / (lead * lead * rq - lead * a1 * (rq2 + qq) + a1 * a1 * qq2)
    surf_ref[...] = a1 * r + a2 * (lead * r - a1 * q1)
    res_ref[...] = r - a1 * q1 - a2 * (lead * q1 - a1 * q2)
    tend_ref[...] = tend_in[...]


def body(features, spline_coef, edge_mask, head_weight, land_mask, shift_coef):
    n_lon, n_lat = lax.axis_size("lon"), lax.axis_size("lat")
    vmem = pl.BlockSpec(memory_space=pltpu.VMEM)
    dma = pltpu.SemaphoreType.DMA
    tend_shape = jax.ShapeDtypeStruct((2, L, ROWS, COLS), BF16)
    field_shape = jax.ShapeDtypeStruct((ROWS, COLS), F32)
    scratch = [
        pltpu.VMEM((C, L, ROWS, COLS), BF16),
        pltpu.VMEM((9 * C, C * J), BF16),
        pltpu.VMEM((C, C), jnp.int32),
        pltpu.VMEM((2, C), BF16),
        pltpu.VMEM((ROWS, COLS), jnp.int32),
        pltpu.VMEM((ROWS, COLS), F32),
        pltpu.VMEM((GROUPS, 64, 128 * J), BF16),
        pltpu.VMEM((128 * J, COLS), BF16),
        pltpu.VMEM((L, 64, WIDE), F32),
        pltpu.VMEM((16, WIDE + 256), F32),
        pltpu.VMEM((16, WIDE + 256), F32),
        pltpu.VMEM((64, 128), F32),
        pltpu.VMEM((64, 128), F32),
        pltpu.VMEM((6, 16, WIDE), F32),
        pltpu.VMEM((2, 64, 128), F32),
        pltpu.VMEM((n_lat, 1, 128), F32),
        pltpu.VMEM((n_lon, 1, 128), F32),
        dma((GROUPS,)), dma((5,)), dma((8,)), dma((8,)), dma((2,)), dma((2,)),
    ]
    tendency, fields, sums = pl.pallas_call(
        functools.partial(kernel, n_lon, n_lat),
        out_shape=(
            pltpu.VMEM((2, L, ROWS, COLS), BF16),
            pltpu.VMEM((3 * ROWS, COLS), F32),
            pltpu.VMEM((1, 128), F32),
        ),
        in_specs=[pl.BlockSpec(memory_space=pl.ANY)] * 6,
        out_specs=(vmem, vmem, vmem),
        scratch_shapes=scratch,
        compiler_params=pltpu.CompilerParams(collective_id=0, has_side_effects=True),
        name="closure_and_sums",
    )(features, spline_coef, edge_mask, head_weight, land_mask, shift_coef)
    return pl.pallas_call(
        finish,
        out_shape=(tend_shape, field_shape, field_shape),
        in_specs=[vmem] * 3,
        out_specs=(vmem, vmem, vmem),
        compiler_params=pltpu.CompilerParams(vmem_limit_bytes=4 * 1024 * 1024),
        name="finish",
    )(fields, sums, tendency)


def solution(mesh):
    in_specs = (P(None, None, "lat", "lon"), P(), P(), P(), P("lat", "lon"), P("lat", "lon"))
    out_specs = (P(None, None, "lat", "lon"), P("lat", "lon"), P("lat", "lon"))
    return jax.shard_map(body, mesh=mesh, in_specs=in_specs, out_specs=out_specs, check_vma=False)
```

```python
import functools
import math

import jax
import jax.numpy as jnp
from jax import lax
from jax.experimental import pallas as pl
from jax.experimental.pallas import tpu as pltpu
from jax.sharding import PartitionSpec as P

C = 48
NB = 9
J = NB + 1
L = 2
ROWS = 8
COLS = 512
WIDE = COLS + 128
F32 = jnp.float32
BF16 = jnp.bfloat16
MESH = pl.DeviceIdType.MESH
LOG2E = math.log2(math.e)
LIFT = 82
GROUP = 16
GROUPS = C // GROUP
CHUNK = GROUP * ROWS * J


def iota(shape, axis):
    return lax.broadcasted_iota(jnp.int32, shape, axis)


def dot(a, b):
    return jnp.dot(a, b, preferred_element_type=F32)


def ones_where(cond):
    return jnp.where(cond, 1.0, 0.0).astype(BF16)


def fold_weights(coef_ref, edge_ref, head_ref, wt, top):
    channel, lane = iota((C, C * J), 0), iota((C, C * J), 1)
    spread = ones_where((lane >= channel * J) & (lane < channel * J + J))
    keep = dot(jnp.where(edge_ref[...] > 0, 1.0, 0.0).astype(BF16), spread).astype(BF16)
    o, q = iota((C, 9 * C), 0), iota((C, 9 * C), 1)
    offset = lax.shift_right_logical(q * 1366, 16)
    head = dot(head_ref[...], ones_where(q - offset * C == o))
    r, q = iota((24, 9 * C), 0), iota((24, 9 * C), 1)
    offset = lax.shift_right_logical(q * 1366, 16)
    head = jnp.where((r & 1) == 0, head[0:1], head[1:2])
    head = jnp.where(lax.shift_right_logical(r, 1) == offset, head, 0.0).astype(BF16)
    masked = [coef_ref[C * k : C * k + C, :] * keep for k in range(9)]
    folded = dot(head, jnp.concatenate(masked, axis=0))
    lane = iota((1, C * J), 1)
    j = lane - J * lax.shift_right_logical(lane * 6554, 16)
    off = jnp.abs(j - NB // 2).astype(F32)
    scale = jnp.where(j == NB, 2.0**LIFT, jnp.exp(-off * off))
    folded = folded * scale
    q = iota((1, CHUNK), 1)
    strip = lax.shift_right_logical(q * 13108, 21)
    source = (2 * strip + (lax.shift_right_logical(q, 3) & 1)) * J + lax.shift_right_logical(q - strip * (2 * ROWS * J), 4)
    expand = ones_where(iota((GROUP * J, CHUNK), 0) == source)
    y_out = iota((ROWS, CHUNK), 0)
    y_in = iota((ROWS, CHUNK), 1) & 7
    first_row, last_row = y_in[0:6] == 0, y_in[0:6] == 7
    pad = jnp.zeros((2, CHUNK), F32)
    for group in range(GROUPS):
        g = dot(folded[:, GROUP * J * group : GROUP * J * (group + 1)].astype(BF16), expand)
        tiles = []
        for k in range(6):
            tile = jnp.where(y_in == y_out - 1, g[k : k + 1], 0.0)
            tile = jnp.where(y_in == y_out, g[6 + k : 7 + k], tile)
            tiles.append(jnp.where(y_in == y_out + 1, g[12 + k : 13 + k], tile))
        mirrored = jnp.concatenate([g[16:18], g[14:16], g[12:14]], axis=0)
        above = jnp.where(top, mirrored, g[0:6])
        tiles += [jnp.where(first_row, g[12:18], 0.0), pad, jnp.where(last_row, above, 0.0), pad]
        wt[group] = jnp.concatenate(tiles, axis=0).astype(BF16)


def basis(x):
    half = x * 0.5
    middle = jnp.exp2((half * half) * (-16.0 * LOG2E) + float(LIFT))
    up = jnp.exp2(half * (8.0 * LOG2E))
    down = jnp.exp2(half * (-8.0 * LOG2E))
    silu = half + half * jnp.tanh(half)
    left, right = [middle], [middle]
    for _ in range(NB // 2):
        left.append(left[-1] * down)
        right.append(right[-1] * up)
    return left[:0:-1] + right + [silu]


def bits(value, flips):
    return jnp.bitwise_xor(value, flips) if flips else value


def kernel(
    n_lon, n_lat,
    feat_hbm, coef_hbm, edge_hbm, head_hbm, land_hbm, shift_hbm,
    tend_ref, fields_ref, sums_ref,
    feat, coef_ref, edge_ref, head_ref, land_ref, shift_ref, wt, bases_a, bases_b, acc,
    north, south, to_east, to_west, got, side, sums_a, sums_b,
    feat_sem, weight_sem, send, recv, send_sum, recv_sum,
):
    lon, lat = lax.axis_index("lon"), lax.axis_index("lat")
    top, bottom = lat == n_lat - 1, lat == 0
    east = jnp.where(lon == n_lon - 1, 0, lon + 1)
    west = jnp.where(lon == 0, n_lon - 1, lon - 1)
    up_lat = jnp.where(top, lat, lat + 1)
    up_lon = jnp.where(top, n_lon - 1 - lon, lon)
    up_east = jnp.where(top, n_lon - 1 - east, east)
    up_west = jnp.where(top, n_lon - 1 - west, west)
    down_lat = jnp.where(bottom, lat, lat - 1)
    east_self, west_self = top & (up_east == lon), top & (up_west == lon)
    east_other, west_other = jnp.logical_not(east_self), jnp.logical_not(west_self)
    has_south = jnp.logical_not(bottom)

    weights_in = [
        pltpu.make_async_copy(src, dst, weight_sem.at[k])
        for k, (src, dst) in enumerate(
            [(edge_hbm, edge_ref), (head_hbm, head_ref), (coef_hbm, coef_ref), (land_hbm, land_ref), (shift_hbm, shift_ref)]
        )
    ]

    def feat_in(k):
        part = pl.ds(k * GROUP, GROUP)
        return pltpu.make_async_copy(feat_hbm.at[part], feat.at[part], feat_sem.at[k])

    for copy in weights_in + [feat_in(k) for k in range(GROUPS)]:
        copy.start()

    half = n_lon // 2
    ring = {0: 0, 1: 1, 2: 2, 3: 3, 4: 4, 5: 3, 6: 2, 7: 2}

    def far_first(count, hops):
        return sorted(range(1, count), key=lambda d: -hops(d))

    first_order = far_first(n_lat, lambda d: ring.get(d // 2, 0))
    first_sum = [(bits(lon, d % 2), bits(lat, d - d % 2)) for d in first_order]
    first_here = lat - lax.rem(lat, 2) + lax.rem(lon, 2)
    second_order = far_first(n_lon, lambda d: (0, 1, 2, 1)[d % 4] + (0, 2, 1, 1)[d // 4 % 4])
    second_sum = [(bits(lon, 2 * (d % half)), bits(lat, d // half)) for d in second_order]
    second_here = lon // 2 + half * lax.rem(lat, 2)

    barrier = pltpu.get_barrier_semaphore()

    def greet(at_lon, at_lat):
        pl.semaphore_signal(barrier, inc=1, device_id={"lon": at_lon, "lat": at_lat}, device_id_type=MESH)

    greet(east, lat)
    greet(west, lat)
    greet(up_lon, up_lat)
    pl.when(east_other)(lambda: greet(up_east, up_lat))
    pl.when(west_other)(lambda: greet(up_west, up_lat))

    @pl.when(has_south)
    def _():
        greet(lon, down_lat)
        greet(east, down_lat)
        greet(west, down_lat)

    for at in first_sum + second_sum:
        greet(*at)
    greetings = n_lon + n_lat + 6 - jnp.where(east_self, 1, 0) - jnp.where(west_self, 1, 0) - jnp.where(bottom, 3, 0)

    def remote(src, dst, send, recv, at_lon, at_lat):
        return pltpu.make_async_remote_copy(
            src_ref=src, dst_ref=dst, send_sem=send, recv_sem=recv,
            device_id={"lon": at_lon, "lat": at_lat}, device_id_type=MESH,
        )

    @pl.when(bottom)
    def _():
        got[0:3] = jnp.zeros((3, 16, WIDE), F32)

    for copy in weights_in:
        copy.wait()
    feat_in(0).wait()
    fold_weights(coef_ref, edge_ref, head_ref, wt, top)

    acc[...] = jnp.zeros(acc.shape, F32)

    def expanded(k, out):
        for at in range(0, GROUP, 2):
            x = feat[pl.ds((k // L) * GROUP + at, 2), lax.rem(k, L)].astype(F32).reshape(2 * ROWS, COLS)
            for j, value in enumerate(basis(x)):
                row = (at * J + 2 * j) * ROWS
                out[row : row + 2 * ROWS, :] = value.astype(BF16)

    def contracted(k, bases):
        acc[lax.rem(k, L), :, 0:COLS] += dot(wt[k // L], bases[...])

    expanded(0, bases_a)
    for k in range(1, GROUPS):
        feat_in(k).wait()

    def step(i, carry):
        expanded(2 * i + 1, bases_b)
        contracted(2 * i, bases_a)
        expanded(jnp.minimum(2 * i + 2, L * GROUPS - 1), bases_a)
        contracted(2 * i + 1, bases_b)
        return carry

    lax.fori_loop(0, GROUPS * L // 2, step, 0)

    @pl.when(bottom)
    def _():
        q = iota((1, CHUNK), 1)
        j = lax.shift_right_logical(q - lax.shift_right_logical(q * 13108, 21) * (2 * ROWS * J), 4)
        outside = jnp.zeros((8, CHUNK), F32)
        for group in range(GROUPS):
            outside = outside + wt[group, 48:64, :].astype(F32)[8:16]
        outside = jnp.sum(jnp.where(j < NB, outside, 0.0), axis=1, keepdims=True) * (2.0**LIFT)
        for level in range(L):
            for c in range(2):
                acc[level, 16 + 8 * c : 17 + 8 * c, 0:COLS] += outside[c : c + 1] + outside[c + 2 : c + 3] + outside[c + 4 : c + 5]

    lane, low = iota((ROWS, 128), 1), iota((ROWS, 128), 1) < 64
    low2 = iota((16, 128), 1) < 64
    row = iota((ROWS, WIDE), 0)
    zero = jnp.zeros((ROWS, WIDE), F32)

    def joined(parts):
        return jnp.concatenate(parts, axis=1)

    def stacked(parts):
        return jnp.concatenate(parts, axis=0)

    def lanes(x, by):
        return pltpu.roll(x, by % WIDE, 1)

    def rows(x, by):
        return pltpu.roll(x, by % 16, 0)

    def placed(entries):
        out = zero
        for at, value in entries:
            out = jnp.where(row == at, value, out)
        return out

    own, above, below = [], [], []
    for level in range(L):
        a = acc[level] * (2.0**-LIFT)
        own.append(a[16:32] + lanes(a[0:16], 1) + lanes(a[32:48], -1))
        outer = a[48:64]
        before, after = lanes(outer, 1), lanes(outer, -1)
        below.append(outer[2:4] + before[0:2] + after[4:6])
        above.append(outer[10:12] + before[8:10] + after[12:14])
    total, total_up, total_down = own[0] + own[1], above[0] + above[1], below[0] + below[1]
    share = [stacked([total[8 * c : 8 * c + 8], placed([(0, total_up[c : c + 1]), (7, total_down[c : c + 1])])]) for c in range(2)]
    upper = own[1]

    ocean = joined([land_ref[...].astype(F32), zero[:, 0:128]])
    shift = joined([shift_ref[...], zero[:, 0:128]])

    def both(r):
        return [total[r : r + 1], total[8 + r : 9 + r]]

    none = [zero[0:1]]
    edge_n = stacked(
        [total_up] + both(7) + both(6) + both(5) + [above[1], ocean[7:8], ocean[6:7], ocean[5:6], shift[7:8]] + none * 2
    )
    edge_s = stacked(
        [total_down] + both(0) + both(1) + none * 2 + [below[1], ocean[0:1], ocean[1:2]] + none + [shift[0:1]] + none * 2
    )
    edge_e = stacked(share + [upper, ocean, shift])

    def eastern(x):
        return jnp.where(iota((x.shape[0], 128), 1) < 64, x[:, COLS:], x[:, COLS - 128 : COLS])

    def western(x):
        return jnp.where(iota((x.shape[0], 128), 1) < 64, x[:, 0:128], x[:, COLS:])

    corner = pl.ds(WIDE, 128), pl.ds(WIDE + 128, 128)
    for edge, ref in ((edge_n, north), (edge_s, south)):
        ref[:, 0:WIDE] = edge
        ref[:, WIDE : WIDE + 128] = eastern(edge)
        ref[:, WIDE + 128 :] = western(edge)
    to_east[...] = eastern(edge_e)
    to_west[...] = western(edge_e)

    whole, part = pl.ds(0, WIDE), pl.ds(0, 128)
    upward = jnp.where(top, 3, 0)
    sends = [
        (east_other, remote(north.at[:, corner[0]], got.at[upward + 1, :, part], send.at[1], recv.at[upward + 1], up_east, up_lat)),
        (west_other, remote(north.at[:, corner[1]], got.at[upward + 2, :, part], send.at[2], recv.at[upward + 2], up_west, up_lat)),
        (has_south, remote(south.at[:, corner[0]], got.at[4, :, part], send.at[4], recv.at[4], east, down_lat)),
        (has_south, remote(south.at[:, corner[1]], got.at[5, :, part], send.at[5], recv.at[5], west, down_lat)),
        (None, remote(north.at[:, whole], got.at[upward], send.at[0], recv.at[upward], up_lon, up_lat)),
        (has_south, remote(south.at[:, whole], got.at[3], send.at[3], recv.at[3], lon, down_lat)),
        (None, remote(to_east, side.at[0], send.at[6], recv.at[6], east, lat)),
        (None, remote(to_west, side.at[1], send.at[7], recv.at[7], west, lat)),
    ]

    def arrival(src, dst, k):
        return remote(src, dst, send.at[0], recv.at[k], east, lat)

    corner_n = north.at[:, corner[0]]
    arrivals = [
        (None, arrival(to_east, side.at[0], 6)),
        (None, arrival(to_west, side.at[1], 7)),
        (has_south, arrival(north.at[:, whole], got.at[0], 0)),
        (has_south, arrival(corner_n, got.at[1, :, part], 1)),
        (has_south, arrival(corner_n, got.at[2, :, part], 2)),
        (None, arrival(north.at[:, whole], got.at[3], 3)),
        (east_other, arrival(corner_n, got.at[4, :, part], 4)),
        (west_other, arrival(corner_n, got.at[5, :, part], 5)),
    ]

    def each(entries, act):
        for cond, copy in entries:
            if cond is None:
                act(copy)
            else:
                pl.when(cond)(functools.partial(act, copy))

    pl.semaphore_wait(barrier, greetings)
    each(sends, lambda copy: copy.start())

    @pl.when(east_self)
    def _():
        got[4, :, 0:128] = north[:, WIDE : WIDE + 128]

    @pl.when(west_self)
    def _():
        got[5, :, 0:128] = north[:, WIDE + 128 :]

    each(arrivals, lambda copy: copy.wait_recv())

    def arrived(k):
        parts = [got[k, :, 128 * t : 128 * t + 128] for t in range(5)]
        w, e = got[k + 1, :, 0:128], got[k + 2, :, 0:128]
        return [
            parts[0] + jnp.where(low2, w, 0.0), parts[1], parts[2],
            parts[3] + jnp.where(low2, 0.0, e), parts[4] + jnp.where(low2, e, w),
        ]

    backwards = 127 - lane

    def turned(x):
        return stacked([jnp.take_along_axis(x[r : r + 8], backwards, axis=1) for r in (0, 8)])

    s_rows = joined(arrived(0))
    n_parts = arrived(3)
    flipped = [turned(x) for x in n_parts]
    flipped = flipped[3::-1] + flipped[4:]
    n_rows = joined([jnp.where(top, f, n) for f, n in zip(flipped, n_parts)])
    from_west, from_east = side[0], side[1]

    def with_sides(x, at):
        count = x.shape[0]
        w, e = from_west[at : at + count], from_east[at : at + count]
        near = iota((count, 128), 1) < 64
        return joined([
            x[:, 0:128] + jnp.where(near, w, 0.0),
            x[:, 128 : COLS - 128],
            x[:, COLS - 128 : COLS] + jnp.where(near, 0.0, e),
            x[:, COLS:] + jnp.where(near, e, w),
        ])

    def one(x, k):
        return x[k : k + 1]

    m = stacked([
        with_sides(ocean, 48),
        placed([(r, one(n_rows, 10 + r)) for r in range(3)] + [(7 - r, one(s_rows, 10 + r)) for r in range(3)]),
    ])
    s = stacked([with_sides(shift, 56), placed([(0, one(n_rows, 13)), (7, one(s_rows, 13))])])
    eastward, northward = [
        m * (
            with_sides(share[c], 16 * c)
            + stacked([
                placed([(0, one(s_rows, c)), (7, one(n_rows, c))]),
                placed([(r, one(n_rows, 2 + 2 * r + c)) for r in range(3)] + [(7 - r, one(s_rows, 2 + 2 * r + c)) for r in range(3)]),
            ])
        )
        for c in range(2)
    ]
    r = m * (eastward - lanes(eastward, 1) + northward - rows(northward, 1))
    beyond = m * (eastward - lanes(eastward, -1) + northward - rows(northward, -1))
    r = stacked([r[0:8], jnp.where(top & (row < 2), beyond[8:16], r[8:16])])

    def operate(v):
        return m * ((4.0 + s) * v - (lanes(v, 1) + lanes(v, -1) + rows(v, 1) + rows(v, -1)))

    q1 = operate(r)
    q2 = operate(q1)[0:8, 0:COLS]
    r, q1 = r[0:8, 0:COLS], q1[0:8, 0:COLS]

    def summed(x):
        x = x[:, 0:128] + x[:, 128:256] + x[:, 256:384] + x[:, 384:512]
        return jnp.sum(x, axis=0, keepdims=True)

    dots = [summed(r * r), summed(r * q1), summed(q1 * q1), summed(r * q2), summed(q1 * q2)]

    def spread(value, ref, stage, here, devices):
        ref[here] = value
        copies = [remote(ref.at[here], ref.at[here], send_sum.at[stage], recv_sum.at[stage], *at) for at in devices]
        for copy in copies:
            copy.start()

    def all_copies(ref, stage, count):
        several = ref.at[pl.ds(0, count - 1)]
        return remote(several, several, send_sum.at[stage], recv_sum.at[stage], east, lat)

    def collect(ref, stage, count):
        all_copies(ref, stage, count).wait_recv()
        return jnp.sum(ref[...], axis=0)

    dots = jnp.sum(stacked(dots + [jnp.zeros((3, 128), F32)]), axis=1, keepdims=True)
    dots = jnp.sum(jnp.where(lane == iota((ROWS, 128), 0), dots, 0.0), axis=0, keepdims=True)
    spread(dots, sums_a, 0, first_here, first_sum)

    ocean = ocean[:, 0:COLS]
    upper = with_sides(upper, 32)
    for c in range(2):
        one_level = upper[8 * c : 8 * c + 8] + placed([(0, one(s_rows, 8 + c)), (7, one(n_rows, 8 + c))])
        one_level = ocean * one_level[:, 0:COLS]
        whole = (eastward, northward)[c][0:8, 0:COLS]
        tend_ref[c, 0] = (whole - one_level).astype(BF16)
        tend_ref[c, 1] = one_level.astype(BF16)
    for k, value in enumerate((r, q1, q2)):
        fields_ref[8 * k : 8 * k + 8, :] = value
    each(sends, lambda copy: copy.wait_send())

    spread(collect(sums_a, 0, n_lat), sums_b, 1, second_here, second_sum)
    sums_ref[...] = collect(sums_b, 1, n_lon)
    all_copies(sums_a, 0, n_lat).wait_send()
    all_copies(sums_b, 1, n_lon).wait_send()


def finish(fields_ref, sums_ref, tend_in, tend_ref, surf_ref, res_ref):
    r, q1, q2 = fields_ref[0:8, :], fields_ref[8:16, :], fields_ref[16:24, :]
    rr, rq, qq, rq2, qq2 = [sums_ref[0:1, k : k + 1] for k in range(5)]
    a1 = rr / rq
    new = rr - 2.0 * a1 * rq + a1 * a1 * qq
    lead = 1.0 + new / rr
    a2 = new / (lead * lead * rq - lead * a1 * (rq2 + qq) + a1 * a1 * qq2)
    surf_ref[...] = a1 * r + a2 * (lead * r - a1 * q1)
    res_ref[...] = r - a1 * q1 - a2 * (lead * q1 - a1 * q2)
    tend_ref[...] = tend_in[...]


def body(features, spline_coef, edge_mask, head_weight, land_mask, shift_coef):
    n_lon, n_lat = lax.axis_size("lon"), lax.axis_size("lat")
    vmem = pl.BlockSpec(memory_space=pltpu.VMEM)
    dma = pltpu.SemaphoreType.DMA
    tend_shape = jax.ShapeDtypeStruct((2, L, ROWS, COLS), BF16)
    field_shape = jax.ShapeDtypeStruct((ROWS, COLS), F32)
    scratch = [
        pltpu.VMEM((C, L, ROWS, COLS), BF16),
        pltpu.VMEM((9 * C, C * J), BF16),
        pltpu.VMEM((C, C), jnp.int32),
        pltpu.VMEM((2, C), BF16),
        pltpu.VMEM((ROWS, COLS), jnp.int32),
        pltpu.VMEM((ROWS, COLS), F32),
        pltpu.VMEM((GROUPS, 64, CHUNK), BF16),
        pltpu.VMEM((CHUNK, COLS), BF16),
        pltpu.VMEM((CHUNK, COLS), BF16),
        pltpu.VMEM((L, 64, WIDE), F32),
        pltpu.VMEM((16, WIDE + 256), F32),
        pltpu.VMEM((16, WIDE + 256), F32),
        pltpu.VMEM((64, 128), F32),
        pltpu.VMEM((64, 128), F32),
        pltpu.VMEM((6, 16, WIDE), F32),
        pltpu.VMEM((2, 64, 128), F32),
        pltpu.VMEM((n_lat, 1, 128), F32),
        pltpu.VMEM((n_lon, 1, 128), F32),
        dma((GROUPS,)), dma((5,)), dma((8,)), dma((8,)), dma((2,)), dma((2,)),
    ]
    tendency, fields, sums = pl.pallas_call(
        functools.partial(kernel, n_lon, n_lat),
        out_shape=(
            pltpu.VMEM((2, L, ROWS, COLS), BF16),
            pltpu.VMEM((3 * ROWS, COLS), F32),
            pltpu.VMEM((1, 128), F32),
        ),
        in_specs=[pl.BlockSpec(memory_space=pl.ANY)] * 6,
        out_specs=(vmem, vmem, vmem),
        scratch_shapes=scratch,
        compiler_params=pltpu.CompilerParams(collective_id=0, has_side_effects=True),
        name="closure_and_sums",
    )(features, spline_coef, edge_mask, head_weight, land_mask, shift_coef)
    return pl.pallas_call(
        finish,
        out_shape=(tend_shape, field_shape, field_shape),
        in_specs=[vmem] * 3,
        out_specs=(vmem, vmem, vmem),
        compiler_params=pltpu.CompilerParams(vmem_limit_bytes=4 * 1024 * 1024),
        name="finish",
    )(fields, sums, tendency)


def solution(mesh):
    in_specs = (P(None, None, "lat", "lon"), P(), P(), P(), P("lat", "lon"), P("lat", "lon"))
    out_specs = (P(None, None, "lat", "lon"), P("lat", "lon"), P("lat", "lon"))
    return jax.shard_map(body, mesh=mesh, in_specs=in_specs, out_specs=out_specs, check_vma=False)
```

```python
import functools
import math

import jax
import jax.numpy as jnp
from jax import lax
from jax.experimental import pallas as pl
from jax.experimental.pallas import tpu as pltpu
from jax.sharding import PartitionSpec as P

C = 48
NB = 9
J = NB + 1
L = 2
ROWS = 8
COLS = 512
WIDE = COLS + 128
F32 = jnp.float32
BF16 = jnp.bfloat16
MESH = pl.DeviceIdType.MESH
LOG2E = math.log2(math.e)
LIFT = 82
GROUP = 16
GROUPS = C // GROUP
CHUNK = GROUP * ROWS * J


def iota(shape, axis):
    return lax.broadcasted_iota(jnp.int32, shape, axis)


def dot(a, b):
    return jnp.dot(a, b, preferred_element_type=F32)


def ones_where(cond):
    return jnp.where(cond, 1.0, 0.0).astype(BF16)


def fold_weights(coef_ref, edge_ref, head_ref, wt, top):
    channel, lane = iota((C, C * J), 0), iota((C, C * J), 1)
    spread = ones_where((lane >= channel * J) & (lane < channel * J + J))
    keep = dot(jnp.where(edge_ref[...] > 0, 1.0, 0.0).astype(BF16), spread).astype(BF16)
    o, q = iota((C, 9 * C), 0), iota((C, 9 * C), 1)
    offset = lax.shift_right_logical(q * 1366, 16)
    head = dot(head_ref[...], ones_where(q - offset * C == o))
    r, q = iota((24, 9 * C), 0), iota((24, 9 * C), 1)
    offset = lax.shift_right_logical(q * 1366, 16)
    head = jnp.where((r & 1) == 0, head[0:1], head[1:2])
    head = jnp.where(lax.shift_right_logical(r, 1) == offset, head, 0.0).astype(BF16)
    masked = [coef_ref[C * k : C * k + C, :] * keep for k in range(9)]
    folded = dot(head, jnp.concatenate(masked, axis=0))
    lane = iota((1, C * J), 1)
    j = lane - J * lax.shift_right_logical(lane * 6554, 16)
    off = jnp.abs(j - NB // 2).astype(F32)
    scale = jnp.where(j == NB, 2.0**LIFT, jnp.exp(-off * off))
    folded = folded * scale
    q = iota((1, CHUNK), 1)
    strip = lax.shift_right_logical(q * 13108, 21)
    source = (2 * strip + (lax.shift_right_logical(q, 3) & 1)) * J + lax.shift_right_logical(q - strip * (2 * ROWS * J), 4)
    expand = ones_where(iota((GROUP * J, CHUNK), 0) == source)
    y_out = iota((ROWS, CHUNK), 0)
    y_in = iota((ROWS, CHUNK), 1) & 7
    first_row, last_row = y_in[0:6] == 0, y_in[0:6] == 7
    pad = jnp.zeros((2, CHUNK), F32)
    for group in range(GROUPS):
        g = dot(folded[:, GROUP * J * group : GROUP * J * (group + 1)].astype(BF16), expand)
        tiles = []
        for k in range(6):
            tile = jnp.where(y_in == y_out - 1, g[k : k + 1], 0.0)
            tile = jnp.where(y_in == y_out, g[6 + k : 7 + k], tile)
            tiles.append(jnp.where(y_in == y_out + 1, g[12 + k : 13 + k], tile))
        mirrored = jnp.concatenate([g[16:18], g[14:16], g[12:14]], axis=0)
        above = jnp.where(top, mirrored, g[0:6])
        tiles += [jnp.where(first_row, g[12:18], 0.0), pad, jnp.where(last_row, above, 0.0), pad]
        wt[group] = jnp.concatenate(tiles, axis=0).astype(BF16)


def basis(x):
    half = x * 0.5
    middle = jnp.exp2((half * half) * (-16.0 * LOG2E) + float(LIFT))
    up = jnp.exp2(half * (8.0 * LOG2E))
    down = jnp.exp2(half * (-8.0 * LOG2E))
    silu = half + half * jnp.tanh(half)
    left, right = [middle], [middle]
    for _ in range(NB // 2):
        left.append(left[-1] * down)
        right.append(right[-1] * up)
    return left[:0:-1] + right + [silu]


def bits(value, flips):
    return jnp.bitwise_xor(value, flips) if flips else value


def kernel(
    n_lon, n_lat,
    feat_hbm, coef_hbm, edge_hbm, head_hbm, land_hbm, shift_hbm,
    tend_ref, fields_ref, sums_ref,
    feat, coef_ref, edge_ref, head_ref, land_ref, shift_ref, wt, bases_a, bases_b, acc,
    north, south, to_east, to_west, got, side, sums_a, sums_b,
    feat_sem, weight_sem, send, recv, send_sum, recv_sum,
):
    lon, lat = lax.axis_index("lon"), lax.axis_index("lat")
    top, bottom = lat == n_lat - 1, lat == 0
    east = jnp.where(lon == n_lon - 1, 0, lon + 1)
    west = jnp.where(lon == 0, n_lon - 1, lon - 1)
    up_lat = jnp.where(top, lat, lat + 1)
    up_lon = jnp.where(top, n_lon - 1 - lon, lon)
    up_east = jnp.where(top, n_lon - 1 - east, east)
    up_west = jnp.where(top, n_lon - 1 - west, west)
    down_lat = jnp.where(bottom, lat, lat - 1)
    east_self, west_self = top & (up_east == lon), top & (up_west == lon)
    east_other, west_other = jnp.logical_not(east_self), jnp.logical_not(west_self)
    has_south = jnp.logical_not(bottom)

    weights_in = [
        pltpu.make_async_copy(src, dst, weight_sem.at[k])
        for k, (src, dst) in enumerate(
            [(edge_hbm, edge_ref), (head_hbm, head_ref), (coef_hbm, coef_ref), (land_hbm, land_ref), (shift_hbm, shift_ref)]
        )
    ]

    def feat_in(k):
        part = pl.ds(k * GROUP, GROUP)
        return pltpu.make_async_copy(feat_hbm.at[part], feat.at[part], feat_sem.at[k])

    for copy in weights_in + [feat_in(k) for k in range(GROUPS)]:
        copy.start()

    half = n_lon // 2
    ring = {0: 0, 1: 1, 2: 2, 3: 3, 4: 4, 5: 3, 6: 2, 7: 2}

    def far_first(count, hops):
        return sorted(range(1, count), key=lambda d: -hops(d))

    first_order = far_first(n_lat, lambda d: ring.get(d // 2, 0))
    first_sum = [(bits(lon, d % 2), bits(lat, d - d % 2)) for d in first_order]
    first_here = lat - lax.rem(lat, 2) + lax.rem(lon, 2)
    second_order = far_first(n_lon, lambda d: (0, 1, 2, 1)[d % 4] + (0, 2, 1, 1)[d // 4 % 4])
    second_sum = [(bits(lon, 2 * (d % half)), bits(lat, d // half)) for d in second_order]
    second_here = lon // 2 + half * lax.rem(lat, 2)

    barrier = pltpu.get_barrier_semaphore()

    def greet(at_lon, at_lat):
        pl.semaphore_signal(barrier, inc=1, device_id={"lon": at_lon, "lat": at_lat}, device_id_type=MESH)

    greet(east, lat)
    greet(west, lat)
    greet(up_lon, up_lat)
    pl.when(east_other)(lambda: greet(up_east, up_lat))
    pl.when(west_other)(lambda: greet(up_west, up_lat))

    @pl.when(has_south)
    def _():
        greet(lon, down_lat)
        greet(east, down_lat)
        greet(west, down_lat)

    for at in first_sum + second_sum:
        greet(*at)
    greetings = n_lon + n_lat + 6 - jnp.where(east_self, 1, 0) - jnp.where(west_self, 1, 0) - jnp.where(bottom, 3, 0)

    def remote(src, dst, send, recv, at_lon, at_lat):
        return pltpu.make_async_remote_copy(
            src_ref=src, dst_ref=dst, send_sem=send, recv_sem=recv,
            device_id={"lon": at_lon, "lat": at_lat}, device_id_type=MESH,
        )

    @pl.when(bottom)
    def _():
        got[0:3] = jnp.zeros((3, 16, WIDE), BF16)

    for copy in weights_in:
        copy.wait()
    feat_in(0).wait()
    fold_weights(coef_ref, edge_ref, head_ref, wt, top)

    acc[...] = jnp.zeros(acc.shape, F32)

    def expanded(k, out):
        for at in range(0, GROUP, 2):
            x = feat[pl.ds((k // L) * GROUP + at, 2), lax.rem(k, L)].astype(F32).reshape(2 * ROWS, COLS)
            for j, value in enumerate(basis(x)):
                row = (at * J + 2 * j) * ROWS
                out[row : row + 2 * ROWS, :] = value.astype(BF16)

    def contracted(k, bases):
        acc[lax.rem(k, L), :, 0:COLS] += dot(wt[k // L], bases[...])

    expanded(0, bases_a)
    for k in range(1, GROUPS):
        feat_in(k).wait()

    def step(i, carry):
        expanded(2 * i + 1, bases_b)
        contracted(2 * i, bases_a)
        expanded(jnp.minimum(2 * i + 2, L * GROUPS - 1), bases_a)
        contracted(2 * i + 1, bases_b)
        return carry

    lax.fori_loop(0, GROUPS * L // 2, step, 0)

    @pl.when(bottom)
    def _():
        q = iota((1, CHUNK), 1)
        j = lax.shift_right_logical(q - lax.shift_right_logical(q * 13108, 21) * (2 * ROWS * J), 4)
        outside = jnp.zeros((8, CHUNK), F32)
        for group in range(GROUPS):
            outside = outside + wt[group, 48:64, :].astype(F32)[8:16]
        outside = jnp.sum(jnp.where(j < NB, outside, 0.0), axis=1, keepdims=True) * (2.0**LIFT)
        for level in range(L):
            for c in range(2):
                acc[level, 16 + 8 * c : 17 + 8 * c, 0:COLS] += outside[c : c + 1] + outside[c + 2 : c + 3] + outside[c + 4 : c + 5]

    lane, low = iota((ROWS, 128), 1), iota((ROWS, 128), 1) < 64
    low2 = iota((16, 128), 1) < 64
    row = iota((ROWS, WIDE), 0)
    zero = jnp.zeros((ROWS, WIDE), F32)

    def joined(parts):
        return jnp.concatenate(parts, axis=1)

    def stacked(parts):
        return jnp.concatenate(parts, axis=0)

    def lanes(x, by):
        return pltpu.roll(x, by % WIDE, 1)

    def rows(x, by):
        return pltpu.roll(x, by % 16, 0)

    def placed(entries):
        out = zero
        for at, value in entries:
            out = jnp.where(row == at, value, out)
        return out

    own, above, below = [], [], []
    for level in range(L):
        a = acc[level] * (2.0**-LIFT)
        own.append(a[16:32] + lanes(a[0:16], 1) + lanes(a[32:48], -1))
        outer = a[48:64]
        before, after = lanes(outer, 1), lanes(outer, -1)
        below.append(outer[2:4] + before[0:2] + after[4:6])
        above.append(outer[10:12] + before[8:10] + after[12:14])
    total, total_up, total_down = own[0] + own[1], above[0] + above[1], below[0] + below[1]
    share = [stacked([total[8 * c : 8 * c + 8], placed([(0, total_up[c : c + 1]), (7, total_down[c : c + 1])])]) for c in range(2)]
    upper = own[1]

    ocean = joined([land_ref[...].astype(F32), zero[:, 0:128]])
    shift = joined([shift_ref[...], zero[:, 0:128]])

    def both(r):
        return [total[r : r + 1], total[8 + r : 9 + r]]

    none = [zero[0:1]]
    edge_n = stacked(
        [total_up] + both(7) + both(6) + both(5) + [above[1], ocean[7:8], ocean[6:7], ocean[5:6], shift[7:8]] + none * 2
    )
    edge_s = stacked(
        [total_down] + both(0) + both(1) + none * 2 + [below[1], ocean[0:1], ocean[1:2]] + none + [shift[0:1]] + none * 2
    )
    edge_e = stacked(share + [upper, ocean, shift])

    def eastern(x):
        return jnp.where(iota((x.shape[0], 128), 1) < 64, x[:, COLS:], x[:, COLS - 128 : COLS])

    def western(x):
        return jnp.where(iota((x.shape[0], 128), 1) < 64, x[:, 0:128], x[:, COLS:])

    corner = pl.ds(WIDE, 128), pl.ds(WIDE + 128, 128)
    for edge, ref in ((edge_n, north), (edge_s, south)):
        ref[...] = joined([edge, eastern(edge), western(edge)]).astype(BF16)
    to_east[...] = eastern(edge_e).astype(BF16)
    to_west[...] = western(edge_e).astype(BF16)

    whole, part = pl.ds(0, WIDE), pl.ds(0, 128)
    upward = jnp.where(top, 3, 0)
    sends = [
        (east_other, remote(north.at[:, corner[0]], got.at[upward + 1, :, part], send.at[1], recv.at[upward + 1], up_east, up_lat)),
        (west_other, remote(north.at[:, corner[1]], got.at[upward + 2, :, part], send.at[2], recv.at[upward + 2], up_west, up_lat)),
        (has_south, remote(south.at[:, corner[0]], got.at[4, :, part], send.at[4], recv.at[4], east, down_lat)),
        (has_south, remote(south.at[:, corner[1]], got.at[5, :, part], send.at[5], recv.at[5], west, down_lat)),
        (None, remote(north.at[:, whole], got.at[upward], send.at[0], recv.at[upward], up_lon, up_lat)),
        (has_south, remote(south.at[:, whole], got.at[3], send.at[3], recv.at[3], lon, down_lat)),
        (None, remote(to_east, side.at[0], send.at[6], recv.at[6], east, lat)),
        (None, remote(to_west, side.at[1], send.at[7], recv.at[7], west, lat)),
    ]

    def arrival(src, dst, k):
        return remote(src, dst, send.at[0], recv.at[k], east, lat)

    corner_n = north.at[:, corner[0]]
    arrivals = [
        (None, arrival(to_east, side.at[0], 6)),
        (None, arrival(to_west, side.at[1], 7)),
        (has_south, arrival(north.at[:, whole], got.at[0], 0)),
        (has_south, arrival(corner_n, got.at[1, :, part], 1)),
        (has_south, arrival(corner_n, got.at[2, :, part], 2)),
        (None, arrival(north.at[:, whole], got.at[3], 3)),
        (east_other, arrival(corner_n, got.at[4, :, part], 4)),
        (west_other, arrival(corner_n, got.at[5, :, part], 5)),
    ]

    def each(entries, act):
        for cond, copy in entries:
            if cond is None:
                act(copy)
            else:
                pl.when(cond)(functools.partial(act, copy))

    pl.semaphore_wait(barrier, greetings)
    each(sends, lambda copy: copy.start())

    @pl.when(east_self)
    def _():
        got[4, :, 0:128] = north[:, WIDE : WIDE + 128]

    @pl.when(west_self)
    def _():
        got[5, :, 0:128] = north[:, WIDE + 128 :]

    each(arrivals, lambda copy: copy.wait_recv())

    def arrived(k):
        parts = [got[k, :, 128 * t : 128 * t + 128].astype(F32) for t in range(5)]
        w, e = got[k + 1, :, 0:128].astype(F32), got[k + 2, :, 0:128].astype(F32)
        return [
            parts[0] + jnp.where(low2, w, 0.0), parts[1], parts[2],
            parts[3] + jnp.where(low2, 0.0, e), parts[4] + jnp.where(low2, e, w),
        ]

    backwards = 127 - lane

    def turned(x):
        return stacked([jnp.take_along_axis(x[r : r + 8], backwards, axis=1) for r in (0, 8)])

    s_rows = joined(arrived(0))
    n_parts = arrived(3)
    flipped = [turned(x) for x in n_parts]
    flipped = flipped[3::-1] + flipped[4:]
    n_rows = joined([jnp.where(top, f, n) for f, n in zip(flipped, n_parts)])
    from_west, from_east = side[0].astype(F32), side[1].astype(F32)

    def with_sides(x, at):
        count = x.shape[0]
        w, e = from_west[at : at + count], from_east[at : at + count]
        near = iota((count, 128), 1) < 64
        return joined([
            x[:, 0:128] + jnp.where(near, w, 0.0),
            x[:, 128 : COLS - 128],
            x[:, COLS - 128 : COLS] + jnp.where(near, 0.0, e),
            x[:, COLS:] + jnp.where(near, e, w),
        ])

    def one(x, k):
        return x[k : k + 1]

    m = stacked([
        with_sides(ocean, 48),
        placed([(r, one(n_rows, 10 + r)) for r in range(3)] + [(7 - r, one(s_rows, 10 + r)) for r in range(3)]),
    ])
    s = stacked([with_sides(shift, 56), placed([(0, one(n_rows, 13)), (7, one(s_rows, 13))])])
    eastward, northward = [
        m * (
            with_sides(share[c], 16 * c)
            + stacked([
                placed([(0, one(s_rows, c)), (7, one(n_rows, c))]),
                placed([(r, one(n_rows, 2 + 2 * r + c)) for r in range(3)] + [(7 - r, one(s_rows, 2 + 2 * r + c)) for r in range(3)]),
            ])
        )
        for c in range(2)
    ]
    r = m * (eastward - lanes(eastward, 1) + northward - rows(northward, 1))
    beyond = m * (eastward - lanes(eastward, -1) + northward - rows(northward, -1))
    r = stacked([r[0:8], jnp.where(top & (row < 2), beyond[8:16], r[8:16])])

    def operate(v):
        return m * ((4.0 + s) * v - (lanes(v, 1) + lanes(v, -1) + rows(v, 1) + rows(v, -1)))

    q1 = operate(r)
    q2 = operate(q1)[0:8, 0:COLS]
    r, q1 = r[0:8, 0:COLS], q1[0:8, 0:COLS]

    def summed(x):
        x = x[:, 0:128] + x[:, 128:256] + x[:, 256:384] + x[:, 384:512]
        return jnp.sum(x, axis=0, keepdims=True)

    dots = [summed(r * r), summed(r * q1), summed(q1 * q1), summed(r * q2), summed(q1 * q2)]

    def spread(value, ref, stage, here, devices):
        ref[here] = value
        copies = [remote(ref.at[here], ref.at[here], send_sum.at[stage], recv_sum.at[stage], *at) for at in devices]
        for copy in copies:
            copy.start()

    def all_copies(ref, stage, count):
        several = ref.at[pl.ds(0, count - 1)]
        return remote(several, several, send_sum.at[stage], recv_sum.at[stage], east, lat)

    def collect(ref, stage, count):
        all_copies(ref, stage, count).wait_recv()
        return jnp.sum(ref[...], axis=0)

    dots = jnp.sum(stacked(dots + [jnp.zeros((3, 128), F32)]), axis=1, keepdims=True)
    dots = jnp.sum(jnp.where(lane == iota((ROWS, 128), 0), dots, 0.0), axis=0, keepdims=True)
    spread(dots, sums_a, 0, first_here, first_sum)

    ocean = ocean[:, 0:COLS]
    upper = with_sides(upper, 32)
    for c in range(2):
        one_level = upper[8 * c : 8 * c + 8] + placed([(0, one(s_rows, 8 + c)), (7, one(n_rows, 8 + c))])
        one_level = ocean * one_level[:, 0:COLS]
        whole = (eastward, northward)[c][0:8, 0:COLS]
        tend_ref[c, 0] = (whole - one_level).astype(BF16)
        tend_ref[c, 1] = one_level.astype(BF16)
    for k, value in enumerate((r, q1, q2)):
        fields_ref[8 * k : 8 * k + 8, :] = value
    each(sends, lambda copy: copy.wait_send())

    spread(collect(sums_a, 0, n_lat), sums_b, 1, second_here, second_sum)
    sums_ref[...] = collect(sums_b, 1, n_lon)
    all_copies(sums_a, 0, n_lat).wait_send()
    all_copies(sums_b, 1, n_lon).wait_send()


def finish(fields_ref, sums_ref, tend_in, tend_ref, surf_ref, res_ref):
    r, q1, q2 = fields_ref[0:8, :], fields_ref[8:16, :], fields_ref[16:24, :]
    rr, rq, qq, rq2, qq2 = [sums_ref[0:1, k : k + 1] for k in range(5)]
    a1 = rr / rq
    new = rr - 2.0 * a1 * rq + a1 * a1 * qq
    lead = 1.0 + new / rr
    a2 = new / (lead * lead * rq - lead * a1 * (rq2 + qq) + a1 * a1 * qq2)
    surf_ref[...] = a1 * r + a2 * (lead * r - a1 * q1)
    res_ref[...] = r - a1 * q1 - a2 * (lead * q1 - a1 * q2)
    tend_ref[...] = tend_in[...]


def body(features, spline_coef, edge_mask, head_weight, land_mask, shift_coef):
    n_lon, n_lat = lax.axis_size("lon"), lax.axis_size("lat")
    vmem = pl.BlockSpec(memory_space=pltpu.VMEM)
    dma = pltpu.SemaphoreType.DMA
    tend_shape = jax.ShapeDtypeStruct((2, L, ROWS, COLS), BF16)
    field_shape = jax.ShapeDtypeStruct((ROWS, COLS), F32)
    scratch = [
        pltpu.VMEM((C, L, ROWS, COLS), BF16),
        pltpu.VMEM((9 * C, C * J), BF16),
        pltpu.VMEM((C, C), jnp.int32),
        pltpu.VMEM((2, C), BF16),
        pltpu.VMEM((ROWS, COLS), jnp.int32),
        pltpu.VMEM((ROWS, COLS), F32),
        pltpu.VMEM((GROUPS, 64, CHUNK), BF16),
        pltpu.VMEM((CHUNK, COLS), BF16),
        pltpu.VMEM((CHUNK, COLS), BF16),
        pltpu.VMEM((L, 64, WIDE), F32),
        pltpu.VMEM((16, WIDE + 256), BF16),
        pltpu.VMEM((16, WIDE + 256), BF16),
        pltpu.VMEM((64, 128), BF16),
        pltpu.VMEM((64, 128), BF16),
        pltpu.VMEM((6, 16, WIDE), BF16),
        pltpu.VMEM((2, 64, 128), BF16),
        pltpu.VMEM((n_lat, 1, 128), F32),
        pltpu.VMEM((n_lon, 1, 128), F32),
        dma((GROUPS,)), dma((5,)), dma((8,)), dma((8,)), dma((2,)), dma((2,)),
    ]
    tendency, fields, sums = pl.pallas_call(
        functools.partial(kernel, n_lon, n_lat),
        out_shape=(
            pltpu.VMEM((2, L, ROWS, COLS), BF16),
            pltpu.VMEM((3 * ROWS, COLS), F32),
            pltpu.VMEM((1, 128), F32),
        ),
        in_specs=[pl.BlockSpec(memory_space=pl.ANY)] * 6,
        out_specs=(vmem, vmem, vmem),
        scratch_shapes=scratch,
        compiler_params=pltpu.CompilerParams(collective_id=0, has_side_effects=True),
        name="closure_and_sums",
    )(features, spline_coef, edge_mask, head_weight, land_mask, shift_coef)
    return pl.pallas_call(
        finish,
        out_shape=(tend_shape, field_shape, field_shape),
        in_specs=[vmem] * 3,
        out_specs=(vmem, vmem, vmem),
        compiler_params=pltpu.CompilerParams(vmem_limit_bytes=4 * 1024 * 1024),
        name="finish",
    )(fields, sums, tendency)


def solution(mesh):
    in_specs = (P(None, None, "lat", "lon"), P(), P(), P(), P("lat", "lon"), P("lat", "lon"))
    out_specs = (P(None, None, "lat", "lon"), P("lat", "lon"), P("lat", "lon"))
    return jax.shard_map(body, mesh=mesh, in_specs=in_specs, out_specs=out_specs, check_vma=False)
```

```python
import functools
import math

import jax
import jax.numpy as jnp
from jax import lax
from jax.experimental import pallas as pl
from jax.experimental.pallas import tpu as pltpu
from jax.sharding import PartitionSpec as P

C = 48
NB = 9
J = NB + 1
L = 2
ROWS = 8
COLS = 512
WIDE = COLS + 128
F32 = jnp.float32
BF16 = jnp.bfloat16
MESH = pl.DeviceIdType.MESH
LOG2E = math.log2(math.e)
LIFT = 82
GROUP = 16
GROUPS = C // GROUP
CHUNK = GROUP * ROWS * J


def iota(shape, axis):
    return lax.broadcasted_iota(jnp.int32, shape, axis)


def dot(a, b):
    return jnp.dot(a, b, preferred_element_type=F32)


def ones_where(cond):
    return jnp.where(cond, 1.0, 0.0).astype(BF16)


def selections(spread_ref, offsets_ref, expand_ref):
    channel, lane = iota((C, C * J), 0), iota((C, C * J), 1)
    spread_ref[...] = ones_where((lane >= channel * J) & (lane < channel * J + J))
    o, q = iota((C, 9 * C), 0), iota((C, 9 * C), 1)
    offsets_ref[...] = ones_where(q - lax.shift_right_logical(q * 1366, 16) * C == o)
    q = iota((1, CHUNK), 1)
    strip = lax.shift_right_logical(q * 13108, 21)
    source = (2 * strip + (lax.shift_right_logical(q, 3) & 1)) * J + lax.shift_right_logical(q - strip * (2 * ROWS * J), 4)
    expand_ref[...] = ones_where(iota((GROUP * J, CHUNK), 0) == source)


def fold_weights(coef_ref, edge_ref, head_ref, spread_ref, offsets_ref):
    keep = dot(jnp.where(edge_ref[...] > 0, 1.0, 0.0).astype(BF16), spread_ref[...]).astype(BF16)
    head = dot(head_ref[...], offsets_ref[...])
    r, q = iota((24, 9 * C), 0), iota((24, 9 * C), 1)
    offset = lax.shift_right_logical(q * 1366, 16)
    head = jnp.where((r & 1) == 0, head[0:1], head[1:2])
    head = jnp.where(lax.shift_right_logical(r, 1) == offset, head, 0.0).astype(BF16)
    masked = [coef_ref[C * k : C * k + C, :] * keep for k in range(9)]
    folded = dot(head, jnp.concatenate(masked, axis=0))
    lane = iota((1, C * J), 1)
    j = lane - J * lax.shift_right_logical(lane * 6554, 16)
    off = jnp.abs(j - NB // 2).astype(F32)
    scale = jnp.where(j == NB, 2.0**LIFT, jnp.exp(-off * off))
    folded = folded * scale
    return folded


def band_weights(folded, expand_ref, wt, top):
    y_out = iota((ROWS, CHUNK), 0)
    y_in = iota((ROWS, CHUNK), 1) & 7
    first_row, last_row = y_in[0:6] == 0, y_in[0:6] == 7
    pad = jnp.zeros((2, CHUNK), F32)
    for group in range(GROUPS):
        g = dot(folded[:, GROUP * J * group : GROUP * J * (group + 1)].astype(BF16), expand_ref[...])
        tiles = []
        for k in range(6):
            tile = jnp.where(y_in == y_out - 1, g[k : k + 1], 0.0)
            tile = jnp.where(y_in == y_out, g[6 + k : 7 + k], tile)
            tiles.append(jnp.where(y_in == y_out + 1, g[12 + k : 13 + k], tile))
        mirrored = jnp.concatenate([g[16:18], g[14:16], g[12:14]], axis=0)
        above = jnp.where(top, mirrored, g[0:6])
        tiles += [jnp.where(first_row, g[12:18], 0.0), pad, jnp.where(last_row, above, 0.0), pad]
        wt[group] = jnp.concatenate(tiles, axis=0).astype(BF16)


def basis(x):
    half = x * 0.5
    middle = jnp.exp2((half * half) * (-16.0 * LOG2E) + float(LIFT))
    up = jnp.exp2(half * (8.0 * LOG2E))
    down = jnp.exp2(half * (-8.0 * LOG2E))
    silu = half + half * jnp.tanh(half)
    left, right = [middle], [middle]
    for _ in range(NB // 2):
        left.append(left[-1] * down)
        right.append(right[-1] * up)
    return left[:0:-1] + right + [silu]


def bits(value, flips):
    return jnp.bitwise_xor(value, flips) if flips else value


def kernel(
    n_lon, n_lat,
    feat_hbm, coef_hbm, edge_hbm, head_hbm, land_hbm, shift_hbm,
    tend_ref, fields_ref, sums_ref,
    feat, coef_ref, edge_ref, head_ref, land_ref, shift_ref, spread_ref, offsets_ref, expand_ref, wt, bases_a, bases_b, acc,
    north, south, to_east, to_west, got, side, sums_a, sums_b, sums_d,
    feat_sem, weight_sem, send, recv, send_sum, recv_sum,
):
    lon, lat = lax.axis_index("lon"), lax.axis_index("lat")
    top, bottom = lat == n_lat - 1, lat == 0
    east = jnp.where(lon == n_lon - 1, 0, lon + 1)
    west = jnp.where(lon == 0, n_lon - 1, lon - 1)
    up_lat = jnp.where(top, lat, lat + 1)
    up_lon = jnp.where(top, n_lon - 1 - lon, lon)
    up_east = jnp.where(top, n_lon - 1 - east, east)
    up_west = jnp.where(top, n_lon - 1 - west, west)
    down_lat = jnp.where(bottom, lat, lat - 1)
    east_self, west_self = top & (up_east == lon), top & (up_west == lon)
    east_other, west_other = jnp.logical_not(east_self), jnp.logical_not(west_self)
    has_south = jnp.logical_not(bottom)

    weights_in = [
        pltpu.make_async_copy(src, dst, weight_sem.at[k])
        for k, (src, dst) in enumerate(
            [(edge_hbm, edge_ref), (head_hbm, head_ref), (coef_hbm, coef_ref), (land_hbm, land_ref), (shift_hbm, shift_ref)]
        )
    ]

    def feat_in(k):
        part = pl.ds(k * GROUP, GROUP)
        return pltpu.make_async_copy(feat_hbm.at[part], feat.at[part], feat_sem.at[k])

    for copy in weights_in + [feat_in(k) for k in range(GROUPS)]:
        copy.start()

    half = n_lon // 2
    ring = {0: 0, 1: 1, 2: 2, 3: 3, 4: 4, 5: 3, 6: 2, 7: 2}

    def far_first(count, hops):
        return sorted(range(1, count), key=lambda d: -hops(d))

    first_order = far_first(n_lat, lambda d: ring.get(d // 2, 0))
    first_sum = [(bits(lon, d % 2), bits(lat, d - d % 2)) for d in first_order]
    first_here = lat - lax.rem(lat, 2) + lax.rem(lon, 2)
    second_order = far_first(n_lon, lambda d: (0, 1, 2, 1)[d % 4] + (0, 2, 1, 1)[d // 4 % 4])
    second_sum = [(bits(lon, 2 * (d % half)), bits(lat, d // half)) for d in second_order]
    second_here = lon // 2 + half * lax.rem(lat, 2)
    hubs = [(a, b) for b in (0, 2) for a in range(4)]

    def is_hub(at_lon, at_lat):
        return (at_lon < 4) & ((at_lat == 0) | (at_lat == 2))

    hub, hub_plane = is_hub(lon, lat), lat < 4
    direct_here = lon * n_lat + lat


    barrier = pltpu.get_barrier_semaphore()

    def greet(at_lon, at_lat):
        pl.semaphore_signal(barrier, inc=1, device_id={"lon": at_lon, "lat": at_lat}, device_id_type=MESH)

    greet(east, lat)
    greet(west, lat)
    greet(up_lon, up_lat)
    pl.when(east_other)(lambda: greet(up_east, up_lat))
    pl.when(west_other)(lambda: greet(up_west, up_lat))

    @pl.when(has_south)
    def _():
        greet(lon, down_lat)
        greet(east, down_lat)
        greet(west, down_lat)

    for at in first_sum + second_sum:
        greet(*at)

    @pl.when(hub)
    def _():
        for f in range(1, n_lon):
            greet(bits(lon, f), lat)

        def band(b, carry):
            for f in range(n_lon):
                greet(bits(lon, f), jnp.bitwise_xor(lat, b))
            return carry

        lax.fori_loop(1, n_lat, band, 0)

    greetings = n_lon + n_lat + 6 - jnp.where(east_self, 1, 0) - jnp.where(west_self, 1, 0) - jnp.where(bottom, 3, 0) + len(hubs) - jnp.where(hub, 1, 0)

    def remote(src, dst, send, recv, at_lon, at_lat):
        return pltpu.make_async_remote_copy(
            src_ref=src, dst_ref=dst, send_sem=send, recv_sem=recv,
            device_id={"lon": at_lon, "lat": at_lat}, device_id_type=MESH,
        )

    @pl.when(bottom)
    def _():
        got[0:3] = jnp.zeros((3, 16, WIDE), BF16)

    selections(spread_ref, offsets_ref, expand_ref)
    acc[...] = jnp.zeros(acc.shape, F32)
    for copy in weights_in[:3]:
        copy.wait()
    folded = fold_weights(coef_ref, edge_ref, head_ref, spread_ref, offsets_ref)
    for copy in weights_in[3:]:
        copy.wait()
    feat_in(0).wait()
    band_weights(folded, expand_ref, wt, top)


    def expanded(k, out):
        for at in range(0, GROUP, 2):
            x = feat[pl.ds((k // L) * GROUP + at, 2), lax.rem(k, L)].astype(F32).reshape(2 * ROWS, COLS)
            for j, value in enumerate(basis(x)):
                row = (at * J + 2 * j) * ROWS
                out[row : row + 2 * ROWS, :] = value.astype(BF16)

    def contracted(k, bases):
        acc[lax.rem(k, L), :, 0:COLS] += dot(wt[k // L], bases[...])

    expanded(0, bases_a)
    for k in range(1, GROUPS):
        feat_in(k).wait()

    def step(i, carry):
        expanded(2 * i + 1, bases_b)
        contracted(2 * i, bases_a)
        expanded(jnp.minimum(2 * i + 2, L * GROUPS - 1), bases_a)
        contracted(2 * i + 1, bases_b)
        return carry

    lax.fori_loop(0, GROUPS * L // 2, step, 0)

    @pl.when(bottom)
    def _():
        q = iota((1, CHUNK), 1)
        j = lax.shift_right_logical(q - lax.shift_right_logical(q * 13108, 21) * (2 * ROWS * J), 4)
        outside = jnp.zeros((8, CHUNK), F32)
        for group in range(GROUPS):
            outside = outside + wt[group, 48:64, :].astype(F32)[8:16]
        outside = jnp.sum(jnp.where(j < NB, outside, 0.0), axis=1, keepdims=True) * (2.0**LIFT)
        for level in range(L):
            for c in range(2):
                acc[level, 16 + 8 * c : 17 + 8 * c, 0:COLS] += outside[c : c + 1] + outside[c + 2 : c + 3] + outside[c + 4 : c + 5]

    lane, low = iota((ROWS, 128), 1), iota((ROWS, 128), 1) < 64
    low2 = iota((16, 128), 1) < 64
    row = iota((ROWS, WIDE), 0)
    zero = jnp.zeros((ROWS, WIDE), F32)

    def joined(parts):
        return jnp.concatenate(parts, axis=1)

    def stacked(parts):
        return jnp.concatenate(parts, axis=0)

    def lanes(x, by):
        return pltpu.roll(x, by % WIDE, 1)

    def rows(x, by):
        return pltpu.roll(x, by % 16, 0)

    def placed(entries):
        out = zero
        for at, value in entries:
            out = jnp.where(row == at, value, out)
        return out

    own, above, below = [], [], []
    for level in range(L):
        a = acc[level] * (2.0**-LIFT)
        own.append(a[16:32] + lanes(a[0:16], 1) + lanes(a[32:48], -1))
        outer = a[48:64]
        before, after = lanes(outer, 1), lanes(outer, -1)
        below.append(outer[2:4] + before[0:2] + after[4:6])
        above.append(outer[10:12] + before[8:10] + after[12:14])
    total, total_up, total_down = own[0] + own[1], above[0] + above[1], below[0] + below[1]
    share = [stacked([total[8 * c : 8 * c + 8], placed([(0, total_up[c : c + 1]), (7, total_down[c : c + 1])])]) for c in range(2)]
    upper = own[1]

    ocean = joined([land_ref[...].astype(F32), zero[:, 0:128]])
    shift = joined([shift_ref[...], zero[:, 0:128]])

    def both(r):
        return [total[r : r + 1], total[8 + r : 9 + r]]

    none = [zero[0:1]]
    edge_n = stacked(
        [total_up] + both(7) + both(6) + both(5) + [above[1], ocean[7:8], ocean[6:7], ocean[5:6], shift[7:8]] + none * 2
    )
    edge_s = stacked(
        [total_down] + both(0) + both(1) + none * 2 + [below[1], ocean[0:1], ocean[1:2]] + none + [shift[0:1]] + none * 2
    )
    edge_e = stacked(share + [upper, ocean, shift])

    def eastern(x):
        return jnp.where(iota((x.shape[0], 128), 1) < 64, x[:, COLS:], x[:, COLS - 128 : COLS])

    def western(x):
        return jnp.where(iota((x.shape[0], 128), 1) < 64, x[:, 0:128], x[:, COLS:])

    corner = pl.ds(WIDE, 128), pl.ds(WIDE + 128, 128)
    for edge, ref in ((edge_n, north), (edge_s, south)):
        ref[...] = joined([edge, eastern(edge), western(edge)]).astype(BF16)
    to_east[...] = eastern(edge_e).astype(BF16)
    to_west[...] = western(edge_e).astype(BF16)

    whole, part = pl.ds(0, WIDE), pl.ds(0, 128)
    upward = jnp.where(top, 3, 0)
    sends = [
        (east_other, remote(north.at[:, corner[0]], got.at[upward + 1, :, part], send.at[1], recv.at[upward + 1], up_east, up_lat)),
        (west_other, remote(north.at[:, corner[1]], got.at[upward + 2, :, part], send.at[2], recv.at[upward + 2], up_west, up_lat)),
        (has_south, remote(south.at[:, corner[0]], got.at[4, :, part], send.at[4], recv.at[4], east, down_lat)),
        (has_south, remote(south.at[:, corner[1]], got.at[5, :, part], send.at[5], recv.at[5], west, down_lat)),
        (None, remote(north.at[:, whole], got.at[upward], send.at[0], recv.at[upward], up_lon, up_lat)),
        (has_south, remote(south.at[:, whole], got.at[3], send.at[3], recv.at[3], lon, down_lat)),
        (None, remote(to_east, side.at[0], send.at[6], recv.at[6], east, lat)),
        (None, remote(to_west, side.at[1], send.at[7], recv.at[7], west, lat)),
    ]

    def arrival(src, dst, k):
        return remote(src, dst, send.at[0], recv.at[k], east, lat)

    corner_n = north.at[:, corner[0]]
    arrivals = [
        (None, arrival(to_east, side.at[0], 6)),
        (None, arrival(to_west, side.at[1], 7)),
        (has_south, arrival(north.at[:, whole], got.at[0], 0)),
        (has_south, arrival(corner_n, got.at[1, :, part], 1)),
        (has_south, arrival(corner_n, got.at[2, :, part], 2)),
        (None, arrival(north.at[:, whole], got.at[3], 3)),
        (east_other, arrival(corner_n, got.at[4, :, part], 4)),
        (west_other, arrival(corner_n, got.at[5, :, part], 5)),
    ]

    def each(entries, act):
        for cond, copy in entries:
            if cond is None:
                act(copy)
            else:
                pl.when(cond)(functools.partial(act, copy))

    pl.semaphore_wait(barrier, greetings)
    each(sends, lambda copy: copy.start())

    @pl.when(east_self)
    def _():
        got[4, :, 0:128] = north[:, WIDE : WIDE + 128]

    @pl.when(west_self)
    def _():
        got[5, :, 0:128] = north[:, WIDE + 128 :]

    each(arrivals, lambda copy: copy.wait_recv())

    def arrived(k):
        parts = [got[k, :, 128 * t : 128 * t + 128].astype(F32) for t in range(5)]
        w, e = got[k + 1, :, 0:128].astype(F32), got[k + 2, :, 0:128].astype(F32)
        return [
            parts[0] + jnp.where(low2, w, 0.0), parts[1], parts[2],
            parts[3] + jnp.where(low2, 0.0, e), parts[4] + jnp.where(low2, e, w),
        ]

    backwards = 127 - lane

    def turned(x):
        return stacked([jnp.take_along_axis(x[r : r + 8], backwards, axis=1) for r in (0, 8)])

    s_rows = joined(arrived(0))
    n_parts = arrived(3)
    flipped = [turned(x) for x in n_parts]
    flipped = flipped[3::-1] + flipped[4:]
    n_rows = joined([jnp.where(top, f, n) for f, n in zip(flipped, n_parts)])
    from_west, from_east = side[0].astype(F32), side[1].astype(F32)

    def with_sides(x, at):
        count = x.shape[0]
        w, e = from_west[at : at + count], from_east[at : at + count]
        near = iota((count, 128), 1) < 64
        return joined([
            x[:, 0:128] + jnp.where(near, w, 0.0),
            x[:, 128 : COLS - 128],
            x[:, COLS - 128 : COLS] + jnp.where(near, 0.0, e),
            x[:, COLS:] + jnp.where(near, e, w),
        ])

    def one(x, k):
        return x[k : k + 1]

    m = stacked([
        with_sides(ocean, 48),
        placed([(r, one(n_rows, 10 + r)) for r in range(3)] + [(7 - r, one(s_rows, 10 + r)) for r in range(3)]),
    ])
    s = stacked([with_sides(shift, 56), placed([(0, one(n_rows, 13)), (7, one(s_rows, 13))])])
    eastward, northward = [
        m * (
            with_sides(share[c], 16 * c)
            + stacked([
                placed([(0, one(s_rows, c)), (7, one(n_rows, c))]),
                placed([(r, one(n_rows, 2 + 2 * r + c)) for r in range(3)] + [(7 - r, one(s_rows, 2 + 2 * r + c)) for r in range(3)]),
            ])
        )
        for c in range(2)
    ]
    r = m * (eastward - lanes(eastward, 1) + northward - rows(northward, 1))
    beyond = m * (eastward - lanes(eastward, -1) + northward - rows(northward, -1))
    r = stacked([r[0:8], jnp.where(top & (row < 2), beyond[8:16], r[8:16])])

    def operate(v):
        return m * ((4.0 + s) * v - (lanes(v, 1) + lanes(v, -1) + rows(v, 1) + rows(v, -1)))

    q1 = operate(r)
    q2 = operate(q1)[0:8, 0:COLS]
    r, q1 = r[0:8, 0:COLS], q1[0:8, 0:COLS]

    def summed(x):
        x = x[:, 0:128] + x[:, 128:256] + x[:, 256:384] + x[:, 384:512]
        return jnp.sum(x, axis=0, keepdims=True)

    dots = [summed(r * r), summed(r * q1), summed(q1 * q1), summed(r * q2), summed(q1 * q2)]

    def row_to(ref, stage, here, at):
        remote(ref.at[here], ref.at[here], send_sum.at[stage], recv_sum.at[stage], *at).start()

    def rows_of(ref, stage, number):
        several = ref.at[pl.ds(0, number)]
        return remote(several, several, send_sum.at[stage], recv_sum.at[stage], east, lat)

    dots = jnp.sum(stacked(dots + [jnp.zeros((3, 128), F32)]), axis=1, keepdims=True)
    dots = jnp.sum(jnp.where(lane == iota((ROWS, 128), 0), dots, 0.0), axis=0, keepdims=True)
    sums_d[direct_here] = dots
    sums_a[first_here] = dots
    for at in hubs:
        other = (lon != at[0]) | (lat != at[1])
        pl.when(other)(functools.partial(row_to, sums_d, 2, direct_here, at))
    for at in first_sum:
        row_to(sums_a, 0, first_here, at)

    @pl.when(lat >= 0)
    def _():
        second = with_sides(upper, 32)
        for c in range(2):
            one_level = second[8 * c : 8 * c + 8] + placed([(0, one(s_rows, 8 + c)), (7, one(n_rows, 8 + c))])
            one_level = ocean[:, 0:COLS] * one_level[:, 0:COLS]
            whole = (eastward, northward)[c][0:8, 0:COLS]
            tend_ref[c, 0] = (whole - one_level).astype(BF16)
            tend_ref[c, 1] = one_level.astype(BF16)
        for k, value in enumerate((r, q1, q2)):
            fields_ref[8 * k : 8 * k + 8, :] = value

    each(sends, lambda copy: copy.wait_send())

    rows_of(sums_a, 0, n_lat - 1).wait_recv()
    sums_b[second_here] = jnp.sum(sums_a[...], axis=0)
    for at in second_sum:
        pl.when(jnp.logical_not(is_hub(*at)))(functools.partial(row_to, sums_b, 1, second_here, at))

    @pl.when(hub)
    def _():
        rows_of(sums_d, 2, n_lon * n_lat - 1).wait_recv()
        sums_ref[...] = jnp.sum(sums_d[...], axis=0)
        rows_of(sums_d, 2, len(hubs) - 1).wait_send()
        rows_of(sums_b, 1, n_lon - 2).wait_send()

    @pl.when(jnp.logical_not(hub))
    def _():
        rows_of(sums_b, 1, n_lon - 1).wait_recv()
        sums_ref[...] = jnp.sum(sums_b[...], axis=0)
        rows_of(sums_d, 2, len(hubs)).wait_send()
        pl.when(hub_plane)(lambda: rows_of(sums_b, 1, n_lon - 3).wait_send())
        pl.when(jnp.logical_not(hub_plane))(lambda: rows_of(sums_b, 1, n_lon - 1).wait_send())

    rows_of(sums_a, 0, n_lat - 1).wait_send()


def finish(fields_ref, sums_ref, tend_in, tend_ref, surf_ref, res_ref):
    r, q1, q2 = fields_ref[0:8, :], fields_ref[8:16, :], fields_ref[16:24, :]
    rr, rq, qq, rq2, qq2 = [sums_ref[0:1, k : k + 1] for k in range(5)]
    a1 = rr / rq
    new = rr - 2.0 * a1 * rq + a1 * a1 * qq
    lead = 1.0 + new / rr
    a2 = new / (lead * lead * rq - lead * a1 * (rq2 + qq) + a1 * a1 * qq2)
    surf_ref[...] = a1 * r + a2 * (lead * r - a1 * q1)
    res_ref[...] = r - a1 * q1 - a2 * (lead * q1 - a1 * q2)
    tend_ref[...] = tend_in[...]


def body(features, spline_coef, edge_mask, head_weight, land_mask, shift_coef):
    n_lon, n_lat = lax.axis_size("lon"), lax.axis_size("lat")
    vmem = pl.BlockSpec(memory_space=pltpu.VMEM)
    dma = pltpu.SemaphoreType.DMA
    tend_shape = jax.ShapeDtypeStruct((2, L, ROWS, COLS), BF16)
    field_shape = jax.ShapeDtypeStruct((ROWS, COLS), F32)
    scratch = [
        pltpu.VMEM((C, L, ROWS, COLS), BF16),
        pltpu.VMEM((9 * C, C * J), BF16),
        pltpu.VMEM((C, C), jnp.int32),
        pltpu.VMEM((2, C), BF16),
        pltpu.VMEM((ROWS, COLS), jnp.int32),
        pltpu.VMEM((ROWS, COLS), F32),
        pltpu.VMEM((C, C * J), BF16),
        pltpu.VMEM((C, 9 * C), BF16),
        pltpu.VMEM((GROUP * J, CHUNK), BF16),
        pltpu.VMEM((GROUPS, 64, CHUNK), BF16),
        pltpu.VMEM((CHUNK, COLS), BF16),
        pltpu.VMEM((CHUNK, COLS), BF16),
        pltpu.VMEM((L, 64, WIDE), F32),
        pltpu.VMEM((16, WIDE + 256), BF16),
        pltpu.VMEM((16, WIDE + 256), BF16),
        pltpu.VMEM((64, 128), BF16),
        pltpu.VMEM((64, 128), BF16),
        pltpu.VMEM((6, 16, WIDE), BF16),
        pltpu.VMEM((2, 64, 128), BF16),
        pltpu.VMEM((n_lat, 1, 128), F32),
        pltpu.VMEM((n_lon, 1, 128), F32),
        pltpu.VMEM((n_lon * n_lat, 1, 128), F32),
        dma((GROUPS,)), dma((5,)), dma((8,)), dma((8,)), dma((3,)), dma((3,)),
    ]
    tendency, fields, sums = pl.pallas_call(
        functools.partial(kernel, n_lon, n_lat),
        out_shape=(
            pltpu.VMEM((2, L, ROWS, COLS), BF16),
            pltpu.VMEM((3 * ROWS, COLS), F32),
            pltpu.VMEM((1, 128), F32),
        ),
        in_specs=[pl.BlockSpec(memory_space=pl.ANY)] * 6,
        out_specs=(vmem, vmem, vmem),
        scratch_shapes=scratch,
        compiler_params=pltpu.CompilerParams(collective_id=0, has_side_effects=True),
        name="closure_and_sums",
    )(features, spline_coef, edge_mask, head_weight, land_mask, shift_coef)
    return pl.pallas_call(
        finish,
        out_shape=(tend_shape, field_shape, field_shape),
        in_specs=[vmem] * 3,
        out_specs=(vmem, vmem, vmem),
        compiler_params=pltpu.CompilerParams(vmem_limit_bytes=4 * 1024 * 1024),
        name="finish",
    )(fields, sums, tendency)


def solution(mesh):
    in_specs = (P(None, None, "lat", "lon"), P(), P(), P(), P("lat", "lon"), P("lat", "lon"))
    out_specs = (P(None, None, "lat", "lon"), P("lat", "lon"), P("lat", "lon"))
    return jax.shard_map(body, mesh=mesh, in_specs=in_specs, out_specs=out_specs, check_vma=False)
```

```python
import functools
import math

import jax
import jax.numpy as jnp
from jax import lax
from jax.experimental import pallas as pl
from jax.experimental.pallas import tpu as pltpu
from jax.sharding import PartitionSpec as P

C = 48
NB = 9
J = NB + 1
L = 2
ROWS = 8
COLS = 512
WIDE = COLS + 128
F32 = jnp.float32
BF16 = jnp.bfloat16
MESH = pl.DeviceIdType.MESH
LOG2E = math.log2(math.e)
LIFT = 82
GROUP = 16
GROUPS = C // GROUP
CHUNK = GROUP * ROWS * J


def iota(shape, axis):
    return lax.broadcasted_iota(jnp.int32, shape, axis)


def dot(a, b):
    return jnp.dot(a, b, preferred_element_type=F32)


def ones_where(cond):
    return jnp.where(cond, 1.0, 0.0).astype(BF16)


def selections(spread_ref, offsets_ref, expand_ref):
    channel, lane = iota((C, C * J), 0), iota((C, C * J), 1)
    spread_ref[...] = ones_where((lane >= channel * J) & (lane < channel * J + J))
    o, q = iota((C, 9 * C), 0), iota((C, 9 * C), 1)
    offsets_ref[...] = ones_where(q - lax.shift_right_logical(q * 1366, 16) * C == o)
    q = iota((1, CHUNK), 1)
    strip = lax.shift_right_logical(q * 13108, 21)
    source = (2 * strip + (lax.shift_right_logical(q, 3) & 1)) * J + lax.shift_right_logical(q - strip * (2 * ROWS * J), 4)
    expand_ref[...] = ones_where(iota((GROUP * J, CHUNK), 0) == source)


def fold_weights(coef_ref, edge_ref, head_ref, spread_ref, offsets_ref):
    keep = dot(jnp.where(edge_ref[...] > 0, 1.0, 0.0).astype(BF16), spread_ref[...]).astype(BF16)
    head = dot(head_ref[...], offsets_ref[...])
    r, q = iota((24, 9 * C), 0), iota((24, 9 * C), 1)
    offset = lax.shift_right_logical(q * 1366, 16)
    head = jnp.where((r & 1) == 0, head[0:1], head[1:2])
    head = jnp.where(lax.shift_right_logical(r, 1) == offset, head, 0.0).astype(BF16)
    masked = [coef_ref[C * k : C * k + C, :] * keep for k in range(9)]
    folded = dot(head, jnp.concatenate(masked, axis=0))
    lane = iota((1, C * J), 1)
    j = lane - J * lax.shift_right_logical(lane * 6554, 16)
    off = jnp.abs(j - NB // 2).astype(F32)
    scale = jnp.where(j == NB, 2.0**LIFT, jnp.exp(-off * off))
    folded = folded * scale
    return folded


def band_weights(folded, expand_ref, wt, top):
    y_out = iota((ROWS, CHUNK), 0)
    y_in = iota((ROWS, CHUNK), 1) & 7
    first_row, last_row = y_in[0:6] == 0, y_in[0:6] == 7
    pad = jnp.zeros((2, CHUNK), F32)
    for group in range(GROUPS):
        g = dot(folded[:, GROUP * J * group : GROUP * J * (group + 1)].astype(BF16), expand_ref[...])
        tiles = []
        for k in range(6):
            tile = jnp.where(y_in == y_out - 1, g[k : k + 1], 0.0)
            tile = jnp.where(y_in == y_out, g[6 + k : 7 + k], tile)
            tiles.append(jnp.where(y_in == y_out + 1, g[12 + k : 13 + k], tile))
        mirrored = jnp.concatenate([g[16:18], g[14:16], g[12:14]], axis=0)
        above = jnp.where(top, mirrored, g[0:6])
        tiles += [jnp.where(first_row, g[12:18], 0.0), pad, jnp.where(last_row, above, 0.0), pad]
        wt[group] = jnp.concatenate(tiles, axis=0).astype(BF16)


def basis(x):
    half = x * 0.5
    middle = jnp.exp2((half * half) * (-16.0 * LOG2E) + float(LIFT))
    up = jnp.exp2(half * (8.0 * LOG2E))
    down = jnp.exp2(half * (-8.0 * LOG2E))
    silu = half + half * jnp.tanh(half)
    left, right = [middle], [middle]
    for _ in range(NB // 2):
        left.append(left[-1] * down)
        right.append(right[-1] * up)
    return left[:0:-1] + right + [silu]


def bits(value, flips):
    return jnp.bitwise_xor(value, flips) if flips else value


def kernel(
    n_lon, n_lat,
    feat_hbm, coef_hbm, edge_hbm, head_hbm, land_hbm, shift_hbm,
    tend_ref, fields_ref, sums_ref,
    feat, coef_ref, edge_ref, head_ref, land_ref, shift_ref, spread_ref, offsets_ref, expand_ref, wt, bases_a, bases_b, acc,
    north, south, to_east, to_west, got, side, sums_a, sums_b, sums_d,
    feat_sem, weight_sem, send, recv, send_sum, recv_sum,
):
    weights_in = [
        pltpu.make_async_copy(src, dst, weight_sem.at[k])
        for k, (src, dst) in enumerate(
            [(edge_hbm, edge_ref), (head_hbm, head_ref), (coef_hbm, coef_ref), (land_hbm, land_ref), (shift_hbm, shift_ref)]
        )
    ]

    def feat_in(k):
        part = pl.ds(k * GROUP, GROUP)
        return pltpu.make_async_copy(feat_hbm.at[part], feat.at[part], feat_sem.at[k])

    for copy in weights_in + [feat_in(k) for k in range(GROUPS)]:
        copy.start()

    lon, lat = lax.axis_index("lon"), lax.axis_index("lat")
    top, bottom = lat == n_lat - 1, lat == 0
    east = jnp.where(lon == n_lon - 1, 0, lon + 1)
    west = jnp.where(lon == 0, n_lon - 1, lon - 1)
    up_lat = jnp.where(top, lat, lat + 1)
    up_lon = jnp.where(top, n_lon - 1 - lon, lon)
    up_east = jnp.where(top, n_lon - 1 - east, east)
    up_west = jnp.where(top, n_lon - 1 - west, west)
    down_lat = jnp.where(bottom, lat, lat - 1)
    east_self, west_self = top & (up_east == lon), top & (up_west == lon)
    east_other, west_other = jnp.logical_not(east_self), jnp.logical_not(west_self)
    has_south = jnp.logical_not(bottom)

    half = n_lon // 2
    ring = {0: 0, 1: 1, 2: 2, 3: 3, 4: 4, 5: 3, 6: 2, 7: 2}

    def far_first(count, hops):
        return sorted(range(1, count), key=lambda d: -hops(d))

    first_order = far_first(n_lat, lambda d: ring.get(d // 2, 0))
    first_sum = [(bits(lon, d % 2), bits(lat, d - d % 2)) for d in first_order]
    first_here = lat - lax.rem(lat, 2) + lax.rem(lon, 2)
    second_order = far_first(n_lon, lambda d: (0, 1, 2, 1)[d % 4] + (0, 2, 1, 1)[d // 4 % 4])
    second_sum = [(bits(lon, 2 * (d % half)), bits(lat, d // half)) for d in second_order]
    second_here = lon // 2 + half * lax.rem(lat, 2)
    hub_lon, hub_lat = max(2, n_lon // 4), max(2, n_lat // 4)
    hubs = [(a, b) for b in range(hub_lat) for a in range(hub_lon)]

    def is_hub(at_lon, at_lat):
        return (at_lon < hub_lon) & (at_lat < hub_lat)

    hub, hub_plane = is_hub(lon, lat), lat < hub_lat
    direct_here = lon * n_lat + lat


    barrier = pltpu.get_barrier_semaphore()

    def greet(at_lon, at_lat):
        pl.semaphore_signal(barrier, inc=1, device_id={"lon": at_lon, "lat": at_lat}, device_id_type=MESH)

    greet(east, lat)
    greet(west, lat)
    greet(up_lon, up_lat)
    pl.when(east_other)(lambda: greet(up_east, up_lat))
    pl.when(west_other)(lambda: greet(up_west, up_lat))

    @pl.when(has_south)
    def _():
        greet(lon, down_lat)
        greet(east, down_lat)
        greet(west, down_lat)

    for at in first_sum + second_sum:
        greet(*at)

    @pl.when(hub)
    def _():
        for f in range(1, n_lon):
            greet(bits(lon, f), lat)

        def band(b, carry):
            for f in range(n_lon):
                greet(bits(lon, f), jnp.bitwise_xor(lat, b))
            return carry

        lax.fori_loop(1, n_lat, band, 0)

    greetings = n_lon + n_lat + 6 - jnp.where(east_self, 1, 0) - jnp.where(west_self, 1, 0) - jnp.where(bottom, 3, 0) + len(hubs) - jnp.where(hub, 1, 0)

    def remote(src, dst, send, recv, at_lon, at_lat):
        return pltpu.make_async_remote_copy(
            src_ref=src, dst_ref=dst, send_sem=send, recv_sem=recv,
            device_id={"lon": at_lon, "lat": at_lat}, device_id_type=MESH,
        )

    @pl.when(bottom)
    def _():
        got[0:3] = jnp.zeros((3, 16, WIDE), BF16)

    selections(spread_ref, offsets_ref, expand_ref)
    acc[...] = jnp.zeros(acc.shape, F32)
    for copy in weights_in[:3]:
        copy.wait()
    folded = fold_weights(coef_ref, edge_ref, head_ref, spread_ref, offsets_ref)
    for copy in weights_in[3:]:
        copy.wait()
    feat_in(0).wait()
    band_weights(folded, expand_ref, wt, top)


    def expanded(k, out):
        for at in range(0, GROUP, 2):
            x = feat[pl.ds((k // L) * GROUP + at, 2), lax.rem(k, L)].astype(F32).reshape(2 * ROWS, COLS)
            for j, value in enumerate(basis(x)):
                row = (at * J + 2 * j) * ROWS
                out[row : row + 2 * ROWS, :] = value.astype(BF16)

    def contracted(k, bases):
        acc[lax.rem(k, L), :, 0:COLS] += dot(wt[k // L], bases[...])

    expanded(0, bases_a)
    for k in range(1, GROUPS):
        feat_in(k).wait()

    def step(i, carry):
        expanded(2 * i + 1, bases_b)
        contracted(2 * i, bases_a)
        expanded(jnp.minimum(2 * i + 2, L * GROUPS - 1), bases_a)
        contracted(2 * i + 1, bases_b)
        return carry

    lax.fori_loop(0, GROUPS * L // 2, step, 0)

    @pl.when(bottom)
    def _():
        q = iota((1, CHUNK), 1)
        j = lax.shift_right_logical(q - lax.shift_right_logical(q * 13108, 21) * (2 * ROWS * J), 4)
        outside = jnp.zeros((8, CHUNK), F32)
        for group in range(GROUPS):
            outside = outside + wt[group, 48:64, :].astype(F32)[8:16]
        outside = jnp.sum(jnp.where(j < NB, outside, 0.0), axis=1, keepdims=True) * (2.0**LIFT)
        for level in range(L):
            for c in range(2):
                acc[level, 16 + 8 * c : 17 + 8 * c, 0:COLS] += outside[c : c + 1] + outside[c + 2 : c + 3] + outside[c + 4 : c + 5]

    lane, low = iota((ROWS, 128), 1), iota((ROWS, 128), 1) < 64
    low2 = iota((16, 128), 1) < 64
    row = iota((ROWS, WIDE), 0)
    zero = jnp.zeros((ROWS, WIDE), F32)

    def joined(parts):
        return jnp.concatenate(parts, axis=1)

    def stacked(parts):
        return jnp.concatenate(parts, axis=0)

    def lanes(x, by):
        return pltpu.roll(x, by % WIDE, 1)

    def rows(x, by):
        return pltpu.roll(x, by % 16, 0)

    def placed(entries):
        out = zero
        for at, value in entries:
            out = jnp.where(row == at, value, out)
        return out

    own, above, below = [], [], []
    for level in range(L):
        a = acc[level] * (2.0**-LIFT)
        own.append(a[16:32] + lanes(a[0:16], 1) + lanes(a[32:48], -1))
        outer = a[48:64]
        before, after = lanes(outer, 1), lanes(outer, -1)
        below.append(outer[2:4] + before[0:2] + after[4:6])
        above.append(outer[10:12] + before[8:10] + after[12:14])
    total, total_up, total_down = own[0] + own[1], above[0] + above[1], below[0] + below[1]
    share = [stacked([total[8 * c : 8 * c + 8], placed([(0, total_up[c : c + 1]), (7, total_down[c : c + 1])])]) for c in range(2)]
    upper = own[1]

    ocean = joined([land_ref[...].astype(F32), zero[:, 0:128]])
    shift = joined([shift_ref[...], zero[:, 0:128]])

    def both(r):
        return [total[r : r + 1], total[8 + r : 9 + r]]

    none = [zero[0:1]]
    edge_n = stacked(
        [total_up] + both(7) + both(6) + both(5) + [above[1], ocean[7:8], ocean[6:7], ocean[5:6], shift[7:8]] + none * 2
    )
    edge_s = stacked(
        [total_down] + both(0) + both(1) + none * 2 + [below[1], ocean[0:1], ocean[1:2]] + none + [shift[0:1]] + none * 2
    )
    edge_e = stacked(share + [upper, ocean, shift])

    def eastern(x):
        return jnp.where(iota((x.shape[0], 128), 1) < 64, x[:, COLS:], x[:, COLS - 128 : COLS])

    def western(x):
        return jnp.where(iota((x.shape[0], 128), 1) < 64, x[:, 0:128], x[:, COLS:])

    corner = pl.ds(WIDE, 128), pl.ds(WIDE + 128, 128)
    for edge, ref in ((edge_n, north), (edge_s, south)):
        ref[...] = joined([edge, eastern(edge), western(edge)]).astype(BF16)
    to_east[...] = eastern(edge_e).astype(BF16)
    to_west[...] = western(edge_e).astype(BF16)

    whole, part = pl.ds(0, WIDE), pl.ds(0, 128)
    upward = jnp.where(top, 3, 0)
    sends = [
        (east_other, remote(north.at[:, corner[0]], got.at[upward + 1, :, part], send.at[1], recv.at[upward + 1], up_east, up_lat)),
        (west_other, remote(north.at[:, corner[1]], got.at[upward + 2, :, part], send.at[2], recv.at[upward + 2], up_west, up_lat)),
        (has_south, remote(south.at[:, corner[0]], got.at[4, :, part], send.at[4], recv.at[4], east, down_lat)),
        (has_south, remote(south.at[:, corner[1]], got.at[5, :, part], send.at[5], recv.at[5], west, down_lat)),
        (None, remote(north.at[:, whole], got.at[upward], send.at[0], recv.at[upward], up_lon, up_lat)),
        (has_south, remote(south.at[:, whole], got.at[3], send.at[3], recv.at[3], lon, down_lat)),
        (None, remote(to_east, side.at[0], send.at[6], recv.at[6], east, lat)),
        (None, remote(to_west, side.at[1], send.at[7], recv.at[7], west, lat)),
    ]

    def arrival(src, dst, k):
        return remote(src, dst, send.at[0], recv.at[k], east, lat)

    corner_n = north.at[:, corner[0]]
    arrivals = [
        (None, arrival(to_east, side.at[0], 6)),
        (None, arrival(to_west, side.at[1], 7)),
        (has_south, arrival(north.at[:, whole], got.at[0], 0)),
        (has_south, arrival(corner_n, got.at[1, :, part], 1)),
        (has_south, arrival(corner_n, got.at[2, :, part], 2)),
        (None, arrival(north.at[:, whole], got.at[3], 3)),
        (east_other, arrival(corner_n, got.at[4, :, part], 4)),
        (west_other, arrival(corner_n, got.at[5, :, part], 5)),
    ]

    def each(entries, act):
        for cond, copy in entries:
            if cond is None:
                act(copy)
            else:
                pl.when(cond)(functools.partial(act, copy))

    pl.semaphore_wait(barrier, greetings)
    each(sends, lambda copy: copy.start())

    @pl.when(east_self)
    def _():
        got[4, :, 0:128] = north[:, WIDE : WIDE + 128]

    @pl.when(west_self)
    def _():
        got[5, :, 0:128] = north[:, WIDE + 128 :]

    each(arrivals, lambda copy: copy.wait_recv())

    def arrived(k):
        parts = [got[k, :, 128 * t : 128 * t + 128].astype(F32) for t in range(5)]
        w, e = got[k + 1, :, 0:128].astype(F32), got[k + 2, :, 0:128].astype(F32)
        return [
            parts[0] + jnp.where(low2, w, 0.0), parts[1], parts[2],
            parts[3] + jnp.where(low2, 0.0, e), parts[4] + jnp.where(low2, e, w),
        ]

    backwards = 127 - lane

    def turned(x):
        return stacked([jnp.take_along_axis(x[r : r + 8], backwards, axis=1) for r in (0, 8)])

    s_rows = joined(arrived(0))
    n_parts = arrived(3)
    flipped = [turned(x) for x in n_parts]
    flipped = flipped[3::-1] + flipped[4:]
    n_rows = joined([jnp.where(top, f, n) for f, n in zip(flipped, n_parts)])
    from_west, from_east = side[0].astype(F32), side[1].astype(F32)

    def with_sides(x, at):
        count = x.shape[0]
        w, e = from_west[at : at + count], from_east[at : at + count]
        near = iota((count, 128), 1) < 64
        return joined([
            x[:, 0:128] + jnp.where(near, w, 0.0),
            x[:, 128 : COLS - 128],
            x[:, COLS - 128 : COLS] + jnp.where(near, 0.0, e),
            x[:, COLS:] + jnp.where(near, e, w),
        ])

    def one(x, k):
        return x[k : k + 1]

    m = stacked([
        with_sides(ocean, 48),
        placed([(r, one(n_rows, 10 + r)) for r in range(3)] + [(7 - r, one(s_rows, 10 + r)) for r in range(3)]),
    ])
    s = stacked([with_sides(shift, 56), placed([(0, one(n_rows, 13)), (7, one(s_rows, 13))])])
    eastward, northward = [
        m * (
            with_sides(share[c], 16 * c)
            + stacked([
                placed([(0, one(s_rows, c)), (7, one(n_rows, c))]),
                placed([(r, one(n_rows, 2 + 2 * r + c)) for r in range(3)] + [(7 - r, one(s_rows, 2 + 2 * r + c)) for r in range(3)]),
            ])
        )
        for c in range(2)
    ]
    r = m * (eastward - lanes(eastward, 1) + northward - rows(northward, 1))
    beyond = m * (eastward - lanes(eastward, -1) + northward - rows(northward, -1))
    r = stacked([r[0:8], jnp.where(top & (row < 2), beyond[8:16], r[8:16])])

    def operate(v):
        return m * ((4.0 + s) * v - (lanes(v, 1) + lanes(v, -1) + rows(v, 1) + rows(v, -1)))

    q1 = operate(r)
    q2 = operate(q1)[0:8, 0:COLS]
    r, q1 = r[0:8, 0:COLS], q1[0:8, 0:COLS]

    def summed(x):
        x = x[:, 0:128] + x[:, 128:256] + x[:, 256:384] + x[:, 384:512]
        return jnp.sum(x, axis=0, keepdims=True)

    dots = [summed(r * r), summed(r * q1), summed(q1 * q1), summed(r * q2), summed(q1 * q2)]

    def row_to(ref, stage, here, at):
        remote(ref.at[here], ref.at[here], send_sum.at[stage], recv_sum.at[stage], *at).start()

    def rows_of(ref, stage, number):
        several = ref.at[pl.ds(0, number)]
        return remote(several, several, send_sum.at[stage], recv_sum.at[stage], east, lat)

    dots = jnp.sum(stacked(dots + [jnp.zeros((3, 128), F32)]), axis=1, keepdims=True)
    dots = jnp.sum(jnp.where(lane == iota((ROWS, 128), 0), dots, 0.0), axis=0, keepdims=True)
    direct_row = sums_d.at[pl.ds(direct_here, 1)]
    direct_row[...] = dots
    sums_a[first_here] = dots
    for at in hubs:
        other = (lon != at[0]) | (lat != at[1])
        pl.when(other)(remote(direct_row, direct_row, send_sum.at[2], recv_sum.at[2], *at).start)
    for at in first_sum:
        row_to(sums_a, 0, first_here, at)

    @pl.when(lat >= 0)
    def _():
        second = with_sides(upper, 32)
        for c in range(2):
            one_level = second[8 * c : 8 * c + 8] + placed([(0, one(s_rows, 8 + c)), (7, one(n_rows, 8 + c))])
            one_level = ocean[:, 0:COLS] * one_level[:, 0:COLS]
            whole = (eastward, northward)[c][0:8, 0:COLS]
            tend_ref[c, 0] = (whole - one_level).astype(BF16)
            tend_ref[c, 1] = one_level.astype(BF16)
        for k, value in enumerate((r, q1, q2)):
            fields_ref[8 * k : 8 * k + 8, :] = value

    each(sends, lambda copy: copy.wait_send())

    rows_of(sums_a, 0, n_lat - 1).wait_recv()
    sums_b[second_here] = jnp.sum(sums_a[...], axis=0)
    for at in second_sum:
        pl.when(jnp.logical_not(is_hub(*at)))(functools.partial(row_to, sums_b, 1, second_here, at))

    @pl.when(hub)
    def _():
        rows_of(sums_d, 2, n_lon * n_lat - 1).wait_recv()
        sums_ref[...] = jnp.sum(sums_d[...], axis=0, keepdims=True)
        rows_of(sums_d, 2, len(hubs) - 1).wait_send()
        rows_of(sums_b, 1, n_lon - hub_lon).wait_send()

    @pl.when(jnp.logical_not(hub))
    def _():
        rows_of(sums_b, 1, n_lon - 1).wait_recv()
        sums_ref[...] = jnp.sum(sums_b[...], axis=0)
        rows_of(sums_d, 2, len(hubs)).wait_send()
        pl.when(hub_plane)(lambda: rows_of(sums_b, 1, n_lon - 1 - hub_lon).wait_send())
        pl.when(jnp.logical_not(hub_plane))(lambda: rows_of(sums_b, 1, n_lon - 1).wait_send())

    rows_of(sums_a, 0, n_lat - 1).wait_send()


def finish(fields_ref, sums_ref, tend_in, tend_ref, surf_ref, res_ref):
    r, q1, q2 = fields_ref[0:8, :], fields_ref[8:16, :], fields_ref[16:24, :]
    rr, rq, qq, rq2, qq2 = [sums_ref[0:1, k : k + 1] for k in range(5)]
    a1 = rr / rq
    new = rr - 2.0 * a1 * rq + a1 * a1 * qq
    lead = 1.0 + new / rr
    a2 = new / (lead * lead * rq - lead * a1 * (rq2 + qq) + a1 * a1 * qq2)
    surf_ref[...] = a1 * r + a2 * (lead * r - a1 * q1)
    res_ref[...] = r - a1 * q1 - a2 * (lead * q1 - a1 * q2)
    tend_ref[...] = tend_in[...]


def body(features, spline_coef, edge_mask, head_weight, land_mask, shift_coef):
    n_lon, n_lat = lax.axis_size("lon"), lax.axis_size("lat")
    vmem = pl.BlockSpec(memory_space=pltpu.VMEM)
    dma = pltpu.SemaphoreType.DMA
    tend_shape = jax.ShapeDtypeStruct((2, L, ROWS, COLS), BF16)
    field_shape = jax.ShapeDtypeStruct((ROWS, COLS), F32)
    scratch = [
        pltpu.VMEM((C, L, ROWS, COLS), BF16),
        pltpu.VMEM((9 * C, C * J), BF16),
        pltpu.VMEM((C, C), jnp.int32),
        pltpu.VMEM((2, C), BF16),
        pltpu.VMEM((ROWS, COLS), jnp.int32),
        pltpu.VMEM((ROWS, COLS), F32),
        pltpu.VMEM((C, C * J), BF16),
        pltpu.VMEM((C, 9 * C), BF16),
        pltpu.VMEM((GROUP * J, CHUNK), BF16),
        pltpu.VMEM((GROUPS, 64, CHUNK), BF16),
        pltpu.VMEM((CHUNK, COLS), BF16),
        pltpu.VMEM((CHUNK, COLS), BF16),
        pltpu.VMEM((L, 64, WIDE), F32),
        pltpu.VMEM((16, WIDE + 256), BF16),
        pltpu.VMEM((16, WIDE + 256), BF16),
        pltpu.VMEM((64, 128), BF16),
        pltpu.VMEM((64, 128), BF16),
        pltpu.VMEM((6, 16, WIDE), BF16),
        pltpu.VMEM((2, 64, 128), BF16),
        pltpu.VMEM((n_lat, 1, 128), F32),
        pltpu.VMEM((n_lon, 1, 128), F32),
        pltpu.VMEM((n_lon * n_lat, 128), F32),
        dma((GROUPS,)), dma((5,)), dma((8,)), dma((8,)), dma((3,)), dma((3,)),
    ]
    tendency, fields, sums = pl.pallas_call(
        functools.partial(kernel, n_lon, n_lat),
        out_shape=(
            pltpu.VMEM((2, L, ROWS, COLS), BF16),
            pltpu.VMEM((3 * ROWS, COLS), F32),
            pltpu.VMEM((1, 128), F32),
        ),
        in_specs=[pl.BlockSpec(memory_space=pl.ANY)] * 6,
        out_specs=(vmem, vmem, vmem),
        scratch_shapes=scratch,
        compiler_params=pltpu.CompilerParams(collective_id=0, has_side_effects=True),
        name="closure_and_sums",
    )(features, spline_coef, edge_mask, head_weight, land_mask, shift_coef)
    return pl.pallas_call(
        finish,
        out_shape=(tend_shape, field_shape, field_shape),
        in_specs=[vmem] * 3,
        out_specs=(vmem, vmem, vmem),
        compiler_params=pltpu.CompilerParams(vmem_limit_bytes=4 * 1024 * 1024),
        name="finish",
    )(fields, sums, tendency)


def solution(mesh):
    in_specs = (P(None, None, "lat", "lon"), P(), P(), P(), P("lat", "lon"), P("lat", "lon"))
    out_specs = (P(None, None, "lat", "lon"), P("lat", "lon"), P("lat", "lon"))
    return jax.shard_map(body, mesh=mesh, in_specs=in_specs, out_specs=out_specs, check_vma=False)
```

```python
import functools
import math

import jax
import jax.numpy as jnp
from jax import lax
from jax.experimental import pallas as pl
from jax.experimental.pallas import tpu as pltpu
from jax.sharding import PartitionSpec as P

C = 48
NB = 9
J = NB + 1
L = 2
ROWS = 8
COLS = 512
WIDE = COLS + 128
F32 = jnp.float32
BF16 = jnp.bfloat16
MESH = pl.DeviceIdType.MESH
LOG2E = math.log2(math.e)
LIFT = 82
GROUP = 16
GROUPS = C // GROUP
CHUNK = GROUP * ROWS * J


def iota(shape, axis):
    return lax.broadcasted_iota(jnp.int32, shape, axis)


def dot(a, b):
    return jnp.dot(a, b, preferred_element_type=F32)


def ones_where(cond):
    return jnp.where(cond, 1.0, 0.0).astype(BF16)


def selections(spread_ref, offsets_ref, expand_ref):
    channel, lane = iota((C, C * J), 0), iota((C, C * J), 1)
    spread_ref[...] = ones_where((lane >= channel * J) & (lane < channel * J + J))
    o, q = iota((C, 9 * C), 0), iota((C, 9 * C), 1)
    offsets_ref[...] = ones_where(q - lax.shift_right_logical(q * 1366, 16) * C == o)
    q = iota((1, CHUNK), 1)
    strip = lax.shift_right_logical(q * 13108, 21)
    source = (2 * strip + (lax.shift_right_logical(q, 3) & 1)) * J + lax.shift_right_logical(q - strip * (2 * ROWS * J), 4)
    expand_ref[...] = ones_where(iota((GROUP * J, CHUNK), 0) == source)


def fold_weights(coef_ref, edge_ref, head_ref, spread_ref, offsets_ref):
    keep = dot(jnp.where(edge_ref[...] > 0, 1.0, 0.0).astype(BF16), spread_ref[...]).astype(BF16)
    head = dot(head_ref[...], offsets_ref[...])
    r, q = iota((24, 9 * C), 0), iota((24, 9 * C), 1)
    offset = lax.shift_right_logical(q * 1366, 16)
    head = jnp.where((r & 1) == 0, head[0:1], head[1:2])
    head = jnp.where(lax.shift_right_logical(r, 1) == offset, head, 0.0).astype(BF16)
    masked = [coef_ref[C * k : C * k + C, :] * keep for k in range(9)]
    folded = dot(head, jnp.concatenate(masked, axis=0))
    lane = iota((1, C * J), 1)
    j = lane - J * lax.shift_right_logical(lane * 6554, 16)
    off = jnp.abs(j - NB // 2).astype(F32)
    scale = jnp.where(j == NB, 2.0**LIFT, jnp.exp(-off * off))
    folded = folded * scale
    return folded


def band_weights(folded, expand_ref, wt, top):
    y_out = iota((ROWS, CHUNK), 0)
    y_in = iota((ROWS, CHUNK), 1) & 7
    first_row, last_row = y_in[0:6] == 0, y_in[0:6] == 7
    pad = jnp.zeros((2, CHUNK), F32)
    for group in range(GROUPS):
        g = dot(folded[:, GROUP * J * group : GROUP * J * (group + 1)].astype(BF16), expand_ref[...])
        tiles = []
        for k in range(6):
            tile = jnp.where(y_in == y_out - 1, g[k : k + 1], 0.0)
            tile = jnp.where(y_in == y_out, g[6 + k : 7 + k], tile)
            tiles.append(jnp.where(y_in == y_out + 1, g[12 + k : 13 + k], tile))
        mirrored = jnp.concatenate([g[16:18], g[14:16], g[12:14]], axis=0)
        above = jnp.where(top, mirrored, g[0:6])
        tiles += [jnp.where(first_row, g[12:18], 0.0), pad, jnp.where(last_row, above, 0.0), pad]
        wt[group] = jnp.concatenate(tiles, axis=0).astype(BF16)


def basis(x):
    half = x * 0.5
    middle = jnp.exp2((half * half) * (-16.0 * LOG2E) + float(LIFT))
    up = jnp.exp2(half * (8.0 * LOG2E))
    down = jnp.exp2(half * (-8.0 * LOG2E))
    silu = half + half * jnp.tanh(half)
    left, right = [middle], [middle]
    for _ in range(NB // 2):
        left.append(left[-1] * down)
        right.append(right[-1] * up)
    return left[:0:-1] + right + [silu]


def bits(value, flips):
    return jnp.bitwise_xor(value, flips) if flips else value


def kernel(
    n_lon, n_lat,
    feat_hbm, coef_hbm, edge_hbm, head_hbm, land_hbm, shift_hbm,
    tend_ref, fields_ref, sums_ref,
    feat, coef_ref, edge_ref, head_ref, land_ref, shift_ref, spread_ref, offsets_ref, expand_ref, wt, bases_a, bases_b, acc,
    north, south, to_east, to_west, got, side, sums_a, sums_b, sums_d,
    feat_sem, weight_sem, send, recv, send_sum, recv_sum,
):
    weights_in = [
        pltpu.make_async_copy(src, dst, weight_sem.at[k])
        for k, (src, dst) in enumerate(
            [(edge_hbm, edge_ref), (head_hbm, head_ref), (coef_hbm, coef_ref), (land_hbm, land_ref), (shift_hbm, shift_ref)]
        )
    ]

    def feat_in(k):
        part = pl.ds(k * GROUP, GROUP)
        return pltpu.make_async_copy(feat_hbm.at[part], feat.at[part], feat_sem.at[k])

    for copy in weights_in + [feat_in(k) for k in range(GROUPS)]:
        copy.start()

    lon, lat = lax.axis_index("lon"), lax.axis_index("lat")
    top, bottom = lat == n_lat - 1, lat == 0
    east = jnp.where(lon == n_lon - 1, 0, lon + 1)
    west = jnp.where(lon == 0, n_lon - 1, lon - 1)
    up_lat = jnp.where(top, lat, lat + 1)
    up_lon = jnp.where(top, n_lon - 1 - lon, lon)
    up_east = jnp.where(top, n_lon - 1 - east, east)
    up_west = jnp.where(top, n_lon - 1 - west, west)
    down_lat = jnp.where(bottom, lat, lat - 1)
    east_self, west_self = top & (up_east == lon), top & (up_west == lon)
    east_other, west_other = jnp.logical_not(east_self), jnp.logical_not(west_self)
    has_south = jnp.logical_not(bottom)

    half = n_lon // 2
    ring = {0: 0, 1: 1, 2: 2, 3: 3, 4: 4, 5: 3, 6: 2, 7: 2}

    def far_first(count, hops):
        return sorted(range(1, count), key=lambda d: -hops(d))

    first_order = far_first(n_lat, lambda d: ring.get(d // 2, 0))
    first_sum = [(bits(lon, d % 2), bits(lat, d - d % 2)) for d in first_order]
    first_here = lat - lax.rem(lat, 2) + lax.rem(lon, 2)
    second_order = far_first(n_lon, lambda d: (0, 1, 2, 1)[d % 4] + (0, 2, 1, 1)[d // 4 % 4])
    second_sum = [(bits(lon, 2 * (d % half)), bits(lat, d // half)) for d in second_order]
    second_here = lon // 2 + half * lax.rem(lat, 2)
    hubs = [(1, 0), (0, 2), (2, 0), (0, 1), (1, 2), (2, 2), (0, 4), (4, 0), (6, 0)]

    def is_hub(at_lon, at_lat):
        return functools.reduce(jnp.logical_or, [(at_lon == a) & (at_lat == b) for a, b in hubs])

    hub = is_hub(lon, lat)
    beside = sum(
        jnp.where((lat // 2 == b // 2) & (lax.rem(lon, 2) == a % 2) & ((lon != a) | (lat != b)), 1, 0) for a, b in hubs
    )
    most = max(sum(1 for a, b in hubs if b // 2 == z and a % 2 == c) for z in range(n_lat // 2) for c in range(2))
    direct_here = lon * n_lat + lat


    barrier = pltpu.get_barrier_semaphore()

    def greet(at_lon, at_lat):
        pl.semaphore_signal(barrier, inc=1, device_id={"lon": at_lon, "lat": at_lat}, device_id_type=MESH)

    greet(east, lat)
    greet(west, lat)
    greet(up_lon, up_lat)
    pl.when(east_other)(lambda: greet(up_east, up_lat))
    pl.when(west_other)(lambda: greet(up_west, up_lat))

    @pl.when(has_south)
    def _():
        greet(lon, down_lat)
        greet(east, down_lat)
        greet(west, down_lat)

    for at in first_sum + second_sum:
        greet(*at)

    @pl.when(hub)
    def _():
        for f in range(1, n_lon):
            greet(bits(lon, f), lat)

        def band(b, carry):
            for f in range(n_lon):
                greet(bits(lon, f), jnp.bitwise_xor(lat, n_lat - b))
            return carry

        lax.fori_loop(1, n_lat, band, 0)

    greetings = n_lon + n_lat + 6 - jnp.where(east_self, 1, 0) - jnp.where(west_self, 1, 0) - jnp.where(bottom, 3, 0) + len(hubs) - jnp.where(hub, 1, 0)

    def remote(src, dst, send, recv, at_lon, at_lat):
        return pltpu.make_async_remote_copy(
            src_ref=src, dst_ref=dst, send_sem=send, recv_sem=recv,
            device_id={"lon": at_lon, "lat": at_lat}, device_id_type=MESH,
        )

    @pl.when(bottom)
    def _():
        got[0:3] = jnp.zeros((3, 16, WIDE), BF16)

    selections(spread_ref, offsets_ref, expand_ref)
    acc[...] = jnp.zeros(acc.shape, F32)
    for copy in weights_in[:3]:
        copy.wait()
    folded = fold_weights(coef_ref, edge_ref, head_ref, spread_ref, offsets_ref)
    for copy in weights_in[3:]:
        copy.wait()
    feat_in(0).wait()
    band_weights(folded, expand_ref, wt, top)


    def expanded(k, out):
        for at in range(0, GROUP, 2):
            x = feat[pl.ds((k // L) * GROUP + at, 2), lax.rem(k, L)].astype(F32).reshape(2 * ROWS, COLS)
            for j, value in enumerate(basis(x)):
                row = (at * J + 2 * j) * ROWS
                out[row : row + 2 * ROWS, :] = value.astype(BF16)

    def contracted(k, bases):
        acc[lax.rem(k, L), :, 0:COLS] += dot(wt[k // L], bases[...])

    expanded(0, bases_a)
    for k in range(1, GROUPS):
        feat_in(k).wait()

    def step(i, carry):
        expanded(2 * i + 1, bases_b)
        contracted(2 * i, bases_a)
        expanded(jnp.minimum(2 * i + 2, L * GROUPS - 1), bases_a)
        contracted(2 * i + 1, bases_b)
        return carry

    lax.fori_loop(0, GROUPS * L // 2, step, 0)

    @pl.when(bottom)
    def _():
        q = iota((1, CHUNK), 1)
        j = lax.shift_right_logical(q - lax.shift_right_logical(q * 13108, 21) * (2 * ROWS * J), 4)
        outside = jnp.zeros((8, CHUNK), F32)
        for group in range(GROUPS):
            outside = outside + wt[group, 48:64, :].astype(F32)[8:16]
        outside = jnp.sum(jnp.where(j < NB, outside, 0.0), axis=1, keepdims=True) * (2.0**LIFT)
        for level in range(L):
            for c in range(2):
                acc[level, 16 + 8 * c : 17 + 8 * c, 0:COLS] += outside[c : c + 1] + outside[c + 2 : c + 3] + outside[c + 4 : c + 5]

    lane, low = iota((ROWS, 128), 1), iota((ROWS, 128), 1) < 64
    low2 = iota((16, 128), 1) < 64
    row = iota((ROWS, WIDE), 0)
    zero = jnp.zeros((ROWS, WIDE), F32)

    def joined(parts):
        return jnp.concatenate(parts, axis=1)

    def stacked(parts):
        return jnp.concatenate(parts, axis=0)

    def lanes(x, by):
        return pltpu.roll(x, by % WIDE, 1)

    def rows(x, by):
        return pltpu.roll(x, by % 16, 0)

    def placed(entries):
        out = zero
        for at, value in entries:
            out = jnp.where(row == at, value, out)
        return out

    own, above, below = [], [], []
    for level in range(L):
        a = acc[level] * (2.0**-LIFT)
        own.append(a[16:32] + lanes(a[0:16], 1) + lanes(a[32:48], -1))
        outer = a[48:64]
        before, after = lanes(outer, 1), lanes(outer, -1)
        below.append(outer[2:4] + before[0:2] + after[4:6])
        above.append(outer[10:12] + before[8:10] + after[12:14])
    total, total_up, total_down = own[0] + own[1], above[0] + above[1], below[0] + below[1]
    share = [stacked([total[8 * c : 8 * c + 8], placed([(0, total_up[c : c + 1]), (7, total_down[c : c + 1])])]) for c in range(2)]
    upper = own[1]

    ocean = joined([land_ref[...].astype(F32), zero[:, 0:128]])
    shift = joined([shift_ref[...], zero[:, 0:128]])

    def both(r):
        return [total[r : r + 1], total[8 + r : 9 + r]]

    none = [zero[0:1]]
    edge_n = stacked(
        [total_up] + both(7) + both(6) + both(5) + [above[1], ocean[7:8], ocean[6:7], ocean[5:6], shift[7:8]] + none * 2
    )
    edge_s = stacked(
        [total_down] + both(0) + both(1) + none * 2 + [below[1], ocean[0:1], ocean[1:2]] + none + [shift[0:1]] + none * 2
    )
    edge_e = stacked(share + [upper, ocean, shift])

    def eastern(x):
        return jnp.where(iota((x.shape[0], 128), 1) < 64, x[:, COLS:], x[:, COLS - 128 : COLS])

    def western(x):
        return jnp.where(iota((x.shape[0], 128), 1) < 64, x[:, 0:128], x[:, COLS:])

    corner = pl.ds(WIDE, 128), pl.ds(WIDE + 128, 128)
    for edge, ref in ((edge_n, north), (edge_s, south)):
        ref[...] = joined([edge, eastern(edge), western(edge)]).astype(BF16)
    to_east[...] = eastern(edge_e).astype(BF16)
    to_west[...] = western(edge_e).astype(BF16)

    whole, part = pl.ds(0, WIDE), pl.ds(0, 128)
    upward = jnp.where(top, 3, 0)
    sends = [
        (east_other, remote(north.at[:, corner[0]], got.at[upward + 1, :, part], send.at[1], recv.at[upward + 1], up_east, up_lat)),
        (west_other, remote(north.at[:, corner[1]], got.at[upward + 2, :, part], send.at[2], recv.at[upward + 2], up_west, up_lat)),
        (has_south, remote(south.at[:, corner[0]], got.at[4, :, part], send.at[4], recv.at[4], east, down_lat)),
        (has_south, remote(south.at[:, corner[1]], got.at[5, :, part], send.at[5], recv.at[5], west, down_lat)),
        (None, remote(north.at[:, whole], got.at[upward], send.at[0], recv.at[upward], up_lon, up_lat)),
        (has_south, remote(south.at[:, whole], got.at[3], send.at[3], recv.at[3], lon, down_lat)),
        (None, remote(to_east, side.at[0], send.at[6], recv.at[6], east, lat)),
        (None, remote(to_west, side.at[1], send.at[7], recv.at[7], west, lat)),
    ]

    def arrival(src, dst, k):
        return remote(src, dst, send.at[0], recv.at[k], east, lat)

    corner_n = north.at[:, corner[0]]
    arrivals = [
        (None, arrival(to_east, side.at[0], 6)),
        (None, arrival(to_west, side.at[1], 7)),
        (has_south, arrival(north.at[:, whole], got.at[0], 0)),
        (has_south, arrival(corner_n, got.at[1, :, part], 1)),
        (has_south, arrival(corner_n, got.at[2, :, part], 2)),
        (None, arrival(north.at[:, whole], got.at[3], 3)),
        (east_other, arrival(corner_n, got.at[4, :, part], 4)),
        (west_other, arrival(corner_n, got.at[5, :, part], 5)),
    ]

    def each(entries, act):
        for cond, copy in entries:
            if cond is None:
                act(copy)
            else:
                pl.when(cond)(functools.partial(act, copy))

    pl.semaphore_wait(barrier, greetings)
    each(sends, lambda copy: copy.start())

    @pl.when(east_self)
    def _():
        got[4, :, 0:128] = north[:, WIDE : WIDE + 128]

    @pl.when(west_self)
    def _():
        got[5, :, 0:128] = north[:, WIDE + 128 :]

    each(arrivals, lambda copy: copy.wait_recv())

    def arrived(k):
        parts = [got[k, :, 128 * t : 128 * t + 128].astype(F32) for t in range(5)]
        w, e = got[k + 1, :, 0:128].astype(F32), got[k + 2, :, 0:128].astype(F32)
        return [
            parts[0] + jnp.where(low2, w, 0.0), parts[1], parts[2],
            parts[3] + jnp.where(low2, 0.0, e), parts[4] + jnp.where(low2, e, w),
        ]

    backwards = 127 - lane

    def turned(x):
        return stacked([jnp.take_along_axis(x[r : r + 8], backwards, axis=1) for r in (0, 8)])

    s_rows = joined(arrived(0))
    n_parts = arrived(3)
    flipped = [turned(x) for x in n_parts]
    flipped = flipped[3::-1] + flipped[4:]
    n_rows = joined([jnp.where(top, f, n) for f, n in zip(flipped, n_parts)])
    from_west, from_east = side[0].astype(F32), side[1].astype(F32)

    def with_sides(x, at):
        count = x.shape[0]
        w, e = from_west[at : at + count], from_east[at : at + count]
        near = iota((count, 128), 1) < 64
        return joined([
            x[:, 0:128] + jnp.where(near, w, 0.0),
            x[:, 128 : COLS - 128],
            x[:, COLS - 128 : COLS] + jnp.where(near, 0.0, e),
            x[:, COLS:] + jnp.where(near, e, w),
        ])

    def one(x, k):
        return x[k : k + 1]

    m = stacked([
        with_sides(ocean, 48),
        placed([(r, one(n_rows, 10 + r)) for r in range(3)] + [(7 - r, one(s_rows, 10 + r)) for r in range(3)]),
    ])
    s = stacked([with_sides(shift, 56), placed([(0, one(n_rows, 13)), (7, one(s_rows, 13))])])
    eastward, northward = [
        m * (
            with_sides(share[c], 16 * c)
            + stacked([
                placed([(0, one(s_rows, c)), (7, one(n_rows, c))]),
                placed([(r, one(n_rows, 2 + 2 * r + c)) for r in range(3)] + [(7 - r, one(s_rows, 2 + 2 * r + c)) for r in range(3)]),
            ])
        )
        for c in range(2)
    ]
    r = m * (eastward - lanes(eastward, 1) + northward - rows(northward, 1))
    beyond = m * (eastward - lanes(eastward, -1) + northward - rows(northward, -1))
    r = stacked([r[0:8], jnp.where(top & (row < 2), beyond[8:16], r[8:16])])

    def operate(v):
        return m * ((4.0 + s) * v - (lanes(v, 1) + lanes(v, -1) + rows(v, 1) + rows(v, -1)))

    q1 = operate(r)
    q2 = operate(q1)[0:8, 0:COLS]
    r, q1 = r[0:8, 0:COLS], q1[0:8, 0:COLS]

    def summed(x):
        x = x[:, 0:128] + x[:, 128:256] + x[:, 256:384] + x[:, 384:512]
        return jnp.sum(x, axis=0, keepdims=True)

    dots = [summed(r * r), summed(r * q1), summed(q1 * q1), summed(r * q2), summed(q1 * q2)]

    def row_to(ref, stage, here, at):
        remote(ref.at[here], ref.at[here], send_sum.at[stage], recv_sum.at[stage], *at).start()

    def rows_of(ref, stage, number):
        several = ref.at[pl.ds(0, number)]
        return remote(several, several, send_sum.at[stage], recv_sum.at[stage], east, lat)

    dots = jnp.sum(stacked(dots + [jnp.zeros((3, 128), F32)]), axis=1, keepdims=True)
    dots = jnp.sum(jnp.where(lane == iota((ROWS, 128), 0), dots, 0.0), axis=0, keepdims=True)
    direct_row = sums_d.at[pl.ds(direct_here, 1)]
    direct_row[...] = dots
    sums_a[first_here] = dots
    for at in hubs:
        other = (lon != at[0]) | (lat != at[1])
        pl.when(other)(remote(direct_row, direct_row, send_sum.at[2], recv_sum.at[2], *at).start)
    for at in first_sum:
        row_to(sums_a, 0, first_here, at)

    @pl.when(lat >= 0)
    def _():
        second = with_sides(upper, 32)
        for c in range(2):
            one_level = second[8 * c : 8 * c + 8] + placed([(0, one(s_rows, 8 + c)), (7, one(n_rows, 8 + c))])
            one_level = ocean[:, 0:COLS] * one_level[:, 0:COLS]
            whole = (eastward, northward)[c][0:8, 0:COLS]
            tend_ref[c, 0] = (whole - one_level).astype(BF16)
            tend_ref[c, 1] = one_level.astype(BF16)
        for k, value in enumerate((r, q1, q2)):
            fields_ref[8 * k : 8 * k + 8, :] = value

    each(sends, lambda copy: copy.wait_send())

    rows_of(sums_a, 0, n_lat - 1).wait_recv()
    sums_b[second_here] = jnp.sum(sums_a[...], axis=0)
    for at in second_sum:
        pl.when(jnp.logical_not(is_hub(*at)))(functools.partial(row_to, sums_b, 1, second_here, at))

    @pl.when(hub)
    def _():
        rows_of(sums_d, 2, n_lon * n_lat - 1).wait_recv()
        sums_ref[...] = jnp.sum(sums_d[...], axis=0, keepdims=True)
        rows_of(sums_d, 2, len(hubs) - 1).wait_send()

    @pl.when(jnp.logical_not(hub))
    def _():
        rows_of(sums_b, 1, n_lon - 1).wait_recv()
        sums_ref[...] = jnp.sum(sums_b[...], axis=0)
        rows_of(sums_d, 2, len(hubs)).wait_send()

    for k in range(most + 1):
        pl.when(beside == k)(rows_of(sums_b, 1, n_lon - 1 - k).wait_send)
    rows_of(sums_a, 0, n_lat - 1).wait_send()


def finish(fields_ref, sums_ref, tend_in, tend_ref, surf_ref, res_ref):
    r, q1, q2 = fields_ref[0:8, :], fields_ref[8:16, :], fields_ref[16:24, :]
    rr, rq, qq, rq2, qq2 = [sums_ref[0:1, k : k + 1] for k in range(5)]
    a1 = rr / rq
    new = rr - 2.0 * a1 * rq + a1 * a1 * qq
    lead = 1.0 + new / rr
    a2 = new / (lead * lead * rq - lead * a1 * (rq2 + qq) + a1 * a1 * qq2)
    surf_ref[...] = a1 * r + a2 * (lead * r - a1 * q1)
    res_ref[...] = r - a1 * q1 - a2 * (lead * q1 - a1 * q2)
    tend_ref[...] = tend_in[...]


def body(features, spline_coef, edge_mask, head_weight, land_mask, shift_coef):
    n_lon, n_lat = lax.axis_size("lon"), lax.axis_size("lat")
    vmem = pl.BlockSpec(memory_space=pltpu.VMEM)
    dma = pltpu.SemaphoreType.DMA
    tend_shape = jax.ShapeDtypeStruct((2, L, ROWS, COLS), BF16)
    field_shape = jax.ShapeDtypeStruct((ROWS, COLS), F32)
    scratch = [
        pltpu.VMEM((C, L, ROWS, COLS), BF16),
        pltpu.VMEM((9 * C, C * J), BF16),
        pltpu.VMEM((C, C), jnp.int32),
        pltpu.VMEM((2, C), BF16),
        pltpu.VMEM((ROWS, COLS), jnp.int32),
        pltpu.VMEM((ROWS, COLS), F32),
        pltpu.VMEM((C, C * J), BF16),
        pltpu.VMEM((C, 9 * C), BF16),
        pltpu.VMEM((GROUP * J, CHUNK), BF16),
        pltpu.VMEM((GROUPS, 64, CHUNK), BF16),
        pltpu.VMEM((CHUNK, COLS), BF16),
        pltpu.VMEM((CHUNK, COLS), BF16),
        pltpu.VMEM((L, 64, WIDE), F32),
        pltpu.VMEM((16, WIDE + 256), BF16),
        pltpu.VMEM((16, WIDE + 256), BF16),
        pltpu.VMEM((64, 128), BF16),
        pltpu.VMEM((64, 128), BF16),
        pltpu.VMEM((6, 16, WIDE), BF16),
        pltpu.VMEM((2, 64, 128), BF16),
        pltpu.VMEM((n_lat, 1, 128), F32),
        pltpu.VMEM((n_lon, 1, 128), F32),
        pltpu.VMEM((n_lon * n_lat, 128), F32),
        dma((GROUPS,)), dma((5,)), dma((8,)), dma((8,)), dma((3,)), dma((3,)),
    ]
    tendency, fields, sums = pl.pallas_call(
        functools.partial(kernel, n_lon, n_lat),
        out_shape=(
            pltpu.VMEM((2, L, ROWS, COLS), BF16),
            pltpu.VMEM((3 * ROWS, COLS), F32),
            pltpu.VMEM((1, 128), F32),
        ),
        in_specs=[pl.BlockSpec(memory_space=pl.ANY)] * 6,
        out_specs=(vmem, vmem, vmem),
        scratch_shapes=scratch,
        compiler_params=pltpu.CompilerParams(collective_id=0, has_side_effects=True),
        name="closure_and_sums",
    )(features, spline_coef, edge_mask, head_weight, land_mask, shift_coef)
    return pl.pallas_call(
        finish,
        out_shape=(tend_shape, field_shape, field_shape),
        in_specs=[vmem] * 3,
        out_specs=(vmem, vmem, vmem),
        compiler_params=pltpu.CompilerParams(vmem_limit_bytes=4 * 1024 * 1024),
        name="finish",
    )(fields, sums, tendency)


def solution(mesh):
    in_specs = (P(None, None, "lat", "lon"), P(), P(), P(), P("lat", "lon"), P("lat", "lon"))
    out_specs = (P(None, None, "lat", "lon"), P("lat", "lon"), P("lat", "lon"))
    return jax.shard_map(body, mesh=mesh, in_specs=in_specs, out_specs=out_specs, check_vma=False)
```

```python
import functools
import math

import jax
import jax.numpy as jnp
from jax import lax
from jax.experimental import pallas as pl
from jax.experimental.pallas import tpu as pltpu
from jax.sharding import PartitionSpec as P

C = 48
NB = 9
J = NB + 1
L = 2
ROWS = 8
COLS = 512
WIDE = COLS + 128
F32 = jnp.float32
BF16 = jnp.bfloat16
MESH = pl.DeviceIdType.MESH
LOG2E = math.log2(math.e)
LIFT = 82
GROUP = 16
GROUPS = C // GROUP
CHUNK = GROUP * ROWS * J


def iota(shape, axis):
    return lax.broadcasted_iota(jnp.int32, shape, axis)


def dot(a, b):
    return jnp.dot(a, b, preferred_element_type=F32)


def ones_where(cond):
    return jnp.where(cond, 1.0, 0.0).astype(BF16)


def selections(spread_ref, offsets_ref, expand_ref):
    channel, lane = iota((C, C * J), 0), iota((C, C * J), 1)
    spread_ref[...] = ones_where((lane >= channel * J) & (lane < channel * J + J))
    o, q = iota((C, 9 * C), 0), iota((C, 9 * C), 1)
    offsets_ref[...] = ones_where(q - lax.shift_right_logical(q * 1366, 16) * C == o)
    q = iota((1, CHUNK), 1)
    strip = lax.shift_right_logical(q * 13108, 21)
    source = (2 * strip + (lax.shift_right_logical(q, 3) & 1)) * J + lax.shift_right_logical(q - strip * (2 * ROWS * J), 4)
    expand_ref[...] = ones_where(iota((GROUP * J, CHUNK), 0) == source)


def fold_weights(coef_ref, edge_ref, head_ref, spread_ref, offsets_ref):
    keep = dot(jnp.where(edge_ref[...] > 0, 1.0, 0.0).astype(BF16), spread_ref[...]).astype(BF16)
    head = dot(head_ref[...], offsets_ref[...])
    r, q = iota((24, 9 * C), 0), iota((24, 9 * C), 1)
    offset = lax.shift_right_logical(q * 1366, 16)
    head = jnp.where((r & 1) == 0, head[0:1], head[1:2])
    head = jnp.where(lax.shift_right_logical(r, 1) == offset, head, 0.0).astype(BF16)
    masked = [coef_ref[C * k : C * k + C, :] * keep for k in range(9)]
    folded = dot(head, jnp.concatenate(masked, axis=0))
    lane = iota((1, C * J), 1)
    j = lane - J * lax.shift_right_logical(lane * 6554, 16)
    off = jnp.abs(j - NB // 2).astype(F32)
    scale = jnp.where(j == NB, 2.0**LIFT, jnp.exp(-off * off))
    folded = folded * scale
    return folded


def band_weights(folded, expand_ref, wt, top):
    y_out = iota((ROWS, CHUNK), 0)
    y_in = iota((ROWS, CHUNK), 1) & 7
    first_row, last_row = y_in[0:6] == 0, y_in[0:6] == 7
    pad = jnp.zeros((2, CHUNK), F32)
    for group in range(GROUPS):
        g = dot(folded[:, GROUP * J * group : GROUP * J * (group + 1)].astype(BF16), expand_ref[...])
        tiles = []
        for k in range(6):
            tile = jnp.where(y_in == y_out - 1, g[k : k + 1], 0.0)
            tile = jnp.where(y_in == y_out, g[6 + k : 7 + k], tile)
            tiles.append(jnp.where(y_in == y_out + 1, g[12 + k : 13 + k], tile))
        mirrored = jnp.concatenate([g[16:18], g[14:16], g[12:14]], axis=0)
        above = jnp.where(top, mirrored, g[0:6])
        tiles += [jnp.where(first_row, g[12:18], 0.0), pad, jnp.where(last_row, above, 0.0), pad]
        wt[group] = jnp.concatenate(tiles, axis=0).astype(BF16)


def basis(x):
    half = x * 0.5
    middle = jnp.exp2((half * half) * (-16.0 * LOG2E) + float(LIFT))
    up = jnp.exp2(half * (8.0 * LOG2E))
    down = jnp.exp2(half * (-8.0 * LOG2E))
    silu = half + half * jnp.tanh(half)
    left, right = [middle], [middle]
    for _ in range(NB // 2):
        left.append(left[-1] * down)
        right.append(right[-1] * up)
    return left[:0:-1] + right + [silu]


def bits(value, flips):
    return jnp.bitwise_xor(value, flips) if flips else value


def kernel(
    n_lon, n_lat,
    feat_hbm, coef_hbm, edge_hbm, head_hbm, land_hbm, shift_hbm,
    tend_ref, fields_ref, sums_ref,
    feat, coef_ref, edge_ref, head_ref, land_ref, shift_ref, spread_ref, offsets_ref, expand_ref, wt, bases_a, bases_b, acc,
    north, south, to_east, to_west, got, side, sums_a, sums_b, sums_d,
    feat_sem, weight_sem, send, recv, send_sum, recv_sum,
):
    weights_in = [
        pltpu.make_async_copy(src, dst, weight_sem.at[k])
        for k, (src, dst) in enumerate(
            [(edge_hbm, edge_ref), (head_hbm, head_ref), (coef_hbm, coef_ref), (land_hbm, land_ref), (shift_hbm, shift_ref)]
        )
    ]

    def feat_in(k):
        part = pl.ds(k * GROUP, GROUP)
        return pltpu.make_async_copy(feat_hbm.at[part], feat.at[part], feat_sem.at[k])

    for copy in weights_in + [feat_in(k) for k in range(GROUPS)]:
        copy.start()

    lon, lat = lax.axis_index("lon"), lax.axis_index("lat")
    top, bottom = lat == n_lat - 1, lat == 0
    east = jnp.where(lon == n_lon - 1, 0, lon + 1)
    west = jnp.where(lon == 0, n_lon - 1, lon - 1)
    up_lat = jnp.where(top, lat, lat + 1)
    up_lon = jnp.where(top, n_lon - 1 - lon, lon)
    up_east = jnp.where(top, n_lon - 1 - east, east)
    up_west = jnp.where(top, n_lon - 1 - west, west)
    down_lat = jnp.where(bottom, lat, lat - 1)
    east_self, west_self = top & (up_east == lon), top & (up_west == lon)
    east_other, west_other = jnp.logical_not(east_self), jnp.logical_not(west_self)
    has_south = jnp.logical_not(bottom)

    half = n_lon // 2
    ring = {0: 0, 1: 1, 2: 2, 3: 3, 4: 4, 5: 3, 6: 2, 7: 2}

    def far_first(count, hops):
        return sorted(range(1, count), key=lambda d: -hops(d))

    first_order = far_first(n_lat, lambda d: ring.get(d // 2, 0))
    first_sum = [(bits(lon, d % 2), bits(lat, d - d % 2)) for d in first_order]
    first_here = lat - lax.rem(lat, 2) + lax.rem(lon, 2)
    second_order = far_first(n_lon, lambda d: (0, 1, 2, 1)[d % 4] + (0, 2, 1, 1)[d // 4 % 4])
    second_sum = [(bits(lon, 2 * (d % half)), bits(lat, d // half)) for d in second_order]
    second_here = lon // 2 + half * lax.rem(lat, 2)
    hub_lon, hub_lat = max(2, n_lon // 4), max(2, n_lat // 4)
    hubs = [(a, b) for b in range(hub_lat) for a in range(hub_lon)]

    def is_hub(at_lon, at_lat):
        return (at_lon < hub_lon) & (at_lat < hub_lat)

    hub, hub_plane = is_hub(lon, lat), lat < hub_lat
    direct_here = lon * n_lat + lat


    barrier = pltpu.get_barrier_semaphore()

    def greet(at_lon, at_lat):
        pl.semaphore_signal(barrier, inc=1, device_id={"lon": at_lon, "lat": at_lat}, device_id_type=MESH)

    greet(east, lat)
    greet(west, lat)
    greet(up_lon, up_lat)
    pl.when(east_other)(lambda: greet(up_east, up_lat))
    pl.when(west_other)(lambda: greet(up_west, up_lat))

    @pl.when(has_south)
    def _():
        greet(lon, down_lat)
        greet(east, down_lat)
        greet(west, down_lat)

    for at in first_sum + second_sum:
        greet(*at)

    @pl.when(hub)
    def _():
        for f in range(1, n_lon):
            greet(bits(lon, f), lat)

        def band(b, carry):
            for f in range(n_lon):
                greet(bits(lon, f), jnp.bitwise_xor(lat, b))
            return carry

        lax.fori_loop(1, n_lat, band, 0)

    greetings = n_lon + n_lat + 6 - jnp.where(east_self, 1, 0) - jnp.where(west_self, 1, 0) - jnp.where(bottom, 3, 0) + len(hubs) - jnp.where(hub, 1, 0)

    def remote(src, dst, send, recv, at_lon, at_lat):
        return pltpu.make_async_remote_copy(
            src_ref=src, dst_ref=dst, send_sem=send, recv_sem=recv,
            device_id={"lon": at_lon, "lat": at_lat}, device_id_type=MESH,
        )

    @pl.when(bottom)
    def _():
        got[0:3] = jnp.zeros((3, 16, WIDE), BF16)

    selections(spread_ref, offsets_ref, expand_ref)
    acc[...] = jnp.zeros(acc.shape, F32)
    for copy in weights_in[:3]:
        copy.wait()
    folded = fold_weights(coef_ref, edge_ref, head_ref, spread_ref, offsets_ref)
    for copy in weights_in[3:]:
        copy.wait()
    feat_in(0).wait()
    band_weights(folded, expand_ref, wt, top)


    def expanded(k, out):
        for at in range(0, GROUP, 2):
            x = feat[pl.ds((k // L) * GROUP + at, 2), lax.rem(k, L)].astype(F32).reshape(2 * ROWS, COLS)
            for j, value in enumerate(basis(x)):
                row = (at * J + 2 * j) * ROWS
                out[row : row + 2 * ROWS, :] = value.astype(BF16)

    def contracted(k, bases):
        acc[lax.rem(k, L), :, 0:COLS] += dot(wt[k // L], bases[...])

    expanded(0, bases_a)
    for k in range(1, GROUPS):
        feat_in(k).wait()

    def step(i, carry):
        expanded(2 * i + 1, bases_b)
        contracted(2 * i, bases_a)
        expanded(jnp.minimum(2 * i + 2, L * GROUPS - 1), bases_a)
        contracted(2 * i + 1, bases_b)
        return carry

    lax.fori_loop(0, GROUPS * L // 2, step, 0)

    @pl.when(bottom)
    def _():
        q = iota((1, CHUNK), 1)
        j = lax.shift_right_logical(q - lax.shift_right_logical(q * 13108, 21) * (2 * ROWS * J), 4)
        outside = jnp.zeros((8, CHUNK), F32)
        for group in range(GROUPS):
            outside = outside + wt[group, 48:64, :].astype(F32)[8:16]
        outside = jnp.sum(jnp.where(j < NB, outside, 0.0), axis=1, keepdims=True) * (2.0**LIFT)
        for level in range(L):
            for c in range(2):
                acc[level, 16 + 8 * c : 17 + 8 * c, 0:COLS] += outside[c : c + 1] + outside[c + 2 : c + 3] + outside[c + 4 : c + 5]

    pl.semaphore_wait(barrier, greetings)

    lane, low = iota((ROWS, 128), 1), iota((ROWS, 128), 1) < 64
    low2 = iota((16, 128), 1) < 64
    row = iota((ROWS, WIDE), 0)
    zero = jnp.zeros((ROWS, WIDE), F32)

    def joined(parts):
        return jnp.concatenate(parts, axis=1)

    def stacked(parts):
        return jnp.concatenate(parts, axis=0)

    def lanes(x, by):
        return pltpu.roll(x, by % WIDE, 1)

    def rows(x, by):
        return pltpu.roll(x, by % 16, 0)

    def placed(entries):
        out = zero
        for at, value in entries:
            out = jnp.where(row == at, value, out)
        return out

    own, above, below = [], [], []
    for level in range(L):
        a = acc[level] * (2.0**-LIFT)
        own.append(a[16:32] + lanes(a[0:16], 1) + lanes(a[32:48], -1))
        outer = a[48:64]
        before, after = lanes(outer, 1), lanes(outer, -1)
        below.append(outer[2:4] + before[0:2] + after[4:6])
        above.append(outer[10:12] + before[8:10] + after[12:14])
    total, total_up, total_down = own[0] + own[1], above[0] + above[1], below[0] + below[1]
    share = [stacked([total[8 * c : 8 * c + 8], placed([(0, total_up[c : c + 1]), (7, total_down[c : c + 1])])]) for c in range(2)]
    upper = own[1]

    ocean = joined([land_ref[...].astype(F32), zero[:, 0:128]])
    shift = joined([shift_ref[...], zero[:, 0:128]])

    def both(r):
        return [total[r : r + 1], total[8 + r : 9 + r]]

    none = [zero[0:1]]
    edge_n = stacked(
        [total_up] + both(7) + both(6) + both(5) + [above[1], ocean[7:8], ocean[6:7], ocean[5:6], shift[7:8]] + none * 2
    )
    edge_s = stacked(
        [total_down] + both(0) + both(1) + none * 2 + [below[1], ocean[0:1], ocean[1:2]] + none + [shift[0:1]] + none * 2
    )

    def eastern(x):
        return jnp.where(iota((x.shape[0], 128), 1) < 64, x[:, COLS:], x[:, COLS - 128 : COLS])

    def western(x):
        return jnp.where(iota((x.shape[0], 128), 1) < 64, x[:, 0:128], x[:, COLS:])

    corner = pl.ds(WIDE, 128), pl.ds(WIDE + 128, 128)
    for edge, ref in ((edge_n, north), (edge_s, south)):
        ref[...] = joined([edge, eastern(edge), western(edge)]).astype(BF16)

    whole, part = pl.ds(0, WIDE), pl.ds(0, 128)
    upward = jnp.where(top, 3, 0)
    sends = [
        (east_other, remote(north.at[:, corner[0]], got.at[upward + 1, :, part], send.at[1], recv.at[upward + 1], up_east, up_lat)),
        (west_other, remote(north.at[:, corner[1]], got.at[upward + 2, :, part], send.at[2], recv.at[upward + 2], up_west, up_lat)),
        (has_south, remote(south.at[:, corner[0]], got.at[4, :, part], send.at[4], recv.at[4], east, down_lat)),
        (has_south, remote(south.at[:, corner[1]], got.at[5, :, part], send.at[5], recv.at[5], west, down_lat)),
        (None, remote(north.at[:, whole], got.at[upward], send.at[0], recv.at[upward], up_lon, up_lat)),
        (has_south, remote(south.at[:, whole], got.at[3], send.at[3], recv.at[3], lon, down_lat)),
        (None, remote(to_east, side.at[0], send.at[6], recv.at[6], east, lat)),
        (None, remote(to_west, side.at[1], send.at[7], recv.at[7], west, lat)),
    ]

    def arrival(src, dst, k):
        return remote(src, dst, send.at[0], recv.at[k], east, lat)

    corner_n = north.at[:, corner[0]]
    arrivals = [
        (None, arrival(to_east, side.at[0], 6)),
        (None, arrival(to_west, side.at[1], 7)),
        (has_south, arrival(north.at[:, whole], got.at[0], 0)),
        (has_south, arrival(corner_n, got.at[1, :, part], 1)),
        (has_south, arrival(corner_n, got.at[2, :, part], 2)),
        (None, arrival(north.at[:, whole], got.at[3], 3)),
        (east_other, arrival(corner_n, got.at[4, :, part], 4)),
        (west_other, arrival(corner_n, got.at[5, :, part], 5)),
    ]

    def each(entries, act):
        for cond, copy in entries:
            if cond is None:
                act(copy)
            else:
                pl.when(cond)(functools.partial(act, copy))

    each(sends[:6], lambda copy: copy.start())
    edge_e = stacked(share + [upper, ocean, shift])
    to_east[...] = eastern(edge_e).astype(BF16)
    to_west[...] = western(edge_e).astype(BF16)
    each(sends[6:], lambda copy: copy.start())

    @pl.when(east_self)
    def _():
        got[4, :, 0:128] = north[:, WIDE : WIDE + 128]

    @pl.when(west_self)
    def _():
        got[5, :, 0:128] = north[:, WIDE + 128 :]

    each(arrivals, lambda copy: copy.wait_recv())

    def arrived(k):
        parts = [got[k, :, 128 * t : 128 * t + 128].astype(F32) for t in range(5)]
        w, e = got[k + 1, :, 0:128].astype(F32), got[k + 2, :, 0:128].astype(F32)
        return [
            parts[0] + jnp.where(low2, w, 0.0), parts[1], parts[2],
            parts[3] + jnp.where(low2, 0.0, e), parts[4] + jnp.where(low2, e, w),
        ]

    backwards = 127 - lane

    def turned(x):
        return stacked([jnp.take_along_axis(x[r : r + 8], backwards, axis=1) for r in (0, 8)])

    s_rows = joined(arrived(0))
    n_parts = arrived(3)
    flipped = [turned(x) for x in n_parts]
    flipped = flipped[3::-1] + flipped[4:]
    n_rows = joined([jnp.where(top, f, n) for f, n in zip(flipped, n_parts)])
    from_west, from_east = side[0].astype(F32), side[1].astype(F32)

    def with_sides(x, at):
        count = x.shape[0]
        w, e = from_west[at : at + count], from_east[at : at + count]
        near = iota((count, 128), 1) < 64
        return joined([
            x[:, 0:128] + jnp.where(near, w, 0.0),
            x[:, 128 : COLS - 128],
            x[:, COLS - 128 : COLS] + jnp.where(near, 0.0, e),
            x[:, COLS:] + jnp.where(near, e, w),
        ])

    def one(x, k):
        return x[k : k + 1]

    m = stacked([
        with_sides(ocean, 48),
        placed([(r, one(n_rows, 10 + r)) for r in range(3)] + [(7 - r, one(s_rows, 10 + r)) for r in range(3)]),
    ])
    s = stacked([with_sides(shift, 56), placed([(0, one(n_rows, 13)), (7, one(s_rows, 13))])])
    eastward, northward = [
        m * (
            with_sides(share[c], 16 * c)
            + stacked([
                placed([(0, one(s_rows, c)), (7, one(n_rows, c))]),
                placed([(r, one(n_rows, 2 + 2 * r + c)) for r in range(3)] + [(7 - r, one(s_rows, 2 + 2 * r + c)) for r in range(3)]),
            ])
        )
        for c in range(2)
    ]
    r = m * (eastward - lanes(eastward, 1) + northward - rows(northward, 1))
    beyond = m * (eastward - lanes(eastward, -1) + northward - rows(northward, -1))
    r = stacked([r[0:8], jnp.where(top & (row < 2), beyond[8:16], r[8:16])])

    def operate(v):
        return m * ((4.0 + s) * v - (lanes(v, 1) + lanes(v, -1) + rows(v, 1) + rows(v, -1)))

    q1 = operate(r)
    q2 = operate(q1)[0:8, 0:COLS]
    r, q1 = r[0:8, 0:COLS], q1[0:8, 0:COLS]

    dots = zero[:, 0:128]
    for k, x in enumerate((r * r, r * q1, q1 * q1, r * q2, q1 * q2)):
        x = x[:, 0:128] + x[:, 128:256] + x[:, 256:384] + x[:, 384:512]
        dots = jnp.where(lane == k, jnp.sum(x, axis=1, keepdims=True), dots)
    dots = jnp.sum(dots, axis=0, keepdims=True)

    def row_to(ref, stage, here, at):
        remote(ref.at[here], ref.at[here], send_sum.at[stage], recv_sum.at[stage], *at).start()

    def rows_of(ref, stage, number):
        several = ref.at[pl.ds(0, number)]
        return remote(several, several, send_sum.at[stage], recv_sum.at[stage], east, lat)

    direct_row = sums_d.at[pl.ds(direct_here, 1)]
    direct_row[...] = dots
    sums_a[first_here] = dots
    for at in hubs:
        other = (lon != at[0]) | (lat != at[1])
        pl.when(other)(remote(direct_row, direct_row, send_sum.at[2], recv_sum.at[2], *at).start)
    for at in first_sum:
        row_to(sums_a, 0, first_here, at)

    @pl.when(lat >= 0)
    def _():
        second = with_sides(upper, 32)
        for c in range(2):
            one_level = second[8 * c : 8 * c + 8] + placed([(0, one(s_rows, 8 + c)), (7, one(n_rows, 8 + c))])
            one_level = ocean[:, 0:COLS] * one_level[:, 0:COLS]
            whole = (eastward, northward)[c][0:8, 0:COLS]
            tend_ref[c, 0] = (whole - one_level).astype(BF16)
            tend_ref[c, 1] = one_level.astype(BF16)
        for k, value in enumerate((r, q1, q2)):
            fields_ref[8 * k : 8 * k + 8, :] = value

    each(sends, lambda copy: copy.wait_send())

    rows_of(sums_a, 0, n_lat - 1).wait_recv()
    sums_b[second_here] = jnp.sum(sums_a[...], axis=0)
    for at in second_sum:
        pl.when(jnp.logical_not(is_hub(*at)))(functools.partial(row_to, sums_b, 1, second_here, at))

    @pl.when(hub)
    def _():
        rows_of(sums_d, 2, n_lon * n_lat - 1).wait_recv()
        sums_ref[...] = jnp.sum(sums_d[...], axis=0, keepdims=True)
        rows_of(sums_d, 2, len(hubs) - 1).wait_send()
        rows_of(sums_b, 1, n_lon - hub_lon).wait_send()

    @pl.when(jnp.logical_not(hub))
    def _():
        rows_of(sums_b, 1, n_lon - 1).wait_recv()
        sums_ref[...] = jnp.sum(sums_b[...], axis=0)
        rows_of(sums_d, 2, len(hubs)).wait_send()
        pl.when(hub_plane)(lambda: rows_of(sums_b, 1, n_lon - 1 - hub_lon).wait_send())
        pl.when(jnp.logical_not(hub_plane))(lambda: rows_of(sums_b, 1, n_lon - 1).wait_send())

    rows_of(sums_a, 0, n_lat - 1).wait_send()


def finish(fields_ref, sums_ref, tend_in, tend_ref, surf_ref, res_ref):
    r, q1, q2 = fields_ref[0:8, :], fields_ref[8:16, :], fields_ref[16:24, :]
    rr, rq, qq, rq2, qq2 = [sums_ref[0:1, k : k + 1] for k in range(5)]
    a1 = rr / rq
    new = rr - 2.0 * a1 * rq + a1 * a1 * qq
    lead = 1.0 + new / rr
    a2 = new / (lead * lead * rq - lead * a1 * (rq2 + qq) + a1 * a1 * qq2)
    surf_ref[...] = a1 * r + a2 * (lead * r - a1 * q1)
    res_ref[...] = r - a1 * q1 - a2 * (lead * q1 - a1 * q2)
    tend_ref[...] = tend_in[...]


def body(features, spline_coef, edge_mask, head_weight, land_mask, shift_coef):
    n_lon, n_lat = lax.axis_size("lon"), lax.axis_size("lat")
    vmem = pl.BlockSpec(memory_space=pltpu.VMEM)
    dma = pltpu.SemaphoreType.DMA
    tend_shape = jax.ShapeDtypeStruct((2, L, ROWS, COLS), BF16)
    field_shape = jax.ShapeDtypeStruct((ROWS, COLS), F32)
    scratch = [
        pltpu.VMEM((C, L, ROWS, COLS), BF16),
        pltpu.VMEM((9 * C, C * J), BF16),
        pltpu.VMEM((C, C), jnp.int32),
        pltpu.VMEM((2, C), BF16),
        pltpu.VMEM((ROWS, COLS), jnp.int32),
        pltpu.VMEM((ROWS, COLS), F32),
        pltpu.VMEM((C, C * J), BF16),
        pltpu.VMEM((C, 9 * C), BF16),
        pltpu.VMEM((GROUP * J, CHUNK), BF16),
        pltpu.VMEM((GROUPS, 64, CHUNK), BF16),
        pltpu.VMEM((CHUNK, COLS), BF16),
        pltpu.VMEM((CHUNK, COLS), BF16),
        pltpu.VMEM((L, 64, WIDE), F32),
        pltpu.VMEM((16, WIDE + 256), BF16),
        pltpu.VMEM((16, WIDE + 256), BF16),
        pltpu.VMEM((64, 128), BF16),
        pltpu.VMEM((64, 128), BF16),
        pltpu.VMEM((6, 16, WIDE), BF16),
        pltpu.VMEM((2, 64, 128), BF16),
        pltpu.VMEM((n_lat, 1, 128), F32),
        pltpu.VMEM((n_lon, 1, 128), F32),
        pltpu.VMEM((n_lon * n_lat, 128), F32),
        dma((GROUPS,)), dma((5,)), dma((8,)), dma((8,)), dma((3,)), dma((3,)),
    ]
    tendency, fields, sums = pl.pallas_call(
        functools.partial(kernel, n_lon, n_lat),
        out_shape=(
            pltpu.VMEM((2, L, ROWS, COLS), BF16),
            pltpu.VMEM((3 * ROWS, COLS), F32),
            pltpu.VMEM((1, 128), F32),
        ),
        in_specs=[pl.BlockSpec(memory_space=pl.ANY)] * 6,
        out_specs=(vmem, vmem, vmem),
        scratch_shapes=scratch,
        compiler_params=pltpu.CompilerParams(collective_id=0, has_side_effects=True),
        name="closure_and_sums",
    )(features, spline_coef, edge_mask, head_weight, land_mask, shift_coef)
    return pl.pallas_call(
        finish,
        out_shape=(tend_shape, field_shape, field_shape),
        in_specs=[vmem] * 3,
        out_specs=(vmem, vmem, vmem),
        compiler_params=pltpu.CompilerParams(vmem_limit_bytes=4 * 1024 * 1024),
        name="finish",
    )(fields, sums, tendency)


def solution(mesh):
    in_specs = (P(None, None, "lat", "lon"), P(), P(), P(), P("lat", "lon"), P("lat", "lon"))
    out_specs = (P(None, None, "lat", "lon"), P("lat", "lon"), P("lat", "lon"))
    return jax.shard_map(body, mesh=mesh, in_specs=in_specs, out_specs=out_specs, check_vma=False)
```
